32 devices in a mesh: clu: 8 (over z, x), frq: 4 (over y, core).
Axes of the slice: x: 2, y: 2, z: 4, core: 2. Of those that a mesh axis runs over, the one named last changes fastest.
Arguments:
- incident: float32 [4, 2, 16384, 128], P('frq', None, 'clu'), may hold values from -6 to 6
- initial: float32 [4, 2, 16384, 128], P('frq', None, 'clu'), may hold values from -3 to 3
- near_blocks: bfloat16 [128, 8, 4, 2, 128, 128], P('clu', None, 'frq'), may hold values from -0.125 to 0.125
- near_pattern: int32 [128, 8], P('clu'), may hold values from 0 to 47
- crack_blocks: bfloat16 [256, 4, 2, 128, 128], P('clu', 'frq'), may hold values from -0.25 to 0.25
- crack_cluster: int32 [256, 1], P('clu'), may hold values from 0 to 7; in each aligned block of 32 rows (0 to 31, 32 to 63, ...) at most 8 rows name the same one
- crack_source: int32 [256], P('clu'), may hold values from 0 to 3
- crack_target: int32 [256], P('clu'), may hold values from 0 to 15
- pulse_spectrum: float32 [4, 2], P('frq'), may hold values from -4 to 4
Outputs:
- scattered: float32 [4, 2, 16384, 128], P('frq', None, 'clu')
- time_trace: float32 [4, 16384, 128], P('frq', 'clu')
The draws below stay inside these ranges and needn't reach their ends.
Inputs may be any that keep to these rules, and one draw needn't show every extreme that they name: `crack_cluster`: in the rows of one cluster no source cluster is named more than 8 times, a bound that some block reaches.
All inputs are finite; a program needn't handle non-finite values.
Results may differ from the reference program's by a relative error of at most 0.0014.
Values may be sent and summed in bfloat16 or wider, within the bound.
No kernel may reach another device: no remote copies, remote signals or barrier semaphores. Data moves between devices by JAX's collectives and lax.ppermute only.
A program may use at most 128 MiB of HBM per device.

```python
import math
import jax
import jax.numpy as jnp
import numpy as np
from jax import lax

BLK = 128
NB_DEV = 16
NEAR = 8
DIRS = 128
E_DEV = 32
FRONT = 4
CAP = 8
FREQ = 4
NBLK = 128
NPANEL = 16384
EDGES = 256
NT = 4
N_CLU = 8


def set_ends(values, key, smallest, top_value):
    longest = values.shape.index(max(values.shape))
    spots = []
    for shift in (0, 1):
        where = [jax.random.randint(jax.random.fold_in(key, axis), (), 0, length) for axis, length in enumerate(values.shape)]
        where[longest] = (where[longest] + shift) % values.shape[longest]
        spots.append(tuple(where))
    return values.at[spots[0]].set(smallest).at[spots[1]].set(top_value)


def level_of(stream_key, shape, shards, low, high):
    factor_of, own = 1.0, jax.random.fold_in(stream_key, 6)
    for position, parts in shards:
        draws = jnp.exp(jax.random.uniform(jax.random.fold_in(own, position), (parts,), jnp.float32, low / len(shards), high / len(shards)))
        factor_of = factor_of * jnp.repeat(draws, shape[position] // parts).reshape([-1 if axis == position else 1 for axis in range(len(shape))])
    return factor_of


def routed_block(key, own, number, rows, amount, top, most, slope):
    order = jax.random.permutation(key, amount)
    heavy_load, usual = load_shares(amount, rows * top, most, slope, True), load_shares(amount, rows * top, most, slope, False)
    places = jnp.arange(amount)

    def named(tallies, rotation):
        used = int((tallies > 0).sum())
        fixed = max(1, used // 4)
        passed = fixed + (places - fixed + rotation * (used - fixed)) % max(1, amount - fixed)
        return jnp.zeros((amount,), jnp.int32).at[order[jnp.where(places < fixed, places, passed)]].set(jnp.asarray(tallies, jnp.int32))

    tallies = jnp.where(number % 4 == 0, named(heavy_load, number // 4), named(usual, number - number // 4 - 1))
    mixed = jax.random.permutation(jax.random.fold_in(own, 3), amount)
    giver, receiver = mixed[0:amount // 2 * 2:2], mixed[1:amount // 2 * 2:2]
    room = jnp.minimum(tallies[giver] - 1, most - tallies[receiver]) // 2
    room = jnp.where((giver == order[0]) | (receiver == order[0]) | (tallies[receiver] == 0), 0, jnp.maximum(room, 0))
    passed = jax.random.randint(jax.random.fold_in(own, 4), (amount // 2,), 0, 1 << 20) % (room + 1)
    tallies = tallies.at[giver].add(-passed).at[receiver].add(passed)
    members = jnp.searchsorted(jnp.cumsum(tallies), jnp.arange(rows * top), side="right").astype(jnp.int32)
    table = members.reshape(top, rows).T
    table = table[jax.random.permutation(jax.random.fold_in(own, 1), rows)]
    rotation = jax.random.randint(jax.random.fold_in(own, 2), (rows, 1), 0, top)
    return jnp.take_along_axis(table, (jnp.arange(top)[None, :] + rotation) % top, axis=1)


def load_shares(count, total, most, skew, full):
    loads = [(1 << 20) // math.isqrt(rank ** skew) + 1 for rank in range(1, count + 1)]
    largest = most if full else min(most, max(-(-total // count), total * loads[0] // sum(loads)))
    least = 1 if total - largest >= count - 1 else 0
    given, surplus = [largest] + [least] * (count - 1), total - largest - least * (count - 1)
    while surplus > 0:
        movable = [i for i in range(1, count) if given[i] < largest] or [i for i in range(1, count) if given[i] < most]
        mass, budget = sum([loads[i] for i in movable]), surplus
        for i in movable:
            extra = min(most - given[i], max(1, budget * loads[i] // mass), surplus)
            given[i] = given[i] + extra
            surplus = surplus - extra
    return np.array(given)


def centred(key, dims, scale, bound, pieces=(), kind=jnp.bfloat16):
    array = jax.random.normal(key, dims, jnp.float32) * scale
    if len(pieces) > 0:
        array = level_of(key, dims, pieces, -0.22, 0.18) * array
    return jnp.clip(array, min=-bound, max=bound).astype(kind)


def setup_inputs(seed: int = 0) -> dict:
    key_list = jax.random.split(jax.random.key(seed), 10)
    incident = centred(key_list[0], (FREQ, 2, NPANEL, DIRS), 1.0, 6.0, ((0, 4), (2, 8)), jnp.float32)
    initial = centred(key_list[1], (FREQ, 2, NPANEL, DIRS), 0.5, 3.0, ((0, 4), (2, 8)), jnp.float32)
    near_blocks = centred(key_list[2], (NBLK, NEAR, FREQ, 2, BLK, BLK), (2 * NEAR * BLK) ** -0.5, 0.125, ((0, 8), (2, 4)))
    near_pattern = set_ends(jax.random.randint(key_list[3], (NBLK, NEAR), 0, 3 * NB_DEV), jax.random.fold_in(key_list[3], 1), 0, (3 * NB_DEV) - 1).astype(jnp.int32)
    crack_blocks = centred(key_list[4], (EDGES, FREQ, 2, BLK, BLK), (4 * BLK) ** -0.5, 0.25, ((0, 8), (1, 4)))
    crack_cluster_keys = jax.random.split(jax.random.fold_in(key_list[5], 1), EDGES // E_DEV)
    crack_cluster_turns = jax.random.permutation(jax.random.fold_in(key_list[5], 3), EDGES // E_DEV)
    crack_cluster = jax.vmap(lambda own, number: routed_block(jax.random.fold_in(key_list[5], 2), own, number, E_DEV, N_CLU, 1, CAP, 2))(crack_cluster_keys, crack_cluster_turns).reshape((EDGES, 1))
    crack_source = set_ends(jax.random.randint(key_list[6], (EDGES,), 0, FRONT), jax.random.fold_in(key_list[6], 1), 0, FRONT - 1).astype(jnp.int32)
    crack_target = set_ends(jax.random.randint(key_list[7], (EDGES,), 0, NB_DEV), jax.random.fold_in(key_list[7], 1), 0, NB_DEV - 1).astype(jnp.int32)
    pulse_spectrum = centred(key_list[8], (FREQ, 2), 1.0, 4.0, ((0, 4),), jnp.float32)
    return dict(incident=incident, initial=initial, near_blocks=near_blocks, near_pattern=near_pattern, crack_blocks=crack_blocks, crack_cluster=crack_cluster, crack_source=crack_source, crack_target=crack_target, pulse_spectrum=pulse_spectrum)


epsilon = 1e-06

def complex_times(factor, vector):
    real_part = factor[0][:, None, :] * vector[:, 0] - factor[1][:, None, :] * vector[:, 1]
    imag_part = factor[0][:, None, :] * vector[:, 1] + factor[1][:, None, :] * vector[:, 0]
    return jnp.stack([real_part, imag_part], axis=1)

def inner_local(former, latter):
    real_part = lax.optimization_barrier(jnp.sum(former[:, 0] * latter[:, 0] + former[:, 1] * latter[:, 1], axis=1))
    imag_part = lax.optimization_barrier(jnp.sum(former[:, 0] * latter[:, 1] - former[:, 1] * latter[:, 0], axis=1))
    return (real_part, imag_part)

def square_local(vector):
    return lax.optimization_barrier(jnp.sum(vector[:, 0] * vector[:, 0] + vector[:, 1] * vector[:, 1], axis=1))

def least_squares(beta_norm, first_h, sub_one, second_h, third_h, sub_two):
    r_one = jnp.sqrt(first_h[0] ** 2 + first_h[1] ** 2 + sub_one ** 2)
    q_real = first_h[0] / r_one
    q_imag = first_h[1] / r_one
    q_low = sub_one / r_one
    mix_real = q_real * second_h[0] + q_imag * second_h[1] + q_low * third_h[0]
    mix_imag = q_real * second_h[1] - q_imag * second_h[0] + q_low * third_h[1]
    top_real = second_h[0] - (mix_real * q_real - mix_imag * q_imag)
    top_imag = second_h[1] - (mix_real * q_imag + mix_imag * q_real)
    mid_real = third_h[0] - mix_real * q_low
    mid_imag = third_h[1] - mix_imag * q_low
    r_two_sq = top_real ** 2 + top_imag ** 2 + mid_real ** 2 + mid_imag ** 2 + sub_two ** 2
    later_real = beta_norm * top_real / r_two_sq
    later_imag = -beta_norm * top_imag / r_two_sq
    early_real = (beta_norm * q_real - (mix_real * later_real - mix_imag * later_imag)) / r_one
    early_imag = (-beta_norm * q_imag - (mix_real * later_imag + mix_imag * later_real)) / r_one
    return ((early_real, early_imag), (later_real, later_imag))

def reference(incident, initial, near_blocks, near_pattern, crack_blocks, crack_cluster, crack_source, crack_target, pulse_spectrum):
    rows = jnp.arange(NBLK, dtype=jnp.int32)
    cluster_of = rows // NB_DEV
    columns = ((cluster_of[:, None] + near_pattern // NB_DEV - 1) % N_CLU * NB_DEV + near_pattern % NB_DEV).astype(jnp.int32)
    edge_rows = jnp.arange(EDGES, dtype=jnp.int32)
    targets = (edge_rows // E_DEV * NB_DEV + crack_target).astype(jnp.int32)
    sources = (crack_cluster[:, 0] * NB_DEV + crack_source).astype(jnp.int32)

    def apply(vector):
        low = vector.astype(jnp.bfloat16).reshape(FREQ, 2, NBLK, BLK, DIRS)

        def one_freq(freq_index):
            blocks = lax.dynamic_index_in_dim(near_blocks, freq_index, 2, keepdims=False).astype(jnp.float32)
            field = lax.dynamic_index_in_dim(low, freq_index, 0, keepdims=False).astype(jnp.float32)
            picked = field[:, columns]
            products = jnp.einsum('bscpq,dbsqk->cdbpk', blocks, picked)
            near_real = products[0, 0] - products[1, 1]
            near_imag = products[0, 1] + products[1, 0]
            couple = lax.dynamic_index_in_dim(crack_blocks, freq_index, 1, keepdims=False).astype(jnp.float32)
            chosen = field[:, sources]
            crack_prod = jnp.einsum('ecpq,deqk->cdepk', couple, chosen)
            crack_real = crack_prod[0, 0] - crack_prod[1, 1]
            crack_imag = crack_prod[0, 1] + crack_prod[1, 0]
            zeros = jnp.zeros((NBLK, BLK, DIRS), jnp.float32)
            total_real = near_real + zeros.at[targets].add(crack_real)
            total_imag = near_imag + zeros.at[targets].add(crack_imag)
            return jnp.stack([total_real, total_imag], axis=0)
        result = lax.map(one_freq, jnp.arange(FREQ, dtype=jnp.int32))
        return 0.5 * vector + result.reshape(FREQ, 2, NPANEL, DIRS)
    residual = incident - apply(initial)
    beta_norm = jnp.sqrt(square_local(residual) + epsilon)
    basis_one = residual / beta_norm[:, None, None, :]
    image = apply(basis_one)
    first_h = inner_local(basis_one, image)
    image = image - complex_times(first_h, basis_one)
    sub_one = jnp.sqrt(square_local(image) + epsilon)
    basis_two = image / sub_one[:, None, None, :]
    image = apply(basis_two)
    second_h = inner_local(basis_one, image)
    third_h = inner_local(basis_two, image)
    image = image - complex_times(second_h, basis_one) - complex_times(third_h, basis_two)
    sub_two = jnp.sqrt(square_local(image) + epsilon)
    early, later = least_squares(beta_norm, first_h, sub_one, second_h, third_h, sub_two)
    scattered = initial + complex_times(early, basis_one) + complex_times(later, basis_two)
    times = jnp.arange(NT, dtype=jnp.float32)[:, None]
    freqs = jnp.arange(FREQ, dtype=jnp.float32)[None, :]
    angle = 2.0 * jnp.pi * times * freqs / NT
    coef_real = pulse_spectrum[None, :, 0] * jnp.cos(angle) - pulse_spectrum[None, :, 1] * jnp.sin(angle)
    coef_imag = -(pulse_spectrum[None, :, 0] * jnp.sin(angle) + pulse_spectrum[None, :, 1] * jnp.cos(angle))
    time_trace = jnp.einsum('tf,fpk->tpk', coef_real, scattered[:, 0], precision=lax.Precision.HIGHEST)
    time_trace = time_trace + jnp.einsum('tf,fpk->tpk', coef_imag, scattered[:, 1], precision=lax.Precision.HIGHEST)
    return (scattered, time_trace)
```

```python
import functools

import jax
import jax.numpy as jnp
from jax import lax
from jax.experimental import pallas as pl
from jax.experimental.pallas import tpu as pltpu
from jax.sharding import PartitionSpec as P

EPS = 1e-06
STREAMS = 1
VMEM_LIMIT = 44 * 1024 * 1024


def turn(rows):
    half = rows.shape[1] // 2
    if half % 128 == 0:
        return jnp.concatenate([-rows[:, half:], rows[:, :half]], axis=1)
    lane = lax.broadcasted_iota(jnp.int32, rows.shape, 1)
    rolled = pltpu.roll(rows, half, 1)
    return jnp.where(lane < half, -rolled, rolled)


def join(real, imag, stream, streams):
    if streams == 1:
        return jnp.concatenate([real, imag], axis=1)
    half = real.shape[1] // 2
    lane = lax.broadcasted_iota(jnp.int32, real.shape, 1)
    if stream == 0:
        return jnp.where(lane < half, real, pltpu.roll(imag, half, 1))
    return jnp.where(lane < half, pltpu.roll(real, half, 1), imag)


def col_sum(rows):
    return jnp.sum(rows.reshape(rows.shape[0] // 8, 8, rows.shape[1]), axis=0)


def apply_kernel(step, stream, streams, sizes, offsets, *refs):
    nblocks, span, edges, width = sizes
    nparts = len(offsets)
    near_idx, crack_idx, crack_tgt, near_ref, crack_ref = refs[:5]
    parts = refs[5 : 5 + nparts]
    rest = refs[5 + nparts :]
    extras = rest[:2] if step != 2 else rest[:1]
    rest = rest[len(extras) :]
    nouts = (3, 3, 1)[step - 1]
    outs, rest = rest[:nouts], rest[nouts:]
    near_v, crack_v, source_v, extra_v, acc, part_sem, near_sem, crack_sem, extra_sem = rest

    part_copies = []
    for place, (part, offset) in enumerate(zip(parts, offsets)):
        part_copies.append(
            pltpu.make_async_copy(
                part, source_v.at[pl.ds(offset, part.shape[0])], part_sem.at[place]
            )
        )
    for copy in part_copies:
        copy.start()

    def near_copy(g):
        return pltpu.make_async_copy(near_ref.at[g], near_v.at[g], near_sem.at[g])

    for g in range(nblocks):
        near_copy(g).start()
    crack_copy = pltpu.make_async_copy(crack_ref, crack_v, crack_sem)
    crack_copy.start()
    extra_copies = [
        pltpu.make_async_copy(extra, extra_v.at[place], extra_sem.at[place])
        for place, extra in enumerate(extras)
    ]
    for copy in extra_copies:
        copy.start()
    for copy in part_copies:
        copy.wait()

    def near_row(g, carry):
        near_copy(g).wait()
        left = jnp.concatenate([near_v[g, s] for s in range(span)], axis=1)
        right = jnp.concatenate([source_v[near_idx[g * span + s]] for s in range(span)], axis=0)
        acc[g] = jnp.dot(left, right, preferred_element_type=jnp.float32)
        return carry

    lax.fori_loop(0, nblocks, near_row, 0)
    crack_copy.wait()

    def crack_edge(e, carry):
        target = crack_tgt[e]
        acc[target] += jnp.dot(
            crack_v[e], source_v[crack_idx[e]], preferred_element_type=jnp.float32
        )
        return carry

    lax.fori_loop(0, edges, crack_edge, 0)
    for copy in extra_copies:
        copy.wait()

    def image(g):
        total = acc[g]
        return total[:width] + turn(total[width:])

    lanes = acc.shape[2]
    nsums = (1, 3, 5)[step - 1]
    zero = jnp.zeros((8, lanes), jnp.float32)

    def finish(g, sums):
        rows = pl.ds(pl.multiple_of(g * width, width), width)
        new = image(g)
        if step == 1:
            incident = join(extra_v[0, 0, rows], extra_v[0, 1, rows], stream, streams)
            initial = join(extra_v[1, 0, rows], extra_v[1, 1, rows], stream, streams)
            new = incident - 0.5 * initial - new
            terms = (new * new,)
        elif step == 2:
            first = extra_v[0, rows]
            terms = (first * new, first * turn(new), new * new)
        else:
            first, second, turned = extra_v[0, rows], extra_v[1, rows], turn(new)
            terms = (first * new, first * turned, second * new, second * turned, new * new)
        if step != 3:
            outs[0][rows, :] = new
            outs[1][rows, :] = new.astype(jnp.bfloat16)
        return tuple(total + col_sum(term) for total, term in zip(sums, terms))

    sums = lax.fori_loop(0, nblocks, finish, (zero,) * nsums)
    sums = [jnp.sum(total, axis=0, keepdims=True) for total in sums]
    sums.append(jnp.zeros((8 - nsums, lanes), jnp.float32))
    outs[-1][...] = jnp.concatenate(sums, axis=0)


def apply_call(step, stream, streams, tables, near, crack, parts, extras):
    nblocks, span = near.shape[:2]
    edges, width = crack.shape[0], near.shape[3]
    lanes = parts[0].shape[2]
    rows = nblocks * width
    offsets, total = [], 0
    for part in parts:
        offsets.append(total)
        total += part.shape[0]
    vector = jax.ShapeDtypeStruct((rows, lanes), jnp.float32)
    gram = jax.ShapeDtypeStruct((8, lanes), jnp.float32)
    if step == 3:
        out_shape = (gram,)
    else:
        out_shape = (vector, jax.ShapeDtypeStruct((rows, lanes), jnp.bfloat16), gram)
    smem = pl.BlockSpec(memory_space=pltpu.SMEM)
    anywhere = pl.BlockSpec(memory_space=pl.ANY)
    whole = pl.BlockSpec(memory_space=pltpu.VMEM)
    body = functools.partial(
        apply_kernel, step, stream, streams, (nblocks, span, edges, width), tuple(offsets)
    )
    return pl.pallas_call(
        body,
        out_shape=out_shape,
        in_specs=[smem] * 3 + [anywhere] * (2 + len(parts) + len(extras)),
        out_specs=tuple(whole for _ in out_shape),
        scratch_shapes=[
            pltpu.VMEM(near.shape, near.dtype),
            pltpu.VMEM(crack.shape, crack.dtype),
            pltpu.VMEM((total, width, lanes), jnp.bfloat16),
            pltpu.VMEM((len(extras), *extras[0].shape), jnp.float32),
            pltpu.VMEM((nblocks, 2 * width, lanes), jnp.float32),
            pltpu.SemaphoreType.DMA((len(parts),)),
            pltpu.SemaphoreType.DMA((nblocks,)),
            pltpu.SemaphoreType.DMA,
            pltpu.SemaphoreType.DMA((len(extras),)),
        ],
        compiler_params=pltpu.CompilerParams(vmem_limit_bytes=VMEM_LIMIT),
        cost_estimate=pl.CostEstimate(
            flops=4 * width * width * lanes * (nblocks * span + edges),
            bytes_accessed=near.size * 2 + crack.size * 2,
            transcendentals=0,
        ),
        name=f"operator_{step}_{stream}",
    )(*tables, near, crack, *parts, *extras)


def swap(value, axis, distance):
    count = lax.axis_size(axis)
    return lax.ppermute(value, axis, [(i, i ^ distance) for i in range(count)])


def shift(value, axis, distance):
    count = lax.axis_size(axis)
    return lax.ppermute(value, axis, [(i, (i + distance) % count) for i in range(count)])


def tuned():
    return lax.axis_size("clu") == 8


def exchange(low, front):
    count = lax.axis_size("clu")
    head = low[:front]
    if not tuned():
        every = lax.all_gather(head, "clu", axis=0, tiled=True)
        return [low, shift(low, "clu", -1), shift(low, "clu", 1), every]
    even = lax.axis_index("clu") % 2 == 0
    beside = swap(low, "clu", 1)
    before, across, after = (shift(head, "clu", d) for d in (2, 4, 6))
    ring = [(i, (i + 2) % count if i % 2 == 0 else (i - 2) % count) for i in range(count)]
    beyond = lax.ppermute(beside, "clu", ring)
    near_side = jnp.where(even, before, after)
    others = swap(jnp.concatenate([near_side, across], axis=0), "clu", 1)
    return [low, beside, beyond, before, across, after, others]


def source_tables(near_pattern, crack_cluster, crack_source, nblocks, front):
    count = lax.axis_size("clu")
    me = lax.axis_index("clu")
    side, block = near_pattern.reshape(-1) // nblocks, near_pattern.reshape(-1) % nblocks
    if not tuned():
        place = jnp.where(side == 1, 0, jnp.where(side == 2, 1, 2))
        return place * nblocks + block, 3 * nblocks + crack_cluster * front + crack_source
    odd = me % 2
    place = jnp.where(side == 1, 0, jnp.where((side == 2) ^ (odd == 1), 1, 2))
    offset = (crack_cluster - me) % count
    offset = jnp.where(odd == 1, (-offset) % count, offset)
    base = 3 * nblocks
    before = jnp.where(odd == 1, base + 2 * front, base)
    after = jnp.where(odd == 1, base, base + 2 * front)
    start = jnp.select(
        [offset == d for d in (0, 1, 7, 6, 4, 2, 3)],
        [
            jnp.zeros_like(offset),
            jnp.full_like(offset, nblocks),
            jnp.full_like(offset, 2 * nblocks),
            jnp.zeros_like(offset) + before,
            jnp.full_like(offset, base + front),
            jnp.zeros_like(offset) + after,
            jnp.full_like(offset, base + 3 * front),
        ],
        jnp.full_like(offset, base + 4 * front),
    )
    return place * nblocks + block, start + crack_source


def sum_over_clusters(value):
    if not tuned():
        return [lax.psum(value, "clu")]
    value = value + swap(value, "clu", 1)
    return [value, *(shift(value, "clu", d) for d in (2, 4, 6))]


def cmul(a, b):
    return (a[0] * b[0] - a[1] * b[1], a[0] * b[1] + a[1] * b[0])


def cjmul(a, b):
    return (a[0] * b[0] + a[1] * b[1], a[0] * b[1] - a[1] * b[0])


def cadd(*terms):
    return (sum(t[0] for t in terms), sum(t[1] for t in terms))


def scale(factor, a):
    return (factor * a[0], factor * a[1])


def norm2(a):
    return a[0] * a[0] + a[1] * a[1]


def least_squares(beta_norm, first_h, sub_one, second_h, third_h, sub_two):
    r_one = jnp.sqrt(first_h[0] ** 2 + first_h[1] ** 2 + sub_one**2)
    q_real = first_h[0] / r_one
    q_imag = first_h[1] / r_one
    q_low = sub_one / r_one
    mix_real = q_real * second_h[0] + q_imag * second_h[1] + q_low * third_h[0]
    mix_imag = q_real * second_h[1] - q_imag * second_h[0] + q_low * third_h[1]
    top_real = second_h[0] - (mix_real * q_real - mix_imag * q_imag)
    top_imag = second_h[1] - (mix_real * q_imag + mix_imag * q_real)
    mid_real = third_h[0] - mix_real * q_low
    mid_imag = third_h[1] - mix_imag * q_low
    r_two_sq = top_real**2 + top_imag**2 + mid_real**2 + mid_imag**2 + sub_two**2
    later_real = beta_norm * top_real / r_two_sq
    later_imag = -beta_norm * top_imag / r_two_sq
    early_real = (beta_norm * q_real - (mix_real * later_real - mix_imag * later_imag)) / r_one
    early_imag = (-beta_norm * q_imag - (mix_real * later_imag + mix_imag * later_real)) / r_one
    return ((early_real, early_imag), (later_real, later_imag))


def combine(g00, g01, g11, g02, g12, g22):
    beta2 = g00 + EPS
    beta = jnp.sqrt(beta2)
    h11 = ((0.5 * g00 + g01[0]) / beta2, g01[1] / beta2)
    s = (0.5 - h11[0], -h11[1])
    s01 = cjmul(s, g01)
    w2w2 = g11 + 2.0 * s01[0] + norm2(s) * g00
    h21 = jnp.sqrt(jnp.maximum(w2w2 / beta2, 0.0) + EPS)
    k = 1.0 / (beta * h21)
    d = (s[0] + 0.5, s[1])
    e = scale(0.5, s)
    r0u = cadd(g02, cmul(d, g01), scale(g00, e))
    z1u = cadd(g12, scale(g11, d), cmul(e, (g01[0], -g01[1])))
    h12 = scale(k / beta, r0u)
    h22 = scale(k * k, cadd(z1u, cjmul(s, r0u)))
    uu = (
        g22
        + norm2(d) * g11
        + norm2(e) * g00
        + 2.0 * cjmul(d, g12)[0]
        + 2.0 * cjmul(e, g02)[0]
        + 2.0 * cjmul(e, cmul(d, g01))[0]
    )
    n11 = g00 / beta2
    n22 = k * k * w2w2
    n12 = scale(k / beta, cadd(g01, scale(g00, s)))
    rest = (
        k * k * uu
        + norm2(h12) * (n11 - 2.0)
        + norm2(h22) * (n22 - 2.0)
        + 2.0 * cmul(cjmul(h12, h22), n12)[0]
    )
    h32 = jnp.sqrt(jnp.maximum(rest, 0.0) + EPS)
    early, later = least_squares(beta, h11, h21, h12, h22, h32)
    b = scale(k, later)
    a = cadd(scale(1.0 / beta, early), cmul(b, s))
    return a, b


def result_kernel(stream, streams, nsums, *refs):
    phases, rows_of = refs[0], refs[1 : 1 + nsums]
    initial, first, second, scattered, send, keep = refs[1 + nsums :]
    sums = rows_of[0][...]
    for other in rows_of[1:]:
        sums = sums + other[...]
    half = sums.shape[1] // 2
    if half % 128 == 0:
        sums = sums[:, :half] + sums[:, half:]
    else:
        sums = sums + pltpu.roll(sums, half, 1)

    def row(i):
        return sums[i : i + 1]

    a, b = combine(
        row(0),
        (row(8), -row(9)),
        row(10),
        (row(16), -row(17)),
        (row(18), -row(19)),
        row(20),
    )
    width = 128
    blocks = first.shape[0] // width

    def one(g, carry):
        rows = pl.ds(pl.multiple_of(g * width, width), width)
        x, y = first[rows, :], second[rows, :]
        xr, xi, yr, yi = x[:, :half], x[:, half:], y[:, :half], y[:, half:]
        real = initial[0, rows] + a[0] * xr - a[1] * xi + b[0] * yr - b[1] * yi
        imag = initial[1, rows] + a[0] * xi + a[1] * xr + b[0] * yi + b[1] * yr
        scattered[0, rows, :] = real
        scattered[1, rows, :] = imag
        send[rows, :] = phases[0] * real - phases[1] * imag
        keep[rows, :] = phases[2] * real - phases[3] * imag
        return carry

    lax.fori_loop(0, blocks, one, 0)


def result_call(phases, sums, initial, first, second):
    rows = initial.shape[1]
    real = jax.ShapeDtypeStruct((rows, 128), jnp.float32)
    whole = pl.BlockSpec(memory_space=pltpu.VMEM)
    return pl.pallas_call(
        functools.partial(result_kernel, 0, 1, len(sums)),
        out_shape=(jax.ShapeDtypeStruct(initial.shape, jnp.float32), real, real),
        in_specs=[pl.BlockSpec(memory_space=pltpu.SMEM)] + [whole] * (len(sums) + 3),
        out_specs=(whole, whole, whole),
        compiler_params=pltpu.CompilerParams(vmem_limit_bytes=VMEM_LIMIT),
        name="result",
    )(phases, *sums, initial, first, second)


def mix_kernel(signs, keep, taken, here, away):
    here[...] = signs[0] * keep[...] + signs[1] * taken[...]
    away[...] = (signs[2] * keep[...] + signs[3] * taken[...]).astype(jnp.bfloat16)


def mix_call(signs, keep, taken):
    whole = pl.BlockSpec(memory_space=pltpu.VMEM)
    return pl.pallas_call(
        mix_kernel,
        out_shape=(
            jax.ShapeDtypeStruct(keep.shape, jnp.float32),
            jax.ShapeDtypeStruct(keep.shape, jnp.bfloat16),
        ),
        in_specs=[pl.BlockSpec(memory_space=pltpu.SMEM), whole, whole],
        out_specs=(whole, whole),
        name="mix",
    )(signs, keep, taken)


def power_of_i(exponent):
    exponent = exponent % 4
    real = jnp.where(exponent == 0, 1.0, jnp.where(exponent == 2, -1.0, 0.0))
    imag = jnp.where(exponent == 1, 1.0, jnp.where(exponent == 3, -1.0, 0.0))
    return real, imag


def local(
    incident,
    initial,
    near_blocks,
    near_pattern,
    crack_blocks,
    crack_cluster,
    crack_source,
    crack_target,
    pulse_spectrum,
):
    panels, directions = incident.shape[2:]
    nblocks, span = near_blocks.shape[:2]
    width = near_blocks.shape[4]
    edges = crack_blocks.shape[0]
    front = 4
    near = near_blocks.reshape(nblocks, span, 2 * width, width)
    crack = crack_blocks.reshape(edges, 2 * width, width)
    near_idx, crack_idx = source_tables(
        near_pattern, crack_cluster[:, 0], crack_source, nblocks, front
    )
    tables = (near_idx.astype(jnp.int32), crack_idx.astype(jnp.int32), crack_target)
    incident, initial = incident[0], initial[0]

    def blocks_of(low):
        return low.reshape(nblocks, width, low.shape[1])

    low = jnp.concatenate([initial[0], initial[1]], axis=1).astype(jnp.bfloat16)
    parts = exchange(blocks_of(low), front)
    first, low, sums_one = apply_call(1, 0, 1, tables, near, crack, parts, (incident, initial))
    parts = exchange(blocks_of(low), front)
    second, low, sums_two = apply_call(2, 0, 1, tables, near, crack, parts, (first,))
    parts = exchange(blocks_of(low), front)
    (sums_three,) = apply_call(3, 0, 1, tables, near, crack, parts, (first, second))
    sums = sum_over_clusters(jnp.concatenate([sums_one, sums_two, sums_three], axis=0))

    f = lax.axis_index("frq")
    side, core = f // 2, f % 2
    pulse = (pulse_spectrum[0, 0], pulse_spectrum[0, 1])
    phase_send = cmul(pulse, power_of_i((1 - core) * f))
    phase_keep = cmul(pulse, power_of_i(core * f))
    phases = jnp.stack([*phase_send, *phase_keep])
    scattered, send, keep = result_call(phases, sums, initial, first, second)
    taken = swap(send, "frq", 1)
    sign_keep = jnp.where(core == 0, 1.0, -1.0)
    signs = jnp.stack(
        [
            jnp.where(side == 1, sign_keep, 1.0),
            jnp.where(side == 1, -sign_keep, 1.0),
            jnp.where(side == 0, sign_keep, 1.0),
            jnp.where(side == 0, -sign_keep, 1.0),
        ]
    )
    here, away = mix_call(signs, keep, taken)
    time_trace = here + swap(away, "frq", 2).astype(jnp.float32)
    return (scattered[None], time_trace[None])


def solution(mesh):
    in_specs = (
        P("frq", None, "clu", None),
        P("frq", None, "clu", None),
        P("clu", None, "frq", None, None, None),
        P("clu", None),
        P("clu", "frq", None, None, None),
        P("clu", None),
        P("clu"),
        P("clu"),
        P("frq", None),
    )
    out_specs = (P("frq", None, "clu", None), P("frq", "clu", None))
    return jax.shard_map(local, mesh=mesh, in_specs=in_specs, out_specs=out_specs, check_vma=False)
```

```python
import functools

import jax
import jax.numpy as jnp
from jax import lax
from jax.experimental import pallas as pl
from jax.experimental.pallas import tpu as pltpu
from jax.sharding import PartitionSpec as P

EPS = 1e-06
MIB = 1024 * 1024
PLAIN_VMEM = 10 * MIB


def turn(rows):
    half = rows.shape[1] // 2
    return jnp.concatenate([-rows[:, half:], rows[:, :half]], axis=1)


def col_sum(rows):
    return jnp.sum(rows.reshape(rows.shape[0] // 8, 8, rows.shape[1]), axis=0)


def apply_kernel(step, sizes, moves, *refs):
    nblocks, span, edges, width, group, front = sizes
    early, late, nparts = moves
    near_idx, crack_idx, crack_tgt, near_in, crack_in = refs[:5]
    parts = refs[5 : 5 + nparts]
    rest = refs[5 + nparts :]
    extras = rest[:2] if step != 2 else rest[:1]
    rest = rest[len(extras) :]
    nouts = (5, 5, 1)[step - 1]
    outs, rest = rest[:nouts], rest[nouts:]
    front_v, source_v, acc, front_sem, source_sem = rest[:5]
    near_v, crack_v = near_in, crack_in
    matrix_copies, extra_copies = [], []
    if step == 1:
        near_v, crack_v, extra_v, matrix_sem, extra_sem = rest[5:]
        matrix_copies = [pltpu.make_async_copy(crack_in, crack_v, matrix_sem.at[nblocks])]
        for g in range(nblocks):
            matrix_copies.append(
                pltpu.make_async_copy(near_in.at[g], near_v.at[g], matrix_sem.at[g])
            )
        extra_copies = [
            pltpu.make_async_copy(extra, extra_v.at[place], extra_sem.at[place])
            for place, extra in enumerate(extras)
        ]
        extras = [extra_v.at[place] for place in range(2)]

    def copies(which, target, sems):
        return [
            pltpu.make_async_copy(
                parts[part].at[pl.ds(begin, count)],
                target.at[pl.ds(offset, count)],
                sems.at[place],
            )
            for place, (part, begin, count, offset) in enumerate(which)
        ]

    front_copies = copies(early, front_v, front_sem)
    source_copies = copies(late, source_v, source_sem)
    for copy in front_copies + matrix_copies[:1] + source_copies + extra_copies:
        copy.start()
    for copy in matrix_copies[1:]:
        copy.start()
    acc[...] = jnp.zeros(acc.shape, jnp.float32)
    for copy in front_copies + matrix_copies[:1]:
        copy.wait()

    def crack_edges(i, carry):
        products = [
            jnp.dot(
                crack_v[i * group + k],
                front_v[crack_idx[i * group + k]],
                preferred_element_type=jnp.float32,
            )
            for k in range(group)
        ]
        for k in range(group):
            acc[crack_tgt[i * group + k]] += products[k]
        return carry

    lax.fori_loop(0, edges // group, crack_edges, 0)
    for copy in source_copies + extra_copies:
        copy.wait()

    lanes = acc.shape[2]
    nsums = (1, 3, 5)[step - 1]
    zero = jnp.zeros((8, lanes), jnp.float32)

    def row(part, start, g, sums):
        if step == 1:
            pltpu.make_async_copy(near_in.at[g], near_v.at[g], matrix_sem.at[g]).wait()
        left = jnp.concatenate([near_v[g, s] for s in range(span)], axis=1)
        right = jnp.concatenate([source_v[near_idx[g * span + s]] for s in range(span)], axis=0)
        total = acc[g] + jnp.dot(left, right, preferred_element_type=jnp.float32)
        new = total[:width] + turn(total[width:])
        rows = pl.ds(pl.multiple_of(g * width, width), width)
        if step == 1:
            incident = jnp.concatenate([extras[0][0, rows], extras[0][1, rows]], axis=1)
            initial = jnp.concatenate([extras[1][0, rows], extras[1][1, rows]], axis=1)
            new = incident - 0.5 * initial - new
            terms = (new * new,)
        elif step == 2:
            first = extras[0][rows, :]
            terms = (first * new, first * turn(new), new * new)
        else:
            first, second, turned = extras[0][rows, :], extras[1][rows, :], turn(new)
            terms = (first * new, first * turned, second * new, second * turned, new * new)
        if step != 3:
            outs[0][rows, :] = new
            rounded = new.astype(jnp.bfloat16)
            outs[1 + part][g - start] = rounded
            if part == 0:

                @pl.when(g < front)
                def _():
                    outs[3][g] = rounded

        return tuple(total + col_sum(term) for total, term in zip(sums, terms))

    sums = (zero,) * nsums
    cut = nblocks // 2
    for part, (start, end) in enumerate(((0, cut), (cut, nblocks))):
        sums = lax.fori_loop(start, end, functools.partial(row, part, start), sums, unroll=2)
    sums = [jnp.sum(total, axis=0, keepdims=True) for total in sums]
    sums.append(jnp.zeros((8 - nsums, lanes), jnp.float32))
    outs[-1][...] = jnp.concatenate(sums, axis=0)


def low_shapes(nblocks, width, lanes, front):
    cut = nblocks // 2
    return tuple(
        jax.ShapeDtypeStruct((count, width, lanes), jnp.bfloat16)
        for count in (cut, nblocks - cut, front)
    )


def apply_call(step, front, tables, near, crack, found, extras):
    parts, early, late = found
    nblocks, span = near.shape[:2]
    edges, width = crack.shape[0], near.shape[3]
    lanes = parts[0].shape[2]
    group = 4 if edges % 4 == 0 else 1
    gram = jax.ShapeDtypeStruct((8, lanes), jnp.float32)
    out_shape = (gram,)
    if step != 3:
        vector = jax.ShapeDtypeStruct((nblocks * width, lanes), jnp.float32)
        out_shape = (vector, *low_shapes(nblocks, width, lanes, front), gram)
    smem = pl.BlockSpec(memory_space=pltpu.SMEM)
    anywhere = pl.BlockSpec(memory_space=pltpu.HBM if step == 1 else pl.ANY)
    whole = pl.BlockSpec(memory_space=pltpu.VMEM)
    scratch = []
    if step == 1:
        scratch = [
            pltpu.VMEM(near.shape, near.dtype),
            pltpu.VMEM(crack.shape, crack.dtype),
            pltpu.VMEM((2, *extras[0].shape), jnp.float32),
            pltpu.SemaphoreType.DMA((nblocks + 1,)),
            pltpu.SemaphoreType.DMA((2,)),
        ]
    nearby = sum(move[2] for move in early), sum(move[2] for move in late)
    held = 2 * sum(nearby) * width * lanes + 8 * nblocks * width * lanes
    if step == 1:
        held += 8 * extras[0].size + 2 * (near.size + crack.size)
    body = functools.partial(
        apply_kernel,
        step,
        (nblocks, span, edges, width, group, front),
        (early, late, len(parts)),
    )
    return pl.pallas_call(
        body,
        out_shape=out_shape,
        in_specs=[smem] * 3
        + [anywhere if step == 1 else whole] * 2
        + [anywhere] * len(parts)
        + [anywhere if step == 1 else whole] * len(extras),
        out_specs=tuple(whole for _ in out_shape),
        scratch_shapes=[
            pltpu.VMEM((nearby[0], width, lanes), jnp.bfloat16),
            pltpu.VMEM((nearby[1], width, lanes), jnp.bfloat16),
            pltpu.VMEM((nblocks, 2 * width, lanes), jnp.float32),
            pltpu.SemaphoreType.DMA((len(early),)),
            pltpu.SemaphoreType.DMA((len(late),)),
            *scratch,
        ],
        compiler_params=pltpu.CompilerParams(vmem_limit_bytes=44 * MIB if step == 1 else held + 2 * MIB),
        cost_estimate=pl.CostEstimate(
            flops=4 * width * width * lanes * (nblocks * span + edges),
            bytes_accessed=near.size * 2 + crack.size * 2,
            transcendentals=0,
        ),
        name=f"operator_{step}",
    )(*tables, near, crack, *parts, *extras)


def prepare_kernel(initial, low_a, low_b, head):
    width = low_a.shape[1]

    def one(target, start, g, carry):
        rows = pl.ds(pl.multiple_of((start + g) * width, width), width)
        rounded = jnp.concatenate([initial[0, rows], initial[1, rows]], axis=1)
        target[g] = rounded.astype(jnp.bfloat16)
        return carry

    cut = low_a.shape[0]
    lax.fori_loop(0, cut, functools.partial(one, low_a, 0), 0)
    lax.fori_loop(0, low_b.shape[0], functools.partial(one, low_b, cut), 0)
    lax.fori_loop(0, head.shape[0], functools.partial(one, head, 0), 0)


def swap(value, axis, distance):
    count = lax.axis_size(axis)
    return lax.ppermute(value, axis, [(i, i ^ distance) for i in range(count)])


def shift(value, axis, distance):
    count = lax.axis_size(axis)
    return lax.ppermute(value, axis, [(i, (i + distance) % count) for i in range(count)])


def ring(value, distance):
    count = lax.axis_size("clu")
    pairs = [(i, (i + (-distance if i % 2 else distance)) % count) for i in range(count)]
    return lax.ppermute(value, "clu", pairs)


def tuned():
    return lax.axis_size("clu") == 8


def tie(*values):
    return lax.optimization_barrier(values)


def exchange(lows, early_ties=(), late_ties=()):
    low_a, low_b, head = lows
    cut, rest, front = (low.shape[0] for low in lows)
    nblocks = cut + rest
    if not tuned():
        count = lax.axis_size("clu")
        low = jnp.concatenate([low_a, low_b], axis=0)
        every = lax.all_gather(head, "clu", axis=0, tiled=True)
        parts = [low, shift(low, "clu", -1), shift(low, "clu", 1), every]
        late = tuple((k, 0, nblocks, k * nblocks) for k in range(3))
        return (parts, ((3, 0, count * front, 0),), late), early_ties, late_ties
    beside_a = swap(low_a, "clu", 1)
    same = ring(head, 2)
    other = ring(head, -2)
    tail, beside_a, same, other, *early_ties = tie(low_b, beside_a, same, other, *early_ties)
    beyond_a = ring(jnp.concatenate([beside_a, same], axis=0), 2)
    beside_b = swap(tail, "clu", 1)
    same_pair = swap(same, "clu", 1)
    beside_b, *late_ties = tie(beside_b, *late_ties)
    beyond_b = ring(beside_b, 2)
    far_pair = swap(beyond_a[cut:], "clu", 1)
    parts = [low_a, low_b, beside_a, beside_b, beyond_a, beyond_b]
    parts += [same, other, same_pair, far_pair]
    early = tuple(
        (part, begin, front, place * front)
        for place, (part, begin) in enumerate(
            [(0, 0), (2, 0), (4, 0), (6, 0), (7, 0), (4, cut), (8, 0), (9, 0)]
        )
    )
    late = tuple(
        (2 * k + half, 0, (cut, rest)[half], k * nblocks + half * cut)
        for k in range(3)
        for half in range(2)
    )
    return (parts, early, late), early_ties, late_ties


def source_tables(near_pattern, crack_cluster, crack_source, nblocks, front):
    count = lax.axis_size("clu")
    me = lax.axis_index("clu")
    side, block = near_pattern.reshape(-1) // nblocks, near_pattern.reshape(-1) % nblocks
    if not tuned():
        place = jnp.where(side == 1, 0, jnp.where(side == 2, 1, 2))
        return place * nblocks + block, crack_cluster * front + crack_source
    odd = me % 2 == 1
    place = jnp.where(side == 1, 0, jnp.where((side == 2) ^ odd, 1, 2))
    offset = (crack_cluster - me) % count
    offset = jnp.where(odd, (-offset) % count, offset)
    slot = jnp.zeros_like(offset)
    for position, distance in enumerate((0, 1, 7, 6, 2, 4, 3, 5)):
        slot = jnp.where(offset == distance, position, slot)
    return place * nblocks + block, slot * front + crack_source


def sum_over_clusters(value):
    if not tuned():
        return [lax.psum(value, "clu")]
    value = value + swap(value, "clu", 1)
    return [value, *(shift(value, "clu", d) for d in (2, 4, 6))]


def cmul(a, b):
    return (a[0] * b[0] - a[1] * b[1], a[0] * b[1] + a[1] * b[0])


def cjmul(a, b):
    return (a[0] * b[0] + a[1] * b[1], a[0] * b[1] - a[1] * b[0])


def cadd(*terms):
    return (sum(t[0] for t in terms), sum(t[1] for t in terms))


def scale(factor, a):
    return (factor * a[0], factor * a[1])


def norm2(a):
    return a[0] * a[0] + a[1] * a[1]


def least_squares(beta_norm, first_h, sub_one, second_h, third_h, sub_two):
    r_one = jnp.sqrt(first_h[0] ** 2 + first_h[1] ** 2 + sub_one**2)
    q_real = first_h[0] / r_one
    q_imag = first_h[1] / r_one
    q_low = sub_one / r_one
    mix_real = q_real * second_h[0] + q_imag * second_h[1] + q_low * third_h[0]
    mix_imag = q_real * second_h[1] - q_imag * second_h[0] + q_low * third_h[1]
    top_real = second_h[0] - (mix_real * q_real - mix_imag * q_imag)
    top_imag = second_h[1] - (mix_real * q_imag + mix_imag * q_real)
    mid_real = third_h[0] - mix_real * q_low
    mid_imag = third_h[1] - mix_imag * q_low
    r_two_sq = top_real**2 + top_imag**2 + mid_real**2 + mid_imag**2 + sub_two**2
    later_real = beta_norm * top_real / r_two_sq
    later_imag = -beta_norm * top_imag / r_two_sq
    early_real = (beta_norm * q_real - (mix_real * later_real - mix_imag * later_imag)) / r_one
    early_imag = (-beta_norm * q_imag - (mix_real * later_imag + mix_imag * later_real)) / r_one
    return ((early_real, early_imag), (later_real, later_imag))


def combine(g00, g01, g11, g02, g12, g22):
    beta2 = g00 + EPS
    beta = jnp.sqrt(beta2)
    h11 = ((0.5 * g00 + g01[0]) / beta2, g01[1] / beta2)
    s = (0.5 - h11[0], -h11[1])
    s01 = cjmul(s, g01)
    w2w2 = g11 + 2.0 * s01[0] + norm2(s) * g00
    h21 = jnp.sqrt(jnp.maximum(w2w2 / beta2, 0.0) + EPS)
    k = 1.0 / (beta * h21)
    d = (s[0] + 0.5, s[1])
    e = scale(0.5, s)
    r0u = cadd(g02, cmul(d, g01), scale(g00, e))
    z1u = cadd(g12, scale(g11, d), cmul(e, (g01[0], -g01[1])))
    h12 = scale(k / beta, r0u)
    h22 = scale(k * k, cadd(z1u, cjmul(s, r0u)))
    uu = (
        g22
        + norm2(d) * g11
        + norm2(e) * g00
        + 2.0 * cjmul(d, g12)[0]
        + 2.0 * cjmul(e, g02)[0]
        + 2.0 * cjmul(e, cmul(d, g01))[0]
    )
    n11 = g00 / beta2
    n22 = k * k * w2w2
    n12 = scale(k / beta, cadd(g01, scale(g00, s)))
    rest = (
        k * k * uu
        + norm2(h12) * (n11 - 2.0)
        + norm2(h22) * (n22 - 2.0)
        + 2.0 * cmul(cjmul(h12, h22), n12)[0]
    )
    h32 = jnp.sqrt(jnp.maximum(rest, 0.0) + EPS)
    early, later = least_squares(beta, h11, h21, h12, h22, h32)
    b = scale(k, later)
    a = cadd(scale(1.0 / beta, early), cmul(b, s))
    return a, b


def small_kernel(nsums, pulse, *refs):
    coefs, sent = refs[nsums:]
    sums = refs[0][...]
    for other in refs[1:nsums]:
        sums = sums + other[...]
    half = sums.shape[1] // 2
    sums = sums[:, :half] + sums[:, half:]

    def row(i):
        return sums[i : i + 1]

    a, b = combine(
        row(0),
        (row(8), -row(9)),
        row(10),
        (row(16), -row(17)),
        (row(18), -row(19)),
        row(20),
    )
    zero = jnp.zeros((4, half), jnp.float32)
    coefs[...] = jnp.concatenate([*a, *b, zero], axis=0)
    factor = (pulse[0, 0], pulse[0, 1])
    sent[...] = jnp.concatenate([*cmul(factor, a), *cmul(factor, b), zero], axis=0)


def scattered_kernel(coefs, initial, first, second, scattered):
    half = initial.shape[2]
    a = (coefs[0:1], coefs[1:2])
    b = (coefs[2:3], coefs[3:4])
    width = 256

    def one(g, carry):
        rows = pl.ds(pl.multiple_of(g * width, width), width)
        x, y = first[rows, :], second[rows, :]
        xr, xi, yr, yi = x[:, :half], x[:, half:], y[:, :half], y[:, half:]
        scattered[0, rows, :] = initial[0, rows] + a[0] * xr - a[1] * xi + b[0] * yr - b[1] * yi
        scattered[1, rows, :] = initial[1, rows] + a[0] * xi + a[1] * xr + b[0] * yi + b[1] * yr
        return carry

    lax.fori_loop(0, first.shape[0] // width, one, 0)


def power_of_i(exponent):
    exponent = lax.rem(exponent, 4)
    real = jnp.where(exponent == 0, 1.0, jnp.where(exponent == 2, -1.0, 0.0))
    imag = jnp.where(exponent == 1, 1.0, jnp.where(exponent == 3, -1.0, 0.0))
    return real, imag


def terms_kernel(place, pulse, initial, send, keep):
    width = 256
    f, core = place[0], lax.rem(place[0], 2)
    factor = (pulse[0, 0], pulse[0, 1])
    sent = cmul(factor, power_of_i((1 - core) * f))
    kept = cmul(factor, power_of_i(core * f))

    def one(g, carry):
        rows = pl.ds(pl.multiple_of(g * width, width), width)
        real, imag = initial[0, rows], initial[1, rows]
        send[rows, :] = sent[0] * real - sent[1] * imag
        keep[rows, :] = kept[0] * real - kept[1] * imag
        return carry

    lax.fori_loop(0, initial.shape[1] // width, one, 0)


def mix_kernel(place, keep, taken, here, away):
    side, sign = place[0] // 2, 1.0 - 2.0 * lax.rem(place[0], 2).astype(jnp.float32)
    near_sign, far_sign = jnp.where(side == 1, sign, 1.0), jnp.where(side == 0, sign, 1.0)
    near_other, far_other = jnp.where(side == 1, -sign, 1.0), jnp.where(side == 0, -sign, 1.0)
    here[...] = near_sign * keep[...] + near_other * taken[...]
    away[...] = far_sign * keep[...] + far_other * taken[...]


def trace_kernel(count, place, here, away, *refs):
    coefs, firsts, seconds = refs[:count], refs[count : 2 * count], refs[2 * count : 3 * count]
    trace = refs[3 * count]
    half = trace.shape[1]
    width = 256
    weights = []
    for k in range(count):
        turned = power_of_i(place[0] * place[k])
        values = coefs[k][...]
        weights.append(
            (
                cmul(turned, (values[0:1], values[1:2])),
                cmul(turned, (values[2:3], values[3:4])),
            )
        )

    def one(g, carry):
        rows = pl.ds(pl.multiple_of(g * width, width), width)
        total = here[rows, :] + away[rows, :]
        for k in range(count):
            a, b = weights[k]
            x, y = firsts[k][rows, :], seconds[k][rows, :]
            total = total + (a[0] * x[:, :half] - a[1] * x[:, half:])
            total = total + (b[0] * y[:, :half] - b[1] * y[:, half:])
        trace[rows, :] = total
        return carry

    lax.fori_loop(0, trace.shape[0] // width, one, 0)


def on_vmem(body, out_shape, smem_args, args, name):
    outs = jax.tree.leaves(out_shape)
    moved = sum(a.size * a.dtype.itemsize for a in (*args, *outs))
    whole = pl.BlockSpec(memory_space=pltpu.VMEM)
    smem = pl.BlockSpec(memory_space=pltpu.SMEM)
    return pl.pallas_call(
        body,
        out_shape=out_shape,
        in_specs=[smem] * len(smem_args) + [whole] * len(args),
        out_specs=jax.tree.map(lambda _: whole, out_shape),
        compiler_params=pltpu.CompilerParams(vmem_limit_bytes=PLAIN_VMEM),
        cost_estimate=pl.CostEstimate(flops=0, bytes_accessed=moved, transcendentals=0),
        name=name,
    )(*smem_args, *args)


def local(
    incident,
    initial,
    near_blocks,
    near_pattern,
    crack_blocks,
    crack_cluster,
    crack_source,
    crack_target,
    pulse_spectrum,
):
    panels, directions = incident.shape[2:]
    nblocks, span = near_blocks.shape[:2]
    width = near_blocks.shape[4]
    edges = crack_blocks.shape[0]
    front = 4
    near = near_blocks.reshape(nblocks, span, 2 * width, width)
    crack = crack_blocks.reshape(edges, 2 * width, width)
    near_idx, crack_idx = source_tables(
        near_pattern, crack_cluster[:, 0], crack_source, nblocks, front
    )
    tables = (near_idx.astype(jnp.int32), crack_idx.astype(jnp.int32), crack_target)
    incident, initial = incident[0], initial[0]
    lows = on_vmem(
        prepare_kernel,
        low_shapes(nblocks, width, 2 * directions, front),
        (),
        (initial,),
        "prepare",
    )

    place = lax.axis_index("frq") ^ jnp.arange(4, dtype=jnp.int32)
    real = jax.ShapeDtypeStruct((panels, directions), jnp.float32)
    send, keep = on_vmem(
        terms_kernel, (real, real), (place, pulse_spectrum), (initial,), "terms"
    )
    taken = swap(send, "frq", 1)
    here, away = on_vmem(mix_kernel, (real, real), (place,), (keep, taken), "mix")

    found, _, (here, away) = exchange(lows, (), (here, away))
    away = swap(away, "frq", 2)
    first, *lows, sums_one = apply_call(1, front, tables, near, crack, found, (incident, initial))

    first_sent, away, *lows = tie(first, away, *lows)
    first_across = swap(first_sent, "frq", 2)
    first_one = swap(first, "frq", 1)
    found, _, _ = exchange(lows)
    second, *lows, sums_two = apply_call(2, front, tables, near, crack, found, (first,))

    second_sent, first_across, *lows = tie(second, first_across, *lows)
    second_across = swap(second_sent, "frq", 2)
    found, (first_across,), _ = exchange(lows, (first_across,))
    parts, early, late = found
    first_three = swap(first_across, "frq", 1)
    second_across, first_three, *parts = tie(second_across, first_three, *parts)
    second_one, second_three = swap(second, "frq", 1), swap(second_across, "frq", 1)
    (sums_three,) = apply_call(
        3, front, tables, near, crack, (parts, early, late), (first, second)
    )
    sums_three, second_one, second_three = tie(sums_three, second_one, second_three)
    firsts = [first, first_one, first_across, first_three]
    seconds = [second, second_one, second_across, second_three]

    sums = sum_over_clusters(jnp.concatenate([sums_one, sums_two, sums_three], axis=0))
    row = jax.ShapeDtypeStruct((8, directions), jnp.float32)
    coefs, sent = on_vmem(
        functools.partial(small_kernel, len(sums)), (row, row), (pulse_spectrum,), sums, "small"
    )
    every = [sent, *(swap(sent, "frq", d) for d in (1, 2, 3))]
    scattered = on_vmem(
        scattered_kernel,
        jax.ShapeDtypeStruct(initial.shape, jnp.float32),
        (),
        (coefs, initial, first, second),
        "scattered",
    )
    trace = on_vmem(
        functools.partial(trace_kernel, len(firsts)),
        real,
        (place,),
        (here, away, *every, *firsts, *seconds),
        "trace",
    )
    return (scattered[None], trace[None])


def solution(mesh):
    in_specs = (
        P("frq", None, "clu", None),
        P("frq", None, "clu", None),
        P("clu", None, "frq", None, None, None),
        P("clu", None),
        P("clu", "frq", None, None, None),
        P("clu", None),
        P("clu"),
        P("clu"),
        P("frq", None),
    )
    out_specs = (P("frq", None, "clu", None), P("frq", "clu", None))
    return jax.shard_map(local, mesh=mesh, in_specs=in_specs, out_specs=out_specs, check_vma=False)
```

```python
import functools

import jax
import jax.numpy as jnp
from jax import lax
from jax.experimental import pallas as pl
from jax.experimental.pallas import tpu as pltpu
from jax.sharding import PartitionSpec as P

EPS = 1e-06
MIB = 1024 * 1024
PLAIN_VMEM = 10 * MIB


def turn(rows):
    half = rows.shape[1] // 2
    return jnp.concatenate([-rows[:, half:], rows[:, :half]], axis=1)


def col_sum(rows):
    return jnp.sum(rows.reshape(rows.shape[0] // 8, 8, rows.shape[1]), axis=0)


def table_kernel(sizes, place, pattern, cluster, source, target, *outs):
    nblocks, span, edges, front, count, tuned_here = sizes
    near_a, crack_a, near_rows, near_mats, near_srcs, edge_rows, edge_mats, edge_srcs, numbers = outs
    me = place[0]
    odd = lax.rem(me, 2)
    cut = nblocks // 2
    limits = (2 * nblocks + cut, 6 * front) if tuned_here else (3 * nblocks, count * front)
    zeros = (nblocks - cut, 2 * front)

    def fill(i, carry):
        for rows, mats, srcs, zero in (
            (near_rows, near_mats, near_srcs, zeros[0]),
            (edge_rows, edge_mats, edge_srcs, zeros[1]),
        ):

            @pl.when(i < rows.shape[0])
            def _():
                rows[i] = 0
                mats[i] = 0
                srcs[i] = zero

        return carry

    lax.fori_loop(0, max(near_rows.shape[0], edge_rows.shape[0]), fill, 0)

    def note(lists, half, row, mat, src, late, found):
        rows, mats, srcs = lists
        spot = half * (rows.shape[0] // 2) + jnp.where(half == 0, found[0], found[1])

        @pl.when(late)
        def _():
            rows[spot] = row - half * cut
            mats[spot] = mat
            srcs[spot] = src

        step = jnp.where(late, 1, 0)
        return (
            found[0] + jnp.where(half == 0, step, 0),
            found[1] + jnp.where(half == 1, step, 0),
        )

    def near_one(i, found):
        value = pattern[i]
        side, block = value // nblocks, lax.rem(value, nblocks)
        beside = jnp.where(side == 2, 1 - odd, odd) if tuned_here else jnp.where(side == 2, 1, 0)
        spot = jnp.where(side == 1, 0, jnp.where(beside == 1, 1, 2)) * nblocks + block
        late = spot >= limits[0]
        near_a[i] = jnp.where(late, limits[0], spot)
        row = i // span
        half = jnp.where(row >= cut, 1, 0)
        lists = (near_rows, near_mats, near_srcs)
        return note(lists, half, row, i, spot - limits[0], late, found)

    none = (jnp.int32(0), jnp.int32(0))
    near_found = lax.fori_loop(0, nblocks * span, near_one, none)

    def edge_one(e, found):
        if tuned_here:
            offset = lax.rem(cluster[e] - me + count, count)
            offset = jnp.where(odd == 1, lax.rem(count - offset, count), offset)
            slot = jnp.int32(0)
            for position, distance in enumerate((0, 1, 7, 6, 2, 4, 3, 5)):
                slot = jnp.where(offset == distance, position, slot)
        else:
            slot = cluster[e]
        spot = slot * front + source[e]
        late = spot >= limits[1]
        crack_a[e] = jnp.where(late, limits[1], spot)
        row = target[e]
        half = jnp.where(row >= cut, 1, 0)
        lists = (edge_rows, edge_mats, edge_srcs)
        return note(lists, half, row, e, spot - limits[1], late, found)

    edge_found = lax.fori_loop(0, edges, edge_one, none)
    for half in range(2):
        numbers[half] = near_found[half]
        numbers[2 + half] = edge_found[half]


def table_call(me, pattern, cluster, source, target, nblocks, span, front):
    edges = cluster.shape[0]
    cut = nblocks // 2
    near_list = 2 * max(cut, nblocks - cut) * span
    lengths = (nblocks * span, edges, *(near_list,) * 3, *(2 * edges,) * 3, 4)
    smem = pl.BlockSpec(memory_space=pltpu.SMEM)
    sizes = (nblocks, span, edges, front, lax.axis_size("clu"), tuned())
    return pl.pallas_call(
        functools.partial(table_kernel, sizes),
        out_shape=tuple(jax.ShapeDtypeStruct((length,), jnp.int32) for length in lengths),
        in_specs=[smem] * 5,
        out_specs=tuple(smem for _ in lengths),
        name="tables",
    )(me, pattern, cluster, source, target)


def block_copies(parts, moves, target, sems):
    return [
        pltpu.make_async_copy(
            parts[part].at[pl.ds(begin, count)], target.at[pl.ds(offset, count)], sems.at[place]
        )
        for place, (part, begin, count, offset) in enumerate(moves)
    ]


def total_of(moves):
    return sum(move[2] for move in moves)


GROUP = 4
REST_COST = 3


def main_kernel(sizes, moves, *refs):
    nblocks, span, edges, front_moves, source_moves, nparts = (*sizes, *moves)
    near_idx, crack_idx, crack_tgt, near_v, crack_v = refs[:5]
    parts = refs[5 : 5 + nparts]
    acc_a, acc_b, front_v, source_v, front_sem, source_sem = refs[5 + nparts :]
    cut = acc_a.shape[0]
    front_copies = block_copies(parts, front_moves, front_v, front_sem)
    source_copies = block_copies(parts, source_moves, source_v, source_sem)
    for copy in source_copies + front_copies:
        copy.start()
    for store in (front_v, source_v):
        store[store.shape[0] - 1] = jnp.zeros(store.shape[1:], store.dtype)
    for copy in source_copies:
        copy.wait()

    def row(acc, start, g, carry):
        left = jnp.concatenate([near_v[g, s] for s in range(span)], axis=1)
        right = jnp.concatenate([source_v[near_idx[g * span + s]] for s in range(span)], axis=0)
        acc[g - start] = jnp.dot(left, right, preferred_element_type=jnp.float32)
        return carry

    lax.fori_loop(0, cut, functools.partial(row, acc_a, 0), 0, unroll=2)
    lax.fori_loop(cut, nblocks, functools.partial(row, acc_b, cut), 0, unroll=2)
    for copy in front_copies:
        copy.wait()

    def crack_edges(i, carry):
        products = [
            jnp.dot(
                crack_v[i * GROUP + k],
                front_v[crack_idx[i * GROUP + k]],
                preferred_element_type=jnp.float32,
            )
            for k in range(GROUP)
        ]
        for k in range(GROUP):
            target = crack_tgt[i * GROUP + k]

            @pl.when(target < cut)
            def _():
                acc_a[target] += products[k]

            @pl.when(target >= cut)
            def _():
                acc_b[target - cut] += products[k]

        return carry

    lax.fori_loop(0, edges // GROUP, crack_edges, 0)


def main_call(step, tables, near, crack, found):
    parts, front_moves, source_moves = found[:3]
    nblocks, span = near.shape[:2]
    edges, width = crack.shape[0], near.shape[3]
    lanes = parts[0].shape[2]
    cut = nblocks // 2
    smem = pl.BlockSpec(memory_space=pltpu.SMEM)
    anywhere = pl.BlockSpec(memory_space=pl.ANY)
    whole = pl.BlockSpec(memory_space=pltpu.VMEM)
    blocks = total_of(front_moves) + total_of(source_moves) + 2
    return pl.pallas_call(
        functools.partial(
            main_kernel, (nblocks, span, edges), (front_moves, source_moves, len(parts))
        ),
        out_shape=tuple(
            jax.ShapeDtypeStruct((rows, 2 * width, lanes), jnp.float32)
            for rows in (cut, nblocks - cut)
        ),
        in_specs=[smem] * 3 + [whole] * 2 + [anywhere] * len(parts),
        out_specs=(whole, whole),
        scratch_shapes=[
            pltpu.VMEM((total_of(front_moves) + 1, width, lanes), jnp.bfloat16),
            pltpu.VMEM((total_of(source_moves) + 1, width, lanes), jnp.bfloat16),
            pltpu.SemaphoreType.DMA((len(front_moves),)),
            pltpu.SemaphoreType.DMA((len(source_moves),)),
        ],
        compiler_params=pltpu.CompilerParams(
            vmem_limit_bytes=2 * blocks * width * lanes + 2 * MIB
        ),
        cost_estimate=pl.CostEstimate(
            flops=4 * width * width * lanes * (nblocks * span + edges),
            bytes_accessed=near.size * 2 + crack.size * 2,
            transcendentals=0,
        ),
        name=f"operator_{step}",
    )(tables[0], tables[1], tables[-1], near, crack, *parts)


def rest_kernel(step, part, sizes, moves, *refs):
    nblocks, span, width, front, start, nrows = sizes
    near_moves, edge_moves, nparts = moves
    lists, rest = refs[:7], refs[7:]
    near_v, crack_v, acc = rest[:3]
    parts, rest = rest[3 : 3 + nparts], rest[3 + nparts :]
    nextra = 2 if step == 3 else 1
    extras, rest = rest[:nextra], rest[nextra:]
    before = ()
    if part == 1:
        nbefore = 1 if step == 3 else 2
        before, rest = rest[:nbefore], rest[nbefore:]
    nouts = 1 if step == 3 else (4, 3)[part]
    outs, rest = rest[:nouts], rest[nouts:]
    numbers = lists[6]
    lanes = acc.shape[2]
    late = nparts > 0
    if late:
        near_src, edge_src, extra, near_sem, edge_sem = rest
        copies = block_copies(parts, near_moves, near_src, near_sem)
        copies += block_copies(parts, edge_moves, edge_src, edge_sem)
        for copy in copies:
            copy.start()
        extra[...] = jnp.zeros(extra.shape, jnp.float32)
        for store in (near_src, edge_src):
            store[store.shape[0] - 1] = jnp.zeros(store.shape[1:], store.dtype)
        for copy in copies:
            copy.wait()

        def add(rows, mats, srcs, number, matrix, source):
            offset = part * (rows.shape[0] // 2)

            def some(i, carry):
                spots = [offset + i * GROUP + k for k in range(GROUP)]
                products = [
                    jnp.dot(
                        matrix(mats[spot]), source[srcs[spot]], preferred_element_type=jnp.float32
                    )
                    for spot in spots
                ]
                for spot, product in zip(spots, products):
                    extra[rows[spot]] += product
                return carry

            lax.fori_loop(0, (number + GROUP - 1) // GROUP, some, 0)

        add(
            *lists[:3],
            numbers[part],
            lambda i: near_v[i // span, lax.rem(i, span)],
            near_src,
        )
        add(*lists[3:6], numbers[2 + part], lambda i: crack_v[i], edge_src)

    nsums = (1, 3, 5)[step - 1]
    zero = jnp.zeros((8, lanes), jnp.float32)

    def row(g, sums):
        total = acc[g] + extra[g] if late else acc[g]
        new = total[:width] + turn(total[width:])
        rows = pl.ds(pl.multiple_of((start + g) * width, width), width)
        if step == 1:
            new = extras[0][rows, :] - new
            terms = (new * new,)
        elif step == 2:
            first = extras[0][rows, :]
            terms = (first * new, first * turn(new), new * new)
        else:
            first, second, turned = extras[0][rows, :], extras[1][rows, :], turn(new)
            terms = (first * new, first * turned, second * new, second * turned, new * new)
        if step != 3:
            outs[0][rows, :] = new
            rounded = new.astype(jnp.bfloat16)
            outs[1][g] = rounded
            if part == 0:

                @pl.when(g < front)
                def _():
                    outs[2][g] = rounded

        return tuple(total + col_sum(term) for total, term in zip(sums, terms))

    sums = lax.fori_loop(0, nrows, row, (zero,) * nsums, unroll=2)
    sums = [jnp.sum(total, axis=0, keepdims=True) for total in sums]
    sums.append(jnp.zeros((8 - nsums, lanes), jnp.float32))
    sums = jnp.concatenate(sums, axis=0)
    if part == 1:
        sums = sums + before[-1][...]
        if step != 3:
            outs[0][: before[0].shape[0], :] = before[0][...]
    outs[-1][...] = sums


def rest_call(step, part, front, tables, near, crack, found, acc, extras, before=()):
    _, _, _, parts, near_moves, edge_moves = found
    nblocks, span = near.shape[:2]
    width, lanes = near.shape[3], acc.shape[2]
    nrows = acc.shape[0]
    start = part * (nblocks // 2)
    out_shape = [jax.ShapeDtypeStruct((8, lanes), jnp.float32)]
    if step != 3:
        ends = start + nrows
        vector = jax.ShapeDtypeStruct((ends * width, lanes), jnp.float32)
        low_a, low_b, head = low_shapes(nblocks, width, lanes, front)
        out_shape = [vector, *((low_a, head), (low_b,))[part], *out_shape]
    smem = pl.BlockSpec(memory_space=pltpu.SMEM)
    anywhere = pl.BlockSpec(memory_space=pl.ANY)
    whole = pl.BlockSpec(memory_space=pltpu.VMEM)
    scratch, held = [], 0
    if parts:
        shapes = (total_of(near_moves) + 1, total_of(edge_moves) + 1)
        scratch = [pltpu.VMEM((n, width, lanes), jnp.bfloat16) for n in shapes]
        scratch += [
            pltpu.VMEM(acc.shape, jnp.float32),
            pltpu.SemaphoreType.DMA((len(near_moves),)),
            pltpu.SemaphoreType.DMA((len(edge_moves),)),
        ]
        held = 2 * sum(shapes) * width * lanes + 4 * acc.size
    return pl.pallas_call(
        functools.partial(
            rest_kernel,
            step,
            part,
            (nblocks, span, width, front, start, nrows),
            (near_moves, edge_moves, len(parts)),
        ),
        out_shape=tuple(out_shape),
        in_specs=[smem] * 7
        + [whole] * 3
        + [anywhere] * len(parts)
        + [whole] * (len(extras) + len(before)),
        out_specs=tuple(whole for _ in out_shape),
        scratch_shapes=scratch,
        compiler_params=pltpu.CompilerParams(vmem_limit_bytes=held + 2 * MIB),
        cost_estimate=pl.CostEstimate(
            flops=4 * width * width * lanes * nrows * span // 4,
            bytes_accessed=REST_COST * acc.size * 4,
            transcendentals=0,
        ),
        name=f"rest_{step}_{part}",
    )(*tables[2:9], near, crack, acc, *parts, *extras, *before)


def low_shapes(nblocks, width, lanes, front):
    cut = nblocks // 2
    return tuple(
        jax.ShapeDtypeStruct((count, width, lanes), jnp.bfloat16)
        for count in (cut, nblocks - cut, front)
    )


def prepare_kernel(initial, low_a, low_b, head):
    width = low_a.shape[1]

    def one(target, start, g, carry):
        rows = pl.ds(pl.multiple_of((start + g) * width, width), width)
        rounded = jnp.concatenate([initial[0, rows], initial[1, rows]], axis=1)
        target[g] = rounded.astype(jnp.bfloat16)
        return carry

    cut = low_a.shape[0]
    lax.fori_loop(0, cut, functools.partial(one, low_a, 0), 0)
    lax.fori_loop(0, low_b.shape[0], functools.partial(one, low_b, cut), 0)
    lax.fori_loop(0, head.shape[0], functools.partial(one, head, 0), 0)


def swap(value, axis, distance):
    count = lax.axis_size(axis)
    return lax.ppermute(value, axis, [(i, i ^ distance) for i in range(count)])


def shift(value, axis, distance):
    count = lax.axis_size(axis)
    return lax.ppermute(value, axis, [(i, (i + distance) % count) for i in range(count)])


def ring(value, distance):
    count = lax.axis_size("clu")
    pairs = [(i, (i + (-distance if i % 2 else distance)) % count) for i in range(count)]
    return lax.ppermute(value, "clu", pairs)


def tuned():
    return lax.axis_size("clu") == 8


def tie(*values):
    return lax.optimization_barrier(values)


def exchange(lows, early_ties=(), late_ties=()):
    low_a, low_b, head = lows
    cut, rest, front = (low.shape[0] for low in lows)
    nblocks = cut + rest
    if not tuned():
        count = lax.axis_size("clu")
        if callable(late_ties):
            late_ties = late_ties(early_ties)
        low = jnp.concatenate([low_a, low_b], axis=0)
        every = lax.all_gather(head, "clu", axis=0, tiled=True)
        parts = [low, shift(low, "clu", -1), shift(low, "clu", 1), every]
        source_moves = tuple((k, 0, nblocks, k * nblocks) for k in range(3))
        found = (parts, ((3, 0, count * front, 0),), source_moves, [], (), ())
        return found, early_ties, late_ties
    beside_a = swap(low_a, "clu", 1)
    same = ring(head, 2)
    other = ring(head, -2)
    tail, beside_a, same, other, *early_ties = tie(low_b, beside_a, same, other, *early_ties)
    onward = jnp.concatenate([beside_a, same], axis=0)
    beyond_a = ring(onward, 2)
    beside_b = swap(tail, "clu", 1)
    if callable(late_ties):
        late_ties = late_ties(early_ties)
    beside_b, *late_ties = tie(beside_b, *late_ties)
    beyond_b = ring(beside_b, 2)
    pairs = swap(jnp.concatenate([same, beyond_a[cut:]], axis=0), "clu", 1)
    parts = [low_a, low_b, beside_a, beside_b, beyond_a, same, other]
    front_moves = tuple(
        (part, begin, front, place * front)
        for place, (part, begin) in enumerate(
            [(0, 0), (2, 0), (4, 0), (5, 0), (6, 0), (4, cut)]
        )
    )
    source_moves = (
        (0, 0, cut, 0),
        (1, 0, rest, cut),
        (2, 0, cut, nblocks),
        (3, 0, rest, nblocks + cut),
        (4, 0, cut, 2 * nblocks),
    )
    last = [beyond_b, pairs]
    found = (parts, front_moves, source_moves, last, ((0, 0, rest, 0),), ((1, 0, 2 * front, 0),))
    return found, early_ties, late_ties


def sum_over_clusters(value, *tied):
    if not tuned():
        return [lax.psum(value, "clu")], tied
    value, *tied = tie(value + swap(value, "clu", 1), *tied)
    return [value, *(shift(value, "clu", d) for d in (2, 4, 6))], tied


def cmul(a, b):
    return (a[0] * b[0] - a[1] * b[1], a[0] * b[1] + a[1] * b[0])


def cjmul(a, b):
    return (a[0] * b[0] + a[1] * b[1], a[0] * b[1] - a[1] * b[0])


def cadd(*terms):
    return (sum(t[0] for t in terms), sum(t[1] for t in terms))


def scale(factor, a):
    return (factor * a[0], factor * a[1])


def norm2(a):
    return a[0] * a[0] + a[1] * a[1]


def least_squares(beta_norm, first_h, sub_one, second_h, third_h, sub_two):
    r_one = jnp.sqrt(first_h[0] ** 2 + first_h[1] ** 2 + sub_one**2)
    q_real = first_h[0] / r_one
    q_imag = first_h[1] / r_one
    q_low = sub_one / r_one
    mix_real = q_real * second_h[0] + q_imag * second_h[1] + q_low * third_h[0]
    mix_imag = q_real * second_h[1] - q_imag * second_h[0] + q_low * third_h[1]
    top_real = second_h[0] - (mix_real * q_real - mix_imag * q_imag)
    top_imag = second_h[1] - (mix_real * q_imag + mix_imag * q_real)
    mid_real = third_h[0] - mix_real * q_low
    mid_imag = third_h[1] - mix_imag * q_low
    r_two_sq = top_real**2 + top_imag**2 + mid_real**2 + mid_imag**2 + sub_two**2
    later_real = beta_norm * top_real / r_two_sq
    later_imag = -beta_norm * top_imag / r_two_sq
    early_real = (beta_norm * q_real - (mix_real * later_real - mix_imag * later_imag)) / r_one
    early_imag = (-beta_norm * q_imag - (mix_real * later_imag + mix_imag * later_real)) / r_one
    return ((early_real, early_imag), (later_real, later_imag))


def combine(g00, g01, g11, g02, g12, g22):
    beta2 = g00 + EPS
    beta = jnp.sqrt(beta2)
    h11 = ((0.5 * g00 + g01[0]) / beta2, g01[1] / beta2)
    s = (0.5 - h11[0], -h11[1])
    s01 = cjmul(s, g01)
    w2w2 = g11 + 2.0 * s01[0] + norm2(s) * g00
    h21 = jnp.sqrt(jnp.maximum(w2w2 / beta2, 0.0) + EPS)
    k = 1.0 / (beta * h21)
    d = (s[0] + 0.5, s[1])
    e = scale(0.5, s)
    r0u = cadd(g02, cmul(d, g01), scale(g00, e))
    z1u = cadd(g12, scale(g11, d), cmul(e, (g01[0], -g01[1])))
    h12 = scale(k / beta, r0u)
    h22 = scale(k * k, cadd(z1u, cjmul(s, r0u)))
    uu = (
        g22
        + norm2(d) * g11
        + norm2(e) * g00
        + 2.0 * cjmul(d, g12)[0]
        + 2.0 * cjmul(e, g02)[0]
        + 2.0 * cjmul(e, cmul(d, g01))[0]
    )
    n11 = g00 / beta2
    n22 = k * k * w2w2
    n12 = scale(k / beta, cadd(g01, scale(g00, s)))
    rest = (
        k * k * uu
        + norm2(h12) * (n11 - 2.0)
        + norm2(h22) * (n22 - 2.0)
        + 2.0 * cmul(cjmul(h12, h22), n12)[0]
    )
    h32 = jnp.sqrt(jnp.maximum(rest, 0.0) + EPS)
    early, later = least_squares(beta, h11, h21, h12, h22, h32)
    b = scale(k, later)
    a = cadd(scale(1.0 / beta, early), cmul(b, s))
    return a, b


def small_kernel(nsums, pulse, *refs):
    coefs, sent = refs[nsums:]
    sums = refs[0][...]
    for other in refs[1:nsums]:
        sums = sums + other[...]
    half = sums.shape[1] // 2
    sums = sums[:, :half] + sums[:, half:]

    def row(i):
        return sums[i : i + 1]

    a, b = combine(
        row(0),
        (row(8), -row(9)),
        row(10),
        (row(16), -row(17)),
        (row(18), -row(19)),
        row(20),
    )
    zero = jnp.zeros((4, half), jnp.float32)
    coefs[...] = jnp.concatenate([*a, *b, zero], axis=0)
    factor = (pulse[0, 0], pulse[0, 1])
    sent[...] = jnp.concatenate([*cmul(factor, a), *cmul(factor, b), zero], axis=0)


def scattered_kernel(coefs, initial, first, second, scattered):
    half = initial.shape[2]
    a = (coefs[0:1], coefs[1:2])
    b = (coefs[2:3], coefs[3:4])
    width = 256

    def one(g, carry):
        rows = pl.ds(pl.multiple_of(g * width, width), width)
        x, y = first[rows, :], second[rows, :]
        xr, xi, yr, yi = x[:, :half], x[:, half:], y[:, :half], y[:, half:]
        scattered[0, rows, :] = initial[0, rows] + a[0] * xr - a[1] * xi + b[0] * yr - b[1] * yi
        scattered[1, rows, :] = initial[1, rows] + a[0] * xi + a[1] * xr + b[0] * yi + b[1] * yr
        return carry

    lax.fori_loop(0, first.shape[0] // width, one, 0)


def power_of_i(exponent):
    exponent = lax.rem(exponent, 4)
    real = jnp.where(exponent == 0, 1.0, jnp.where(exponent == 2, -1.0, 0.0))
    imag = jnp.where(exponent == 1, 1.0, jnp.where(exponent == 3, -1.0, 0.0))
    return real, imag


def terms_kernel(place, pulse, initial, send, keep):
    width = 256
    f, core = place[0], lax.rem(place[0], 2)
    factor = (pulse[0, 0], pulse[0, 1])
    sent = cmul(factor, power_of_i((1 - core) * f))
    kept = cmul(factor, power_of_i(core * f))

    def one(g, carry):
        rows = pl.ds(pl.multiple_of(g * width, width), width)
        real, imag = initial[0, rows], initial[1, rows]
        send[rows, :] = sent[0] * real - sent[1] * imag
        keep[rows, :] = kept[0] * real - kept[1] * imag
        return carry

    lax.fori_loop(0, initial.shape[1] // width, one, 0)


def base_kernel(incident, initial, base):
    width = 256

    def one(g, carry):
        rows = pl.ds(pl.multiple_of(g * width, width), width)
        base[rows, :] = jnp.concatenate(
            [incident[half, rows] - 0.5 * initial[half, rows] for half in range(2)], axis=1
        )
        return carry

    lax.fori_loop(0, base.shape[0] // width, one, 0)


def mix_kernel(place, keep, taken, here, away):
    side, sign = place[0] // 2, 1.0 - 2.0 * lax.rem(place[0], 2).astype(jnp.float32)
    near_sign, far_sign = jnp.where(side == 1, sign, 1.0), jnp.where(side == 0, sign, 1.0)
    near_other, far_other = jnp.where(side == 1, -sign, 1.0), jnp.where(side == 0, -sign, 1.0)
    here[...] = near_sign * keep[...] + near_other * taken[...]
    away[...] = far_sign * keep[...] + far_other * taken[...]


def trace_kernel(count, place, here, away, *refs):
    coefs, firsts, seconds = refs[:count], refs[count : 2 * count], refs[2 * count : 3 * count]
    trace = refs[3 * count]
    half = trace.shape[1]
    width = 256
    weights = []
    for k in range(count):
        turned = power_of_i(place[0] * place[k])
        values = coefs[k][...]
        weights.append(
            (
                cmul(turned, (values[0:1], values[1:2])),
                cmul(turned, (values[2:3], values[3:4])),
            )
        )

    def one(g, carry):
        rows = pl.ds(pl.multiple_of(g * width, width), width)
        total = here[rows, :] + away[rows, :]
        for k in range(count):
            a, b = weights[k]
            x, y = firsts[k][rows, :], seconds[k][rows, :]
            total = total + (a[0] * x[:, :half] - a[1] * x[:, half:])
            total = total + (b[0] * y[:, :half] - b[1] * y[:, half:])
        trace[rows, :] = total
        return carry

    lax.fori_loop(0, trace.shape[0] // width, one, 0)


def on_vmem(body, out_shape, smem_args, args, name):
    outs = jax.tree.leaves(out_shape)
    moved = sum(a.size * a.dtype.itemsize for a in (*args, *outs))
    whole = pl.BlockSpec(memory_space=pltpu.VMEM)
    smem = pl.BlockSpec(memory_space=pltpu.SMEM)
    return pl.pallas_call(
        body,
        out_shape=out_shape,
        in_specs=[smem] * len(smem_args) + [whole] * len(args),
        out_specs=jax.tree.map(lambda _: whole, out_shape),
        compiler_params=pltpu.CompilerParams(vmem_limit_bytes=PLAIN_VMEM),
        cost_estimate=pl.CostEstimate(flops=0, bytes_accessed=moved, transcendentals=0),
        name=name,
    )(*smem_args, *args)


def local(
    incident,
    initial,
    near_blocks,
    near_pattern,
    crack_blocks,
    crack_cluster,
    crack_source,
    crack_target,
    pulse_spectrum,
):
    panels, directions = incident.shape[2:]
    nblocks, span = near_blocks.shape[:2]
    width = near_blocks.shape[4]
    edges = crack_blocks.shape[0]
    front = 4
    near = near_blocks.reshape(nblocks, span, 2 * width, width)
    crack = crack_blocks.reshape(edges, 2 * width, width)
    incident, initial = incident[0], initial[0]
    lows = on_vmem(
        prepare_kernel,
        low_shapes(nblocks, width, 2 * directions, front),
        (),
        (initial,),
        "prepare",
    )

    place = lax.axis_index("frq") ^ jnp.arange(4, dtype=jnp.int32)
    real = jax.ShapeDtypeStruct((panels, directions), jnp.float32)
    both = jax.ShapeDtypeStruct((panels, 2 * directions), jnp.float32)

    tables = table_call(
        lax.axis_index("clu").reshape(1),
        near_pattern.reshape(-1),
        crack_cluster[:, 0],
        crack_source,
        crack_target,
        nblocks,
        span,
        front,
    )

    found, (from_start, *tables), base = exchange(
        lows,
        (initial, *tables),
        lambda early: [on_vmem(base_kernel, both, (), (incident, early[0]), "base")],
    )
    base = base[0]
    tables = (*tables, crack_target)
    send, keep = on_vmem(
        terms_kernel, (real, real), (place, pulse_spectrum), (from_start,), "terms"
    )
    here, away = on_vmem(
        mix_kernel, (real, real), (place,), (keep, swap(send, "frq", 1)), "mix"
    )
    away = swap(away, "frq", 2)

    def operate(step, found, extras, *tied):
        acc_a, acc_b = main_call(step, tables, near, crack, found)
        both_halves = (front, tables, near, crack, found)
        if step == 3:
            (sums,) = rest_call(3, 0, *both_halves, acc_a, extras)
            (sums,) = rest_call(3, 1, *both_halves, acc_b, extras, (sums,))
            return sums, *tied
        upper, low_a, head, sums = rest_call(step, 0, *both_halves, acc_a, extras)
        vector, low_b, sums = rest_call(step, 1, *both_halves, acc_b, extras, (upper, sums))
        return vector, low_a, low_b, head, sums

    first, *lows, sums_one = operate(1, found, (base,))
    found, (first_sent, away), _ = exchange(lows, (first, away))
    first_across, first_one = swap(first_sent, "frq", 2), swap(first, "frq", 1)

    second, *lows, sums_two = operate(2, found, (first,))
    found, (second_sent, first_across), _ = exchange(lows, (second, first_across))
    second_across, first_three = swap(second_sent, "frq", 2), swap(first_across, "frq", 1)
    (sums_three,) = operate(3, found, (first, second))
    second_one = swap(second, "frq", 1)
    sums = jnp.concatenate([sums_one, sums_two, sums_three], axis=0)
    sums, (second_across, second_one, first_three) = sum_over_clusters(
        sums, second_across, second_one, first_three
    )
    second_three = swap(second_across, "frq", 1)
    firsts = [first, first_one, first_across, first_three]
    seconds = [second, second_one, second_across, second_three]

    row = jax.ShapeDtypeStruct((8, directions), jnp.float32)
    coefs, sent = on_vmem(
        functools.partial(small_kernel, len(sums)), (row, row), (pulse_spectrum,), sums, "small"
    )
    every = [sent, *(swap(sent, "frq", d) for d in (1, 2, 3))]
    scattered = on_vmem(
        scattered_kernel,
        jax.ShapeDtypeStruct(initial.shape, jnp.float32),
        (),
        (coefs, initial, first, second),
        "scattered",
    )
    trace = on_vmem(
        functools.partial(trace_kernel, len(firsts)),
        real,
        (place,),
        (here, away, *every, *firsts, *seconds),
        "trace",
    )
    return (scattered[None], trace[None])


def solution(mesh):
    in_specs = (
        P("frq", None, "clu", None),
        P("frq", None, "clu", None),
        P("clu", None, "frq", None, None, None),
        P("clu", None),
        P("clu", "frq", None, None, None),
        P("clu", None),
        P("clu"),
        P("clu"),
        P("frq", None),
    )
    out_specs = (P("frq", None, "clu", None), P("frq", "clu", None))
    return jax.shard_map(local, mesh=mesh, in_specs=in_specs, out_specs=out_specs, check_vma=False)
```

```python
import functools

import jax
import jax.numpy as jnp
from jax import lax
from jax.experimental import pallas as pl
from jax.experimental.pallas import tpu as pltpu
from jax.sharding import PartitionSpec as P

EPS = 1e-06
MIB = 1024 * 1024
PLAIN_VMEM = 10 * MIB


def turn(rows):
    half = rows.shape[1] // 2
    return jnp.concatenate([-rows[:, half:], rows[:, :half]], axis=1)


def col_sum(rows):
    return jnp.sum(rows.reshape(rows.shape[0] // 8, 8, rows.shape[1]), axis=0)


def table_kernel(sizes, place, pattern, cluster, source, target, *outs):
    nblocks, span, edges, front, count, tuned_here = sizes
    near_a, crack_a, near_rows, near_mats, near_srcs, edge_rows, edge_mats, edge_srcs, numbers = outs
    me = place[0]
    odd = lax.rem(me, 2)
    cut = nblocks // 2
    limits = (2 * nblocks + cut, 6 * front) if tuned_here else (3 * nblocks, count * front)
    zeros = (nblocks - cut, 2 * front)

    def fill(i, carry):
        for rows, mats, srcs, zero in (
            (near_rows, near_mats, near_srcs, zeros[0]),
            (edge_rows, edge_mats, edge_srcs, zeros[1]),
        ):

            @pl.when(i < rows.shape[0])
            def _():
                rows[i] = 0
                mats[i] = 0
                srcs[i] = zero

        return carry

    lax.fori_loop(0, max(near_rows.shape[0], edge_rows.shape[0]), fill, 0)

    def note(lists, half, row, mat, src, late, found):
        rows, mats, srcs = lists
        spot = half * (rows.shape[0] // 2) + jnp.where(half == 0, found[0], found[1])

        @pl.when(late)
        def _():
            rows[spot] = row - half * cut
            mats[spot] = mat
            srcs[spot] = src

        step = jnp.where(late, 1, 0)
        return (
            found[0] + jnp.where(half == 0, step, 0),
            found[1] + jnp.where(half == 1, step, 0),
        )

    def near_one(i, found):
        value = pattern[i]
        side, block = value // nblocks, lax.rem(value, nblocks)
        beside = jnp.where(side == 2, 1 - odd, odd) if tuned_here else jnp.where(side == 2, 1, 0)
        spot = jnp.where(side == 1, 0, jnp.where(beside == 1, 1, 2)) * nblocks + block
        late = spot >= limits[0]
        near_a[i] = jnp.where(late, limits[0], spot)
        row = i // span
        half = jnp.where(row >= cut, 1, 0)
        lists = (near_rows, near_mats, near_srcs)
        return note(lists, half, row, i, spot - limits[0], late, found)

    none = (jnp.int32(0), jnp.int32(0))
    near_found = lax.fori_loop(0, nblocks * span, near_one, none)

    def edge_one(e, found):
        if tuned_here:
            offset = lax.rem(cluster[e] - me + count, count)
            offset = jnp.where(odd == 1, lax.rem(count - offset, count), offset)
            slot = jnp.int32(0)
            for position, distance in enumerate((0, 1, 7, 6, 2, 4, 3, 5)):
                slot = jnp.where(offset == distance, position, slot)
        else:
            slot = cluster[e]
        spot = slot * front + source[e]
        late = spot >= limits[1]
        crack_a[e] = jnp.where(late, limits[1], spot)
        row = target[e]
        half = jnp.where(row >= cut, 1, 0)
        lists = (edge_rows, edge_mats, edge_srcs)
        return note(lists, half, row, e, spot - limits[1], late, found)

    edge_found = lax.fori_loop(0, edges, edge_one, none)
    for half in range(2):
        numbers[half] = near_found[half]
        numbers[2 + half] = edge_found[half]


def table_call(me, pattern, cluster, source, target, nblocks, span, front):
    edges = cluster.shape[0]
    cut = nblocks // 2
    near_list = 2 * max(cut, nblocks - cut) * span
    lengths = (nblocks * span, edges, *(near_list,) * 3, *(2 * edges,) * 3, 4)
    smem = pl.BlockSpec(memory_space=pltpu.SMEM)
    sizes = (nblocks, span, edges, front, lax.axis_size("clu"), tuned())
    return pl.pallas_call(
        functools.partial(table_kernel, sizes),
        out_shape=tuple(jax.ShapeDtypeStruct((length,), jnp.int32) for length in lengths),
        in_specs=[smem] * 5,
        out_specs=tuple(smem for _ in lengths),
        name="tables",
    )(me, pattern, cluster, source, target)


def block_copies(parts, moves, target, sems):
    return [
        pltpu.make_async_copy(
            parts[part].at[pl.ds(begin, count)], target.at[pl.ds(offset, count)], sems.at[place]
        )
        for place, (part, begin, count, offset) in enumerate(moves)
    ]


def total_of(moves):
    return sum(move[2] for move in moves)


GROUP = 4
REST_COST = 3


def main_kernel(sizes, moves, *refs):
    nblocks, span, edges, front_moves, source_moves, nparts = (*sizes, *moves)
    near_idx, crack_idx, crack_tgt, near_v, crack_v = refs[:5]
    parts = refs[5 : 5 + nparts]
    *accs, front_v, source_v, front_sem, source_sem = refs[5 + nparts :]
    cut = nblocks // 2
    if len(accs) == 1:
        accs = [accs[0].at[pl.ds(0, cut)], accs[0].at[pl.ds(cut, nblocks - cut)]]
    acc_a, acc_b = accs
    front_copies = block_copies(parts, front_moves, front_v, front_sem)
    source_copies = block_copies(parts, source_moves, source_v, source_sem)
    for copy in source_copies + front_copies:
        copy.start()
    for store in (front_v, source_v):
        store[store.shape[0] - 1] = jnp.zeros(store.shape[1:], store.dtype)
    for copy in source_copies:
        copy.wait()

    def row(acc, start, g, carry):
        left = jnp.concatenate([near_v[g, s] for s in range(span)], axis=1)
        right = jnp.concatenate([source_v[near_idx[g * span + s]] for s in range(span)], axis=0)
        acc[g - start] = jnp.dot(left, right, preferred_element_type=jnp.float32)
        return carry

    lax.fori_loop(0, cut, functools.partial(row, acc_a, 0), 0, unroll=2)
    lax.fori_loop(cut, nblocks, functools.partial(row, acc_b, cut), 0, unroll=2)
    for copy in front_copies:
        copy.wait()

    def crack_edges(i, carry):
        products = [
            jnp.dot(
                crack_v[i * GROUP + k],
                front_v[crack_idx[i * GROUP + k]],
                preferred_element_type=jnp.float32,
            )
            for k in range(GROUP)
        ]
        for k in range(GROUP):
            target = crack_tgt[i * GROUP + k]

            @pl.when(target < cut)
            def _():
                acc_a[target] += products[k]

            @pl.when(target >= cut)
            def _():
                acc_b[target - cut] += products[k]

        return carry

    lax.fori_loop(0, edges // GROUP, crack_edges, 0)


def main_call(step, tables, near, crack, found):
    parts, front_moves, source_moves = found[:3]
    nblocks, span = near.shape[:2]
    edges, width = crack.shape[0], near.shape[3]
    lanes = parts[0].shape[2]
    cut = nblocks // 2
    smem = pl.BlockSpec(memory_space=pltpu.SMEM)
    anywhere = pl.BlockSpec(memory_space=pl.ANY)
    whole = pl.BlockSpec(memory_space=pltpu.VMEM)
    blocks = total_of(front_moves) + total_of(source_moves) + 2
    counts = (nblocks,) if step == 3 else (cut, nblocks - cut)
    return pl.pallas_call(
        functools.partial(
            main_kernel, (nblocks, span, edges), (front_moves, source_moves, len(parts))
        ),
        out_shape=tuple(
            jax.ShapeDtypeStruct((rows, 2 * width, lanes), jnp.float32)
            for rows in counts
        ),
        in_specs=[smem] * 3 + [whole] * 2 + [anywhere] * len(parts),
        out_specs=tuple(whole for _ in counts),
        scratch_shapes=[
            pltpu.VMEM((total_of(front_moves) + 1, width, lanes), jnp.bfloat16),
            pltpu.VMEM((total_of(source_moves) + 1, width, lanes), jnp.bfloat16),
            pltpu.SemaphoreType.DMA((len(front_moves),)),
            pltpu.SemaphoreType.DMA((len(source_moves),)),
        ],
        compiler_params=pltpu.CompilerParams(
            vmem_limit_bytes=2 * blocks * width * lanes + 2 * MIB
        ),
        cost_estimate=pl.CostEstimate(
            flops=4 * width * width * lanes * (nblocks * span + edges),
            bytes_accessed=near.size * 2 + crack.size * 2,
            transcendentals=0,
        ),
        name=f"operator_{step}",
    )(tables[0], tables[1], tables[-1], near, crack, *parts)


def rest_kernel(step, part, sizes, moves, *refs):
    nblocks, span, width, front, start, nrows = sizes
    near_moves, edge_moves, nparts = moves
    lists, rest = refs[:7], refs[7:]
    near_v, crack_v, acc = rest[:3]
    parts, rest = rest[3 : 3 + nparts], rest[3 + nparts :]
    nextra = 2 if step == 3 else 1
    extras, rest = rest[:nextra], rest[nextra:]
    before = ()
    if part == 1:
        nbefore = 2
        before, rest = rest[:nbefore], rest[nbefore:]
    nouts = 1 if step == 3 else (4, 3)[part]
    outs, rest = rest[:nouts], rest[nouts:]
    numbers = lists[6]
    lanes = acc.shape[2]
    late = nparts > 0
    if late:
        near_src, edge_src, extra, near_sem, edge_sem = rest
        copies = block_copies(parts, near_moves, near_src, near_sem)
        copies += block_copies(parts, edge_moves, edge_src, edge_sem)
        for copy in copies:
            copy.start()
        extra[...] = jnp.zeros(extra.shape, jnp.float32)
        for store in (near_src, edge_src):
            store[store.shape[0] - 1] = jnp.zeros(store.shape[1:], store.dtype)
        for copy in copies:
            copy.wait()

        def add(half, rows, mats, srcs, number, matrix, source):
            offset = half * (rows.shape[0] // 2)
            shift_by = half * (nblocks // 2) if step == 3 else 0

            def some(i, carry):
                spots = [offset + i * GROUP + k for k in range(GROUP)]
                products = [
                    jnp.dot(
                        matrix(mats[spot]), source[srcs[spot]], preferred_element_type=jnp.float32
                    )
                    for spot in spots
                ]
                for spot, product in zip(spots, products):
                    extra[rows[spot] + shift_by] += product
                return carry

            lax.fori_loop(0, (number + GROUP - 1) // GROUP, some, 0)

        for half in (0, 1) if step == 3 else (part,):
            add(
                half,
                *lists[:3],
                numbers[half],
                lambda i: near_v[i // span, lax.rem(i, span)],
                near_src,
            )
            add(half, *lists[3:6], numbers[2 + half], lambda i: crack_v[i], edge_src)

    nsums = (1, 3, 5)[step - 1]
    zero = jnp.zeros((8, lanes), jnp.float32)

    def row(g, sums):
        total = acc[g] + extra[g] if late else acc[g]
        new = total[:width] + turn(total[width:])
        rows = pl.ds(pl.multiple_of((start + g) * width, width), width)
        if step == 1:
            new = extras[0][rows, :] - new
            terms = (new * new,)
        elif step == 2:
            first = extras[0][rows, :]
            terms = (first * new, first * turn(new), new * new)
        else:
            first, second, turned = extras[0][rows, :], extras[1][rows, :], turn(new)
            terms = (first * new, first * turned, second * new, second * turned, new * new)
        if step != 3:
            outs[0][rows, :] = new
            rounded = new.astype(jnp.bfloat16)
            outs[1][g] = rounded
            if part == 0:

                @pl.when(g < front)
                def _():
                    outs[2][g] = rounded

        return tuple(total + col_sum(term) for total, term in zip(sums, terms))

    sums = lax.fori_loop(0, nrows, row, (zero,) * nsums, unroll=2)
    sums = [jnp.sum(total, axis=0, keepdims=True) for total in sums]
    sums.append(jnp.zeros((8 - nsums, lanes), jnp.float32))
    sums = jnp.concatenate(sums, axis=0)
    if part == 1:
        sums = sums + before[-1][...]
        if step != 3:
            outs[0][: before[0].shape[0], :] = before[0][...]
    outs[-1][...] = sums


def rest_call(step, part, front, tables, near, crack, found, acc, extras, before=()):
    _, _, _, parts, near_moves, edge_moves = found
    nblocks, span = near.shape[:2]
    width, lanes = near.shape[3], acc.shape[2]
    nrows = acc.shape[0]
    start = part * (nblocks // 2)
    out_shape = [jax.ShapeDtypeStruct((8, lanes), jnp.float32)]
    if step != 3:
        ends = start + nrows
        vector = jax.ShapeDtypeStruct((ends * width, lanes), jnp.float32)
        low_a, low_b, head = low_shapes(nblocks, width, lanes, front)
        out_shape = [vector, *((low_a, head), (low_b,))[part], *out_shape]
    smem = pl.BlockSpec(memory_space=pltpu.SMEM)
    anywhere = pl.BlockSpec(memory_space=pl.ANY)
    whole = pl.BlockSpec(memory_space=pltpu.VMEM)
    scratch, held = [], 0
    if parts:
        shapes = (total_of(near_moves) + 1, total_of(edge_moves) + 1)
        scratch = [pltpu.VMEM((n, width, lanes), jnp.bfloat16) for n in shapes]
        scratch += [
            pltpu.VMEM(acc.shape, jnp.float32),
            pltpu.SemaphoreType.DMA((len(near_moves),)),
            pltpu.SemaphoreType.DMA((len(edge_moves),)),
        ]
        held = 2 * sum(shapes) * width * lanes + 4 * acc.size
    return pl.pallas_call(
        functools.partial(
            rest_kernel,
            step,
            part,
            (nblocks, span, width, front, start, nrows),
            (near_moves, edge_moves, len(parts)),
        ),
        out_shape=tuple(out_shape),
        in_specs=[smem] * 7
        + [whole] * 3
        + [anywhere] * len(parts)
        + [whole] * (len(extras) + len(before)),
        out_specs=tuple(whole for _ in out_shape),
        scratch_shapes=scratch,
        compiler_params=pltpu.CompilerParams(vmem_limit_bytes=held + 2 * MIB),
        cost_estimate=pl.CostEstimate(
            flops=4 * width * width * lanes * nrows * span // 4,
            bytes_accessed=REST_COST * acc.size * 4,
            transcendentals=0,
        ),
        name=f"rest_{step}_{part}",
    )(*tables[2:9], near, crack, acc, *parts, *extras, *before)


def low_shapes(nblocks, width, lanes, front):
    cut = nblocks // 2
    return tuple(
        jax.ShapeDtypeStruct((count, width, lanes), jnp.bfloat16)
        for count in (cut, nblocks - cut, front)
    )


def prepare_kernel(initial, low_a, low_b, head):
    width = low_a.shape[1]

    def one(target, start, g, carry):
        rows = pl.ds(pl.multiple_of((start + g) * width, width), width)
        rounded = jnp.concatenate([initial[0, rows], initial[1, rows]], axis=1)
        target[g] = rounded.astype(jnp.bfloat16)
        return carry

    cut = low_a.shape[0]
    lax.fori_loop(0, cut, functools.partial(one, low_a, 0), 0)
    lax.fori_loop(0, low_b.shape[0], functools.partial(one, low_b, cut), 0)
    lax.fori_loop(0, head.shape[0], functools.partial(one, head, 0), 0)


def swap(value, axis, distance):
    count = lax.axis_size(axis)
    return lax.ppermute(value, axis, [(i, i ^ distance) for i in range(count)])


def shift(value, axis, distance):
    count = lax.axis_size(axis)
    return lax.ppermute(value, axis, [(i, (i + distance) % count) for i in range(count)])


def ring(value, distance):
    count = lax.axis_size("clu")
    pairs = [(i, (i + (-distance if i % 2 else distance)) % count) for i in range(count)]
    return lax.ppermute(value, "clu", pairs)


def tuned():
    return lax.axis_size("clu") == 8


def tie(*values):
    return lax.optimization_barrier(values)


def exchange(lows, early_ties=(), late_ties=()):
    low_a, low_b, head = lows
    cut, rest, front = (low.shape[0] for low in lows)
    nblocks = cut + rest
    if not tuned():
        count = lax.axis_size("clu")
        if callable(late_ties):
            late_ties = late_ties(early_ties)
        low = jnp.concatenate([low_a, low_b], axis=0)
        every = lax.all_gather(head, "clu", axis=0, tiled=True)
        parts = [low, shift(low, "clu", -1), shift(low, "clu", 1), every]
        source_moves = tuple((k, 0, nblocks, k * nblocks) for k in range(3))
        found = (parts, ((3, 0, count * front, 0),), source_moves, [], (), ())
        return found, early_ties, late_ties
    beside_a = swap(low_a, "clu", 1)
    same = ring(head, 2)
    other = ring(head, -2)
    tail, beside_a, same, other = tie(low_b, beside_a, same, other)
    onward, *early_ties = tie(jnp.concatenate([beside_a, same], axis=0), *early_ties)
    beyond_a = ring(onward, 2)
    beside_b = swap(tail, "clu", 1)
    if callable(late_ties):
        late_ties = late_ties(early_ties)
    beside_b, *late_ties = tie(beside_b, *late_ties)
    beyond_b = ring(beside_b, 2)
    pairs = swap(jnp.concatenate([same, beyond_a[cut:]], axis=0), "clu", 1)
    parts = [low_a, low_b, beside_a, beside_b, beyond_a, same, other]
    front_moves = tuple(
        (part, begin, front, place * front)
        for place, (part, begin) in enumerate(
            [(0, 0), (2, 0), (4, 0), (5, 0), (6, 0), (4, cut)]
        )
    )
    source_moves = (
        (0, 0, cut, 0),
        (1, 0, rest, cut),
        (2, 0, cut, nblocks),
        (3, 0, rest, nblocks + cut),
        (4, 0, cut, 2 * nblocks),
    )
    last = [beyond_b, pairs]
    found = (parts, front_moves, source_moves, last, ((0, 0, rest, 0),), ((1, 0, 2 * front, 0),))
    return found, early_ties, late_ties


def sum_over_clusters(value, *tied):
    if not tuned():
        return [lax.psum(value, "clu")], tied
    value, *tied = tie(value + swap(value, "clu", 1), *tied)
    return [value, *(shift(value, "clu", d) for d in (2, 4, 6))], tied


def cmul(a, b):
    return (a[0] * b[0] - a[1] * b[1], a[0] * b[1] + a[1] * b[0])


def cjmul(a, b):
    return (a[0] * b[0] + a[1] * b[1], a[0] * b[1] - a[1] * b[0])


def cadd(*terms):
    return (sum(t[0] for t in terms), sum(t[1] for t in terms))


def scale(factor, a):
    return (factor * a[0], factor * a[1])


def norm2(a):
    return a[0] * a[0] + a[1] * a[1]


def least_squares(beta_norm, first_h, sub_one, second_h, third_h, sub_two):
    r_one = jnp.sqrt(first_h[0] ** 2 + first_h[1] ** 2 + sub_one**2)
    q_real = first_h[0] / r_one
    q_imag = first_h[1] / r_one
    q_low = sub_one / r_one
    mix_real = q_real * second_h[0] + q_imag * second_h[1] + q_low * third_h[0]
    mix_imag = q_real * second_h[1] - q_imag * second_h[0] + q_low * third_h[1]
    top_real = second_h[0] - (mix_real * q_real - mix_imag * q_imag)
    top_imag = second_h[1] - (mix_real * q_imag + mix_imag * q_real)
    mid_real = third_h[0] - mix_real * q_low
    mid_imag = third_h[1] - mix_imag * q_low
    r_two_sq = top_real**2 + top_imag**2 + mid_real**2 + mid_imag**2 + sub_two**2
    later_real = beta_norm * top_real / r_two_sq
    later_imag = -beta_norm * top_imag / r_two_sq
    early_real = (beta_norm * q_real - (mix_real * later_real - mix_imag * later_imag)) / r_one
    early_imag = (-beta_norm * q_imag - (mix_real * later_imag + mix_imag * later_real)) / r_one
    return ((early_real, early_imag), (later_real, later_imag))


def combine(g00, g01, g11, g02, g12, g22):
    beta2 = g00 + EPS
    beta = jnp.sqrt(beta2)
    h11 = ((0.5 * g00 + g01[0]) / beta2, g01[1] / beta2)
    s = (0.5 - h11[0], -h11[1])
    s01 = cjmul(s, g01)
    w2w2 = g11 + 2.0 * s01[0] + norm2(s) * g00
    h21 = jnp.sqrt(jnp.maximum(w2w2 / beta2, 0.0) + EPS)
    k = 1.0 / (beta * h21)
    d = (s[0] + 0.5, s[1])
    e = scale(0.5, s)
    r0u = cadd(g02, cmul(d, g01), scale(g00, e))
    z1u = cadd(g12, scale(g11, d), cmul(e, (g01[0], -g01[1])))
    h12 = scale(k / beta, r0u)
    h22 = scale(k * k, cadd(z1u, cjmul(s, r0u)))
    uu = (
        g22
        + norm2(d) * g11
        + norm2(e) * g00
        + 2.0 * cjmul(d, g12)[0]
        + 2.0 * cjmul(e, g02)[0]
        + 2.0 * cjmul(e, cmul(d, g01))[0]
    )
    n11 = g00 / beta2
    n22 = k * k * w2w2
    n12 = scale(k / beta, cadd(g01, scale(g00, s)))
    rest = (
        k * k * uu
        + norm2(h12) * (n11 - 2.0)
        + norm2(h22) * (n22 - 2.0)
        + 2.0 * cmul(cjmul(h12, h22), n12)[0]
    )
    h32 = jnp.sqrt(jnp.maximum(rest, 0.0) + EPS)
    early, later = least_squares(beta, h11, h21, h12, h22, h32)
    b = scale(k, later)
    a = cadd(scale(1.0 / beta, early), cmul(b, s))
    return a, b


def small_kernel(nsums, pulse, *refs):
    coefs, sent = refs[nsums:]
    sums = refs[0][...]
    for other in refs[1:nsums]:
        sums = sums + other[...]
    half = sums.shape[1] // 2
    sums = sums[:, :half] + sums[:, half:]

    def row(i):
        return sums[i : i + 1]

    a, b = combine(
        row(0),
        (row(8), -row(9)),
        row(10),
        (row(16), -row(17)),
        (row(18), -row(19)),
        row(20),
    )
    zero = jnp.zeros((4, half), jnp.float32)
    coefs[...] = jnp.concatenate([*a, *b, zero], axis=0)
    factor = (pulse[0, 0], pulse[0, 1])
    sent[...] = jnp.concatenate([*cmul(factor, a), *cmul(factor, b), zero], axis=0)


def scattered_kernel(coefs, initial, first, second, scattered):
    half = initial.shape[2]
    a = (coefs[0:1], coefs[1:2])
    b = (coefs[2:3], coefs[3:4])
    width = 256

    def one(g, carry):
        rows = pl.ds(pl.multiple_of(g * width, width), width)
        x, y = first[rows, :], second[rows, :]
        xr, xi, yr, yi = x[:, :half], x[:, half:], y[:, :half], y[:, half:]
        scattered[0, rows, :] = initial[0, rows] + a[0] * xr - a[1] * xi + b[0] * yr - b[1] * yi
        scattered[1, rows, :] = initial[1, rows] + a[0] * xi + a[1] * xr + b[0] * yi + b[1] * yr
        return carry

    lax.fori_loop(0, first.shape[0] // width, one, 0)


def power_of_i(exponent):
    exponent = lax.rem(exponent, 4)
    real = jnp.where(exponent == 0, 1.0, jnp.where(exponent == 2, -1.0, 0.0))
    imag = jnp.where(exponent == 1, 1.0, jnp.where(exponent == 3, -1.0, 0.0))
    return real, imag


def terms_kernel(place, pulse, initial, send, keep):
    width = 256
    f, core = place[0], lax.rem(place[0], 2)
    factor = (pulse[0, 0], pulse[0, 1])
    sent = cmul(factor, power_of_i((1 - core) * f))
    kept = cmul(factor, power_of_i(core * f))

    def one(g, carry):
        rows = pl.ds(pl.multiple_of(g * width, width), width)
        real, imag = initial[0, rows], initial[1, rows]
        send[rows, :] = sent[0] * real - sent[1] * imag
        keep[rows, :] = kept[0] * real - kept[1] * imag
        return carry

    lax.fori_loop(0, initial.shape[1] // width, one, 0)


def base_kernel(incident, initial, base):
    width = 256

    def one(g, carry):
        rows = pl.ds(pl.multiple_of(g * width, width), width)
        base[rows, :] = jnp.concatenate(
            [incident[half, rows] - 0.5 * initial[half, rows] for half in range(2)], axis=1
        )
        return carry

    lax.fori_loop(0, base.shape[0] // width, one, 0)


def mix_kernel(place, keep, taken, here, away):
    side, sign = place[0] // 2, 1.0 - 2.0 * lax.rem(place[0], 2).astype(jnp.float32)
    near_sign, far_sign = jnp.where(side == 1, sign, 1.0), jnp.where(side == 0, sign, 1.0)
    near_other, far_other = jnp.where(side == 1, -sign, 1.0), jnp.where(side == 0, -sign, 1.0)
    here[...] = near_sign * keep[...] + near_other * taken[...]
    away[...] = far_sign * keep[...] + far_other * taken[...]


def trace_kernel(count, place, here, away, *refs):
    coefs, firsts, seconds = refs[:count], refs[count : 2 * count], refs[2 * count : 3 * count]
    trace = refs[3 * count]
    half = trace.shape[1]
    width = 256
    weights = []
    for k in range(count):
        turned = power_of_i(place[0] * place[k])
        values = coefs[k][...]
        weights.append(
            (
                cmul(turned, (values[0:1], values[1:2])),
                cmul(turned, (values[2:3], values[3:4])),
            )
        )

    def one(g, carry):
        rows = pl.ds(pl.multiple_of(g * width, width), width)
        total = here[rows, :] + away[rows, :]
        for k in range(count):
            a, b = weights[k]
            x, y = firsts[k][rows, :], seconds[k][rows, :]
            total = total + (a[0] * x[:, :half] - a[1] * x[:, half:])
            total = total + (b[0] * y[:, :half] - b[1] * y[:, half:])
        trace[rows, :] = total
        return carry

    lax.fori_loop(0, trace.shape[0] // width, one, 0)


def on_vmem(body, out_shape, smem_args, args, name):
    outs = jax.tree.leaves(out_shape)
    moved = sum(a.size * a.dtype.itemsize for a in (*args, *outs))
    whole = pl.BlockSpec(memory_space=pltpu.VMEM)
    smem = pl.BlockSpec(memory_space=pltpu.SMEM)
    return pl.pallas_call(
        body,
        out_shape=out_shape,
        in_specs=[smem] * len(smem_args) + [whole] * len(args),
        out_specs=jax.tree.map(lambda _: whole, out_shape),
        compiler_params=pltpu.CompilerParams(vmem_limit_bytes=PLAIN_VMEM),
        cost_estimate=pl.CostEstimate(flops=0, bytes_accessed=moved, transcendentals=0),
        name=name,
    )(*smem_args, *args)


def local(
    incident,
    initial,
    near_blocks,
    near_pattern,
    crack_blocks,
    crack_cluster,
    crack_source,
    crack_target,
    pulse_spectrum,
):
    panels, directions = incident.shape[2:]
    nblocks, span = near_blocks.shape[:2]
    width = near_blocks.shape[4]
    edges = crack_blocks.shape[0]
    front = 4
    near = near_blocks.reshape(nblocks, span, 2 * width, width)
    crack = crack_blocks.reshape(edges, 2 * width, width)
    incident, initial = incident[0], initial[0]
    lows = on_vmem(
        prepare_kernel,
        low_shapes(nblocks, width, 2 * directions, front),
        (),
        (initial,),
        "prepare",
    )

    place = lax.axis_index("frq") ^ jnp.arange(4, dtype=jnp.int32)
    real = jax.ShapeDtypeStruct((panels, directions), jnp.float32)
    both = jax.ShapeDtypeStruct((panels, 2 * directions), jnp.float32)

    tables = table_call(
        lax.axis_index("clu").reshape(1),
        near_pattern.reshape(-1),
        crack_cluster[:, 0],
        crack_source,
        crack_target,
        nblocks,
        span,
        front,
    )

    found, (from_start, *tables), base = exchange(
        lows,
        (initial, *tables),
        lambda early: [on_vmem(base_kernel, both, (), (incident, early[0]), "base")],
    )
    base = base[0]
    tables = (*tables, crack_target)
    send, keep = on_vmem(
        terms_kernel, (real, real), (place, pulse_spectrum), (from_start,), "terms"
    )
    here, away = on_vmem(
        mix_kernel, (real, real), (place,), (keep, swap(send, "frq", 1)), "mix"
    )
    away = swap(away, "frq", 2)

    def operate(step, found, extras):
        accs = main_call(step, tables, near, crack, found)
        common = (front, tables, near, crack, found)
        if step == 3:
            return rest_call(3, 0, *common, accs[0], extras)
        upper, low_a, head, sums = rest_call(step, 0, *common, accs[0], extras)
        vector, low_b, sums = rest_call(step, 1, *common, accs[1], extras, (upper, sums))
        return vector, low_a, low_b, head, sums

    first, *lows, sums_one = operate(1, found, (base,))
    found, (first_sent, away), _ = exchange(lows, (first, away))
    first_across, first_one = swap(first_sent, "frq", 2), swap(first, "frq", 1)

    second, *lows, sums_two = operate(2, found, (first,))
    found, (second_sent, first_across), _ = exchange(lows, (second, first_across))
    second_across, first_three = swap(second_sent, "frq", 2), swap(first_across, "frq", 1)
    (sums_three,) = operate(3, found, (first, second))
    second_one = swap(second, "frq", 1)
    sums = jnp.concatenate([sums_one, sums_two, sums_three], axis=0)
    sums, (second_across, second_one, first_three) = sum_over_clusters(
        sums, second_across, second_one, first_three
    )
    second_three = swap(second_across, "frq", 1)
    firsts = [first, first_one, first_across, first_three]
    seconds = [second, second_one, second_across, second_three]

    row = jax.ShapeDtypeStruct((8, directions), jnp.float32)
    coefs, sent = on_vmem(
        functools.partial(small_kernel, len(sums)), (row, row), (pulse_spectrum,), sums, "small"
    )
    every = [sent, *(swap(sent, "frq", d) for d in (1, 2, 3))]
    scattered = on_vmem(
        scattered_kernel,
        jax.ShapeDtypeStruct(initial.shape, jnp.float32),
        (),
        (coefs, initial, first, second),
        "scattered",
    )
    trace = on_vmem(
        functools.partial(trace_kernel, len(firsts)),
        real,
        (place,),
        (here, away, *every, *firsts, *seconds),
        "trace",
    )
    return (scattered[None], trace[None])


def solution(mesh):
    in_specs = (
        P("frq", None, "clu", None),
        P("frq", None, "clu", None),
        P("clu", None, "frq", None, None, None),
        P("clu", None),
        P("clu", "frq", None, None, None),
        P("clu", None),
        P("clu"),
        P("clu"),
        P("frq", None),
    )
    out_specs = (P("frq", None, "clu", None), P("frq", "clu", None))
    return jax.shard_map(local, mesh=mesh, in_specs=in_specs, out_specs=out_specs, check_vma=False)
```

```python
import functools

import jax
import jax.numpy as jnp
from jax import lax
from jax.experimental import pallas as pl
from jax.experimental.pallas import tpu as pltpu
from jax.sharding import PartitionSpec as P

EPS = 1e-06
MIB = 1024 * 1024
PLAIN_VMEM = 10 * MIB


def turn(rows):
    half = rows.shape[1] // 2
    return jnp.concatenate([-rows[:, half:], rows[:, :half]], axis=1)


def col_sum(rows):
    return jnp.sum(rows.reshape(rows.shape[0] // 8, 8, rows.shape[1]), axis=0)


def table_kernel(sizes, place, pattern, cluster, source, target, *outs):
    nblocks, span, edges, front, count, tuned_here = sizes
    near_a, crack_a, near_rows, near_mats, near_srcs, edge_rows, edge_mats, edge_srcs, numbers = outs
    me = place[0]
    odd = lax.rem(me, 2)
    cut = nblocks // 2
    limits = (2 * nblocks + cut, 6 * front) if tuned_here else (3 * nblocks, count * front)
    zeros = (nblocks - cut, 2 * front)

    def fill(i, carry):
        for rows, mats, srcs, zero in (
            (near_rows, near_mats, near_srcs, zeros[0]),
            (edge_rows, edge_mats, edge_srcs, zeros[1]),
        ):

            @pl.when(i < rows.shape[0])
            def _():
                rows[i] = 0
                mats[i] = 0
                srcs[i] = zero

        return carry

    lax.fori_loop(0, max(near_rows.shape[0], edge_rows.shape[0]), fill, 0)

    def note(lists, half, row, mat, src, late, found):
        rows, mats, srcs = lists
        spot = half * (rows.shape[0] // 2) + jnp.where(half == 0, found[0], found[1])

        @pl.when(late)
        def _():
            rows[spot] = row - half * cut
            mats[spot] = mat
            srcs[spot] = src

        step = jnp.where(late, 1, 0)
        return (
            found[0] + jnp.where(half == 0, step, 0),
            found[1] + jnp.where(half == 1, step, 0),
        )

    def near_one(i, found):
        value = pattern[i]
        side, block = value // nblocks, lax.rem(value, nblocks)
        beside = jnp.where(side == 2, 1 - odd, odd) if tuned_here else jnp.where(side == 2, 1, 0)
        spot = jnp.where(side == 1, 0, jnp.where(beside == 1, 1, 2)) * nblocks + block
        late = spot >= limits[0]
        near_a[i] = jnp.where(late, limits[0], spot)
        row = i // span
        half = jnp.where(row >= cut, 1, 0)
        lists = (near_rows, near_mats, near_srcs)
        return note(lists, half, row, i, spot - limits[0], late, found)

    none = (jnp.int32(0), jnp.int32(0))
    near_found = lax.fori_loop(0, nblocks * span, near_one, none)

    def edge_one(e, found):
        if tuned_here:
            offset = lax.rem(cluster[e] - me + count, count)
            offset = jnp.where(odd == 1, lax.rem(count - offset, count), offset)
            slot = jnp.int32(0)
            for position, distance in enumerate((0, 1, 7, 6, 2, 4, 3, 5)):
                slot = jnp.where(offset == distance, position, slot)
        else:
            slot = cluster[e]
        spot = slot * front + source[e]
        late = spot >= limits[1]
        crack_a[e] = jnp.where(late, limits[1], spot)
        row = target[e]
        half = jnp.where(row >= cut, 1, 0)
        lists = (edge_rows, edge_mats, edge_srcs)
        return note(lists, half, row, e, spot - limits[1], late, found)

    edge_found = lax.fori_loop(0, edges, edge_one, none)
    for half in range(2):
        numbers[half] = near_found[half]
        numbers[2 + half] = edge_found[half]


def table_call(me, pattern, cluster, source, target, nblocks, span, front):
    edges = cluster.shape[0]
    cut = nblocks // 2
    near_list = 2 * max(cut, nblocks - cut) * span
    lengths = (nblocks * span, edges, *(near_list,) * 3, *(2 * edges,) * 3, 4)
    smem = pl.BlockSpec(memory_space=pltpu.SMEM)
    sizes = (nblocks, span, edges, front, lax.axis_size("clu"), tuned())
    return pl.pallas_call(
        functools.partial(table_kernel, sizes),
        out_shape=tuple(jax.ShapeDtypeStruct((length,), jnp.int32) for length in lengths),
        in_specs=[smem] * 5,
        out_specs=tuple(smem for _ in lengths),
        name="tables",
    )(me, pattern, cluster, source, target)


def block_copies(parts, moves, target, sems):
    return [
        pltpu.make_async_copy(
            parts[part].at[pl.ds(begin, count)], target.at[pl.ds(offset, count)], sems.at[place]
        )
        for place, (part, begin, count, offset) in enumerate(moves)
    ]


def total_of(moves):
    return sum(move[2] for move in moves)


GROUP = 4
REST_COST = 3


def main_kernel(sizes, moves, *refs):
    nblocks, span, edges, front_moves, source_moves, nparts = (*sizes, *moves)
    near_idx, crack_idx, crack_tgt, near_v, crack_v = refs[:5]
    parts = refs[5 : 5 + nparts]
    *accs, front_v, source_v, front_sem, source_sem = refs[5 + nparts :]
    cut = nblocks // 2
    if len(accs) == 1:
        accs = [accs[0].at[pl.ds(0, cut)], accs[0].at[pl.ds(cut, nblocks - cut)]]
    acc_a, acc_b = accs
    front_copies = block_copies(parts, front_moves, front_v, front_sem)
    source_copies = block_copies(parts, source_moves, source_v, source_sem)
    for copy in source_copies + front_copies:
        copy.start()
    for store in (front_v, source_v):
        store[store.shape[0] - 1] = jnp.zeros(store.shape[1:], store.dtype)
    for copy in source_copies:
        copy.wait()

    def row(acc, start, g, carry):
        left = jnp.concatenate([near_v[g, s] for s in range(span)], axis=1)
        right = jnp.concatenate([source_v[near_idx[g * span + s]] for s in range(span)], axis=0)
        acc[g - start] = jnp.dot(left, right, preferred_element_type=jnp.float32)
        return carry

    lax.fori_loop(0, cut, functools.partial(row, acc_a, 0), 0, unroll=2)
    lax.fori_loop(cut, nblocks, functools.partial(row, acc_b, cut), 0, unroll=2)
    for copy in front_copies:
        copy.wait()

    def crack_edges(i, carry):
        products = [
            jnp.dot(
                crack_v[i * GROUP + k],
                front_v[crack_idx[i * GROUP + k]],
                preferred_element_type=jnp.float32,
            )
            for k in range(GROUP)
        ]
        for k in range(GROUP):
            target = crack_tgt[i * GROUP + k]

            @pl.when(target < cut)
            def _():
                acc_a[target] += products[k]

            @pl.when(target >= cut)
            def _():
                acc_b[target - cut] += products[k]

        return carry

    lax.fori_loop(0, edges // GROUP, crack_edges, 0)


def main_call(step, tables, near, crack, found):
    parts, front_moves, source_moves = found[:3]
    nblocks, span = near.shape[:2]
    edges, width = crack.shape[0], near.shape[3]
    lanes = parts[0].shape[2]
    cut = nblocks // 2
    smem = pl.BlockSpec(memory_space=pltpu.SMEM)
    anywhere = pl.BlockSpec(memory_space=pl.ANY)
    whole = pl.BlockSpec(memory_space=pltpu.VMEM)
    blocks = total_of(front_moves) + total_of(source_moves) + 2
    counts = (nblocks,) if step == 3 else (cut, nblocks - cut)
    return pl.pallas_call(
        functools.partial(
            main_kernel, (nblocks, span, edges), (front_moves, source_moves, len(parts))
        ),
        out_shape=tuple(
            jax.ShapeDtypeStruct((rows, 2 * width, lanes), jnp.float32)
            for rows in counts
        ),
        in_specs=[smem] * 3 + [whole] * 2 + [anywhere] * len(parts),
        out_specs=tuple(whole for _ in counts),
        scratch_shapes=[
            pltpu.VMEM((total_of(front_moves) + 1, width, lanes), jnp.bfloat16),
            pltpu.VMEM((total_of(source_moves) + 1, width, lanes), jnp.bfloat16),
            pltpu.SemaphoreType.DMA((len(front_moves),)),
            pltpu.SemaphoreType.DMA((len(source_moves),)),
        ],
        compiler_params=pltpu.CompilerParams(
            vmem_limit_bytes=2 * blocks * width * lanes + 2 * MIB
        ),
        cost_estimate=pl.CostEstimate(
            flops=4 * width * width * lanes * (nblocks * span + edges),
            bytes_accessed=near.size * 2 + crack.size * 2,
            transcendentals=0,
        ),
        name=f"operator_{step}",
    )(tables[0], tables[1], tables[-1], near, crack, *parts)


def rest_kernel(step, part, sizes, moves, *refs):
    nblocks, span, width, front, start, nrows = sizes
    near_moves, edge_moves, nparts = moves
    lists, rest = refs[:7], refs[7:]
    near_v, crack_v, acc = rest[:3]
    parts, rest = rest[3 : 3 + nparts], rest[3 + nparts :]
    nextra = 2 if step == 3 else 1
    extras, rest = rest[:nextra], rest[nextra:]
    before = ()
    if part == 1:
        nbefore = 2
        before, rest = rest[:nbefore], rest[nbefore:]
    nouts = 1 if step == 3 else (4, 3)[part]
    outs, rest = rest[:nouts], rest[nouts:]
    numbers = lists[6]
    lanes = acc.shape[2]
    late = nparts > 0
    if late:
        near_src, edge_src, extra, near_sem, edge_sem = rest
        copies = block_copies(parts, near_moves, near_src, near_sem)
        copies += block_copies(parts, edge_moves, edge_src, edge_sem)
        for copy in copies:
            copy.start()
        extra[...] = jnp.zeros(extra.shape, jnp.float32)
        for store in (near_src, edge_src):
            store[store.shape[0] - 1] = jnp.zeros(store.shape[1:], store.dtype)
        for copy in copies:
            copy.wait()

        def add(half, rows, mats, srcs, number, matrix, source):
            offset = half * (rows.shape[0] // 2)
            shift_by = half * (nblocks // 2) if step == 3 else 0

            def some(i, carry):
                spots = [offset + i * GROUP + k for k in range(GROUP)]
                products = [
                    jnp.dot(
                        matrix(mats[spot]), source[srcs[spot]], preferred_element_type=jnp.float32
                    )
                    for spot in spots
                ]
                for spot, product in zip(spots, products):
                    extra[rows[spot] + shift_by] += product
                return carry

            lax.fori_loop(0, (number + GROUP - 1) // GROUP, some, 0)

        for half in (0, 1) if step == 3 else (part,):
            add(
                half,
                *lists[:3],
                numbers[half],
                lambda i: near_v[i // span, lax.rem(i, span)],
                near_src,
            )
            add(half, *lists[3:6], numbers[2 + half], lambda i: crack_v[i], edge_src)

    nsums = (1, 3, 5)[step - 1]
    zero = jnp.zeros((8, lanes), jnp.float32)

    def row(g, sums):
        total = acc[g] + extra[g] if late else acc[g]
        new = total[:width] + turn(total[width:])
        rows = pl.ds(pl.multiple_of((start + g) * width, width), width)
        if step == 1:
            new = extras[0][rows, :] - new
            terms = (new * new,)
        elif step == 2:
            first = extras[0][rows, :]
            terms = (first * new, first * turn(new), new * new)
        else:
            first, second, turned = extras[0][rows, :], extras[1][rows, :], turn(new)
            terms = (first * new, first * turned, second * new, second * turned, new * new)
        if step != 3:
            outs[0][rows, :] = new
            rounded = new.astype(jnp.bfloat16)
            outs[1][g] = rounded
            if part == 0:

                @pl.when(g < front)
                def _():
                    outs[2][g] = rounded

        return tuple(total + col_sum(term) for total, term in zip(sums, terms))

    sums = lax.fori_loop(0, nrows, row, (zero,) * nsums, unroll=2)
    sums = [jnp.sum(total, axis=0, keepdims=True) for total in sums]
    sums.append(jnp.zeros((8 - nsums, lanes), jnp.float32))
    sums = jnp.concatenate(sums, axis=0)
    if part == 1:
        sums = sums + before[-1][...]
        if step != 3:
            outs[0][: before[0].shape[0], :] = before[0][...]
    outs[-1][...] = sums


def rest_call(step, part, front, tables, near, crack, found, acc, extras, before=()):
    _, _, _, parts, near_moves, edge_moves = found
    nblocks, span = near.shape[:2]
    width, lanes = near.shape[3], acc.shape[2]
    nrows = acc.shape[0]
    start = part * (nblocks // 2)
    out_shape = [jax.ShapeDtypeStruct((8, lanes), jnp.float32)]
    if step != 3:
        ends = start + nrows
        vector = jax.ShapeDtypeStruct((ends * width, lanes), jnp.float32)
        low_a, low_b, head = low_shapes(nblocks, width, lanes, front)
        out_shape = [vector, *((low_a, head), (low_b,))[part], *out_shape]
    smem = pl.BlockSpec(memory_space=pltpu.SMEM)
    anywhere = pl.BlockSpec(memory_space=pl.ANY)
    whole = pl.BlockSpec(memory_space=pltpu.VMEM)
    scratch, held = [], 0
    if parts:
        shapes = (total_of(near_moves) + 1, total_of(edge_moves) + 1)
        scratch = [pltpu.VMEM((n, width, lanes), jnp.bfloat16) for n in shapes]
        scratch += [
            pltpu.VMEM(acc.shape, jnp.float32),
            pltpu.SemaphoreType.DMA((len(near_moves),)),
            pltpu.SemaphoreType.DMA((len(edge_moves),)),
        ]
        held = 2 * sum(shapes) * width * lanes + 4 * acc.size
    return pl.pallas_call(
        functools.partial(
            rest_kernel,
            step,
            part,
            (nblocks, span, width, front, start, nrows),
            (near_moves, edge_moves, len(parts)),
        ),
        out_shape=tuple(out_shape),
        in_specs=[smem] * 7
        + [whole] * 3
        + [anywhere] * len(parts)
        + [whole] * (len(extras) + len(before)),
        out_specs=tuple(whole for _ in out_shape),
        scratch_shapes=scratch,
        compiler_params=pltpu.CompilerParams(vmem_limit_bytes=held + 2 * MIB),
        cost_estimate=pl.CostEstimate(
            flops=4 * width * width * lanes * nrows * span // 4,
            bytes_accessed=REST_COST * acc.size * 4,
            transcendentals=0,
        ),
        name=f"rest_{step}_{part}",
    )(*tables[2:9], near, crack, acc, *parts, *extras, *before)


def low_shapes(nblocks, width, lanes, front):
    cut = nblocks // 2
    return tuple(
        jax.ShapeDtypeStruct((count, width, lanes), jnp.bfloat16)
        for count in (cut, nblocks - cut, front)
    )


def prepare_kernel(initial, low_a, low_b, head):
    width = low_a.shape[1]

    def one(target, start, g, carry):
        rows = pl.ds(pl.multiple_of((start + g) * width, width), width)
        rounded = jnp.concatenate([initial[0, rows], initial[1, rows]], axis=1)
        target[g] = rounded.astype(jnp.bfloat16)
        return carry

    cut = low_a.shape[0]
    lax.fori_loop(0, cut, functools.partial(one, low_a, 0), 0)
    lax.fori_loop(0, low_b.shape[0], functools.partial(one, low_b, cut), 0)
    lax.fori_loop(0, head.shape[0], functools.partial(one, head, 0), 0)


def swap(value, axis, distance):
    count = lax.axis_size(axis)
    return lax.ppermute(value, axis, [(i, i ^ distance) for i in range(count)])


def shift(value, axis, distance):
    count = lax.axis_size(axis)
    return lax.ppermute(value, axis, [(i, (i + distance) % count) for i in range(count)])


def ring(value, distance):
    count = lax.axis_size("clu")
    pairs = [(i, (i + (-distance if i % 2 else distance)) % count) for i in range(count)]
    return lax.ppermute(value, "clu", pairs)


def tuned():
    return lax.axis_size("clu") == 8


def tie(*values):
    return lax.optimization_barrier(values)


def exchange(lows, early_ties=(), late_ties=(), first_ties=()):
    low_a, low_b, head = lows
    cut, rest, front = (low.shape[0] for low in lows)
    nblocks = cut + rest
    if not tuned():
        count = lax.axis_size("clu")
        if callable(late_ties):
            late_ties = late_ties(early_ties)
        low = jnp.concatenate([low_a, low_b], axis=0)
        every = lax.all_gather(head, "clu", axis=0, tiled=True)
        parts = [low, shift(low, "clu", -1), shift(low, "clu", 1), every]
        source_moves = tuple((k, 0, nblocks, k * nblocks) for k in range(3))
        found = (parts, ((3, 0, count * front, 0),), source_moves, [], (), ())
        return found, early_ties, late_ties, first_ties
    beside_a = swap(low_a, "clu", 1)
    same, *first_ties = tie(ring(head, 2), *first_ties)
    other = ring(head, -2)
    tail, beside_a, same, other = tie(low_b, beside_a, same, other)
    onward, *early_ties = tie(jnp.concatenate([beside_a, same], axis=0), *early_ties)
    beyond_a = ring(onward, 2)
    beside_b = swap(tail, "clu", 1)
    if callable(late_ties):
        late_ties = late_ties(early_ties)
    beside_b, *late_ties = tie(beside_b, *late_ties)
    beyond_b = ring(beside_b, 2)
    pairs = swap(jnp.concatenate([same, beyond_a[cut:]], axis=0), "clu", 1)
    parts = [low_a, low_b, beside_a, beside_b, beyond_a, same, other]
    front_moves = tuple(
        (part, begin, front, place * front)
        for place, (part, begin) in enumerate(
            [(0, 0), (2, 0), (4, 0), (5, 0), (6, 0), (4, cut)]
        )
    )
    source_moves = (
        (0, 0, cut, 0),
        (1, 0, rest, cut),
        (2, 0, cut, nblocks),
        (3, 0, rest, nblocks + cut),
        (4, 0, cut, 2 * nblocks),
    )
    last = [beyond_b, pairs]
    found = (parts, front_moves, source_moves, last, ((0, 0, rest, 0),), ((1, 0, 2 * front, 0),))
    return found, early_ties, late_ties, first_ties


def sum_over_clusters(value, *tied):
    if not tuned():
        return [lax.psum(value, "clu")], tied
    value, *tied = tie(value + swap(value, "clu", 1), *tied)
    return [value, *(shift(value, "clu", d) for d in (2, 4, 6))], tied


def cmul(a, b):
    return (a[0] * b[0] - a[1] * b[1], a[0] * b[1] + a[1] * b[0])


def cjmul(a, b):
    return (a[0] * b[0] + a[1] * b[1], a[0] * b[1] - a[1] * b[0])


def cadd(*terms):
    return (sum(t[0] for t in terms), sum(t[1] for t in terms))


def scale(factor, a):
    return (factor * a[0], factor * a[1])


def norm2(a):
    return a[0] * a[0] + a[1] * a[1]


def least_squares(beta_norm, first_h, sub_one, second_h, third_h, sub_two):
    r_one = jnp.sqrt(first_h[0] ** 2 + first_h[1] ** 2 + sub_one**2)
    q_real = first_h[0] / r_one
    q_imag = first_h[1] / r_one
    q_low = sub_one / r_one
    mix_real = q_real * second_h[0] + q_imag * second_h[1] + q_low * third_h[0]
    mix_imag = q_real * second_h[1] - q_imag * second_h[0] + q_low * third_h[1]
    top_real = second_h[0] - (mix_real * q_real - mix_imag * q_imag)
    top_imag = second_h[1] - (mix_real * q_imag + mix_imag * q_real)
    mid_real = third_h[0] - mix_real * q_low
    mid_imag = third_h[1] - mix_imag * q_low
    r_two_sq = top_real**2 + top_imag**2 + mid_real**2 + mid_imag**2 + sub_two**2
    later_real = beta_norm * top_real / r_two_sq
    later_imag = -beta_norm * top_imag / r_two_sq
    early_real = (beta_norm * q_real - (mix_real * later_real - mix_imag * later_imag)) / r_one
    early_imag = (-beta_norm * q_imag - (mix_real * later_imag + mix_imag * later_real)) / r_one
    return ((early_real, early_imag), (later_real, later_imag))


def combine(g00, g01, g11, g02, g12, g22):
    beta2 = g00 + EPS
    beta = jnp.sqrt(beta2)
    h11 = ((0.5 * g00 + g01[0]) / beta2, g01[1] / beta2)
    s = ((0.5 * EPS - g01[0]) / beta2, -g01[1] / beta2)
    s01 = cjmul(s, g01)
    w2w2 = g11 + 2.0 * s01[0] + norm2(s) * g00
    h21 = jnp.sqrt(jnp.maximum(w2w2 / beta2, 0.0) + EPS)
    k = 1.0 / (beta * h21)
    d = (s[0] + 0.5, s[1])
    e = scale(0.5, s)
    r0u = cadd(g02, cmul(d, g01), scale(g00, e))
    z1u = cadd(g12, scale(g11, d), cmul(e, (g01[0], -g01[1])))
    h12 = scale(k / beta, r0u)
    h22 = scale(k * k, cadd(z1u, cjmul(s, r0u)))
    uu = (
        g22
        + norm2(d) * g11
        + norm2(e) * g00
        + 2.0 * cjmul(d, g12)[0]
        + 2.0 * cjmul(e, g02)[0]
        + 2.0 * cjmul(e, cmul(d, g01))[0]
    )
    n11 = g00 / beta2
    n22 = k * k * w2w2
    n12 = scale(k / beta, cadd(g01, scale(g00, s)))
    rest = (
        k * k * uu
        + norm2(h12) * (n11 - 2.0)
        + norm2(h22) * (n22 - 2.0)
        + 2.0 * cmul(cjmul(h12, h22), n12)[0]
    )
    h32 = jnp.sqrt(jnp.maximum(rest, 0.0) + EPS)
    early, later = least_squares(beta, h11, h21, h12, h22, h32)
    b = scale(k, later)
    a = cadd(scale(1.0 / beta, early), cmul(b, s))
    return a, b


def small_kernel(nsums, pulse, *refs):
    coefs, sent = refs[nsums:]
    sums = refs[0][...]
    for other in refs[1:nsums]:
        sums = sums + other[...]
    half = sums.shape[1] // 2
    sums = sums[:, :half] + sums[:, half:]

    def row(i):
        return sums[i : i + 1]

    a, b = combine(
        row(0),
        (row(8), -row(9)),
        row(10),
        (row(16), -row(17)),
        (row(18), -row(19)),
        row(20),
    )
    zero = jnp.zeros((4, half), jnp.float32)
    coefs[...] = jnp.concatenate([*a, *b, zero], axis=0)
    factor = (pulse[0, 0], pulse[0, 1])
    sent[...] = jnp.concatenate([*cmul(factor, a), *cmul(factor, b), zero], axis=0)


def scattered_kernel(coefs, initial, first, second, scattered):
    half = initial.shape[2]
    a = (coefs[0:1], coefs[1:2])
    b = (coefs[2:3], coefs[3:4])
    width = 256

    def one(g, carry):
        rows = pl.ds(pl.multiple_of(g * width, width), width)
        x, y = first[rows, :], second[rows, :]
        xr, xi, yr, yi = x[:, :half], x[:, half:], y[:, :half], y[:, half:]
        scattered[0, rows, :] = initial[0, rows] + a[0] * xr - a[1] * xi + b[0] * yr - b[1] * yi
        scattered[1, rows, :] = initial[1, rows] + a[0] * xi + a[1] * xr + b[0] * yi + b[1] * yr
        return carry

    lax.fori_loop(0, first.shape[0] // width, one, 0)


def power_of_i(exponent):
    exponent = lax.rem(exponent, 4)
    real = jnp.where(exponent == 0, 1.0, jnp.where(exponent == 2, -1.0, 0.0))
    imag = jnp.where(exponent == 1, 1.0, jnp.where(exponent == 3, -1.0, 0.0))
    return real, imag


def terms_kernel(place, pulse, initial, send, keep):
    width = 256
    f, core = place[0], lax.rem(place[0], 2)
    factor = (pulse[0, 0], pulse[0, 1])
    sent = cmul(factor, power_of_i((1 - core) * f))
    kept = cmul(factor, power_of_i(core * f))

    def one(g, carry):
        rows = pl.ds(pl.multiple_of(g * width, width), width)
        real, imag = initial[0, rows], initial[1, rows]
        send[rows, :] = sent[0] * real - sent[1] * imag
        keep[rows, :] = kept[0] * real - kept[1] * imag
        return carry

    lax.fori_loop(0, initial.shape[1] // width, one, 0)


def base_kernel(incident, initial, base):
    width = 256

    def one(g, carry):
        rows = pl.ds(pl.multiple_of(g * width, width), width)
        base[rows, :] = jnp.concatenate(
            [incident[half, rows] - 0.5 * initial[half, rows] for half in range(2)], axis=1
        )
        return carry

    lax.fori_loop(0, base.shape[0] // width, one, 0)


def mix_kernel(place, keep, taken, here, away):
    side, sign = place[0] // 2, 1.0 - 2.0 * lax.rem(place[0], 2).astype(jnp.float32)
    near_sign, far_sign = jnp.where(side == 1, sign, 1.0), jnp.where(side == 0, sign, 1.0)
    near_other, far_other = jnp.where(side == 1, -sign, 1.0), jnp.where(side == 0, -sign, 1.0)
    here[...] = near_sign * keep[...] + near_other * taken[...]
    away[...] = far_sign * keep[...] + far_other * taken[...]


def trace_kernel(count, place, here, away, *refs):
    coefs, firsts, seconds = refs[:count], refs[count : 2 * count], refs[2 * count : 3 * count]
    trace = refs[3 * count]
    half = trace.shape[1]
    width = 256
    weights = []
    for k in range(count):
        turned = power_of_i(place[0] * place[k])
        values = coefs[k][...]
        weights.append(
            (
                cmul(turned, (values[0:1], values[1:2])),
                cmul(turned, (values[2:3], values[3:4])),
            )
        )

    def one(g, carry):
        rows = pl.ds(pl.multiple_of(g * width, width), width)
        total = here[rows, :] + away[rows, :]
        for k in range(count):
            a, b = weights[k]
            x, y = firsts[k][rows, :], seconds[k][rows, :]
            total = total + (a[0] * x[:, :half] - a[1] * x[:, half:])
            total = total + (b[0] * y[:, :half] - b[1] * y[:, half:])
        trace[rows, :] = total
        return carry

    lax.fori_loop(0, trace.shape[0] // width, one, 0)


def on_vmem(body, out_shape, smem_args, args, name):
    outs = jax.tree.leaves(out_shape)
    moved = sum(a.size * a.dtype.itemsize for a in (*args, *outs))
    whole = pl.BlockSpec(memory_space=pltpu.VMEM)
    smem = pl.BlockSpec(memory_space=pltpu.SMEM)
    return pl.pallas_call(
        body,
        out_shape=out_shape,
        in_specs=[smem] * len(smem_args) + [whole] * len(args),
        out_specs=jax.tree.map(lambda _: whole, out_shape),
        compiler_params=pltpu.CompilerParams(vmem_limit_bytes=PLAIN_VMEM),
        cost_estimate=pl.CostEstimate(flops=0, bytes_accessed=moved, transcendentals=0),
        name=name,
    )(*smem_args, *args)


def local(
    incident,
    initial,
    near_blocks,
    near_pattern,
    crack_blocks,
    crack_cluster,
    crack_source,
    crack_target,
    pulse_spectrum,
):
    panels, directions = incident.shape[2:]
    nblocks, span = near_blocks.shape[:2]
    width = near_blocks.shape[4]
    edges = crack_blocks.shape[0]
    front = 4
    near = near_blocks.reshape(nblocks, span, 2 * width, width)
    crack = crack_blocks.reshape(edges, 2 * width, width)
    incident, initial = incident[0], initial[0]
    lows = on_vmem(
        prepare_kernel,
        low_shapes(nblocks, width, 2 * directions, front),
        (),
        (initial,),
        "prepare",
    )

    place = lax.axis_index("frq") ^ jnp.arange(4, dtype=jnp.int32)
    real = jax.ShapeDtypeStruct((panels, directions), jnp.float32)
    both = jax.ShapeDtypeStruct((panels, 2 * directions), jnp.float32)

    tables = table_call(
        lax.axis_index("clu").reshape(1),
        near_pattern.reshape(-1),
        crack_cluster[:, 0],
        crack_source,
        crack_target,
        nblocks,
        span,
        front,
    )

    found, (from_start, *tables), base, _ = exchange(
        lows,
        (initial, *tables),
        lambda early: [on_vmem(base_kernel, both, (), (incident, early[0]), "base")],
    )
    base = base[0]
    tables = (*tables, crack_target)
    send, keep = on_vmem(
        terms_kernel, (real, real), (place, pulse_spectrum), (from_start,), "terms"
    )
    here, away = on_vmem(
        mix_kernel, (real, real), (place,), (keep, swap(send, "frq", 1)), "mix"
    )
    away = swap(away, "frq", 2)

    def operate(step, found, extras):
        accs = main_call(step, tables, near, crack, found)
        common = (front, tables, near, crack, found)
        if step == 3:
            return rest_call(3, 0, *common, accs[0], extras)
        upper, low_a, head, sums = rest_call(step, 0, *common, accs[0], extras)
        vector, low_b, sums = rest_call(step, 1, *common, accs[1], extras, (upper, sums))
        return vector, low_a, low_b, head, sums

    first, *lows, sums_one = operate(1, found, (base,))
    found, (away,), _, (first_sent,) = exchange(lows, (away,), (), (first,))
    first_across, first_one = swap(first_sent, "frq", 2), swap(first, "frq", 1)

    second, *lows, sums_two = operate(2, found, (first,))
    second_sent, first_across = tie(second, first_across)
    found, _, _, _ = exchange(lows)
    second_across, first_three = swap(second_sent, "frq", 2), swap(first_across, "frq", 1)
    (sums_three,) = operate(3, found, (first, second))
    second_one = swap(second, "frq", 1)
    sums = jnp.concatenate([sums_one, sums_two, sums_three], axis=0)
    sums, (second_across, second_one, first_three) = sum_over_clusters(
        sums, second_across, second_one, first_three
    )
    second_three = swap(second_across, "frq", 1)
    firsts = [first, first_one, first_across, first_three]
    seconds = [second, second_one, second_across, second_three]

    row = jax.ShapeDtypeStruct((8, directions), jnp.float32)
    coefs, sent = on_vmem(
        functools.partial(small_kernel, len(sums)), (row, row), (pulse_spectrum,), sums, "small"
    )
    every = [sent, *(swap(sent, "frq", d) for d in (1, 2, 3))]
    scattered = on_vmem(
        scattered_kernel,
        jax.ShapeDtypeStruct(initial.shape, jnp.float32),
        (),
        (coefs, initial, first, second),
        "scattered",
    )
    trace = on_vmem(
        functools.partial(trace_kernel, len(firsts)),
        real,
        (place,),
        (here, away, *every, *firsts, *seconds),
        "trace",
    )
    return (scattered[None], trace[None])


def solution(mesh):
    in_specs = (
        P("frq", None, "clu", None),
        P("frq", None, "clu", None),
        P("clu", None, "frq", None, None, None),
        P("clu", None),
        P("clu", "frq", None, None, None),
        P("clu", None),
        P("clu"),
        P("clu"),
        P("frq", None),
    )
    out_specs = (P("frq", None, "clu", None), P("frq", "clu", None))
    return jax.shard_map(local, mesh=mesh, in_specs=in_specs, out_specs=out_specs, check_vma=False)
```

```python
import functools

import jax
import jax.numpy as jnp
from jax import lax
from jax.experimental import pallas as pl
from jax.experimental.pallas import tpu as pltpu
from jax.sharding import PartitionSpec as P

EPS = 1e-06
MIB = 1024 * 1024
PLAIN_VMEM = 10 * MIB


def turn(rows):
    half = rows.shape[1] // 2
    return jnp.concatenate([-rows[:, half:], rows[:, :half]], axis=1)


def col_sum(rows):
    return jnp.sum(rows.reshape(rows.shape[0] // 8, 8, rows.shape[1]), axis=0)


def table_kernel(sizes, place, pattern, cluster, source, target, *outs):
    nblocks, span, edges, front, count, tuned_here = sizes
    near_a, crack_a, near_rows, near_mats, near_srcs, edge_rows, edge_mats, edge_srcs, numbers = outs
    me = place[0]
    odd = lax.rem(me, 2)
    cut = nblocks // 2
    limits = (2 * nblocks + cut, 6 * front) if tuned_here else (3 * nblocks, count * front)

    def fill(i, carry):
        for rows, mats, srcs in (
            (near_rows, near_mats, near_srcs),
            (edge_rows, edge_mats, edge_srcs),
        ):

            @pl.when(i < rows.shape[0])
            def _():
                rows[i] = 0
                mats[i] = 0
                srcs[i] = 0

        return carry

    lax.fori_loop(0, max(near_rows.shape[0], edge_rows.shape[0]), fill, 0)

    def note(lists, half, row, mat, src, late, found):
        rows, mats, srcs = lists
        spot = half * (rows.shape[0] // 2) + jnp.where(half == 0, found[0], found[1])

        @pl.when(late)
        def _():
            rows[spot] = row - half * cut
            mats[spot] = mat
            srcs[spot] = src

        step = jnp.where(late, 1, 0)
        return (
            found[0] + jnp.where(half == 0, step, 0),
            found[1] + jnp.where(half == 1, step, 0),
        )

    def near_one(i, found):
        value = pattern[i]
        side, block = value // nblocks, lax.rem(value, nblocks)
        beside = jnp.where(side == 2, 1 - odd, odd) if tuned_here else jnp.where(side == 2, 1, 0)
        spot = jnp.where(side == 1, 0, jnp.where(beside == 1, 1, 2)) * nblocks + block
        late = spot >= limits[0]
        near_a[i] = jnp.where(late, limits[0], spot)
        row = i // span
        half = jnp.where(row >= cut, 1, 0)
        lists = (near_rows, near_mats, near_srcs)
        return note(lists, half, row, i, spot - limits[0], late, found)

    none = (jnp.int32(0), jnp.int32(0))
    near_found = lax.fori_loop(0, nblocks * span, near_one, none)

    def edge_one(e, found):
        if tuned_here:
            offset = lax.rem(cluster[e] - me + count, count)
            offset = jnp.where(odd == 1, lax.rem(count - offset, count), offset)
            slot = jnp.int32(0)
            for position, distance in enumerate((0, 1, 7, 6, 2, 4, 3, 5)):
                slot = jnp.where(offset == distance, position, slot)
        else:
            slot = cluster[e]
        spot = slot * front + source[e]
        late = spot >= limits[1]
        crack_a[e] = jnp.where(late, limits[1], spot)
        row = target[e]
        half = jnp.where(row >= cut, 1, 0)
        lists = (edge_rows, edge_mats, edge_srcs)
        return note(lists, half, row, e, spot - limits[1], late, found)

    edge_found = lax.fori_loop(0, edges, edge_one, none)
    for half in range(2):
        numbers[half] = near_found[half]
        numbers[2 + half] = edge_found[half]


def table_call(me, pattern, cluster, source, target, nblocks, span, front):
    edges = cluster.shape[0]
    cut = nblocks // 2
    near_list = 2 * max(cut, nblocks - cut) * span
    lengths = (nblocks * span, edges, *(near_list,) * 3, *(2 * edges,) * 3, 4)
    smem = pl.BlockSpec(memory_space=pltpu.SMEM)
    sizes = (nblocks, span, edges, front, lax.axis_size("clu"), tuned())
    return pl.pallas_call(
        functools.partial(table_kernel, sizes),
        out_shape=tuple(jax.ShapeDtypeStruct((length,), jnp.int32) for length in lengths),
        in_specs=[smem] * 5,
        out_specs=tuple(smem for _ in lengths),
        name="tables",
    )(me, pattern, cluster, source, target)


def block_copies(parts, moves, target, sems):
    return [
        pltpu.make_async_copy(
            parts[part].at[pl.ds(begin, count)], target.at[pl.ds(offset, count)], sems.at[place]
        )
        for place, (part, begin, count, offset) in enumerate(moves)
    ]


def total_of(moves):
    return sum(move[2] for move in moves)


GROUP = 4
REST_COST = 3


def main_kernel(sizes, moves, *refs):
    nblocks, span, edges, front_moves, source_moves, nparts = (*sizes, *moves)
    near_idx, crack_idx, crack_tgt, near_v, crack_v = refs[:5]
    parts = refs[5 : 5 + nparts]
    *accs, front_v, source_v, front_sem, source_sem = refs[5 + nparts :]
    cut = nblocks // 2
    if len(accs) == 1:
        accs = [accs[0].at[pl.ds(0, cut)], accs[0].at[pl.ds(cut, nblocks - cut)]]
    acc_a, acc_b = accs
    front_copies = block_copies(parts, front_moves, front_v, front_sem)
    source_copies = block_copies(parts, source_moves, source_v, source_sem)
    for copy in source_copies + front_copies:
        copy.start()
    for store in (front_v, source_v):
        store[store.shape[0] - 1] = jnp.zeros(store.shape[1:], store.dtype)
    for copy in source_copies:
        copy.wait()

    def row(acc, start, g, carry):
        left = jnp.concatenate([near_v[g, s] for s in range(span)], axis=1)
        right = jnp.concatenate([source_v[near_idx[g * span + s]] for s in range(span)], axis=0)
        acc[g - start] = jnp.dot(left, right, preferred_element_type=jnp.float32)
        return carry

    lax.fori_loop(0, cut, functools.partial(row, acc_a, 0), 0, unroll=4)
    lax.fori_loop(cut, nblocks, functools.partial(row, acc_b, cut), 0, unroll=4)
    for copy in front_copies:
        copy.wait()

    def crack_edges(i, carry):
        products = [
            jnp.dot(
                crack_v[i * GROUP + k],
                front_v[crack_idx[i * GROUP + k]],
                preferred_element_type=jnp.float32,
            )
            for k in range(GROUP)
        ]
        for k in range(GROUP):
            target = crack_tgt[i * GROUP + k]

            @pl.when(target < cut)
            def _():
                acc_a[target] += products[k]

            @pl.when(target >= cut)
            def _():
                acc_b[target - cut] += products[k]

        return carry

    lax.fori_loop(0, edges // GROUP, crack_edges, 0)


def main_call(step, tables, near, crack, found):
    parts, front_moves, source_moves = found[:3]
    nblocks, span = near.shape[:2]
    edges, width = crack.shape[0], near.shape[3]
    lanes = parts[0].shape[2]
    cut = nblocks // 2
    smem = pl.BlockSpec(memory_space=pltpu.SMEM)
    anywhere = pl.BlockSpec(memory_space=pl.ANY)
    whole = pl.BlockSpec(memory_space=pltpu.VMEM)
    blocks = total_of(front_moves) + total_of(source_moves) + 2
    counts = (nblocks,) if step == 3 else (cut, nblocks - cut)
    return pl.pallas_call(
        functools.partial(
            main_kernel, (nblocks, span, edges), (front_moves, source_moves, len(parts))
        ),
        out_shape=tuple(
            jax.ShapeDtypeStruct((rows, 2 * width, lanes), jnp.float32)
            for rows in counts
        ),
        in_specs=[smem] * 3 + [whole] * 2 + [anywhere] * len(parts),
        out_specs=tuple(whole for _ in counts),
        scratch_shapes=[
            pltpu.VMEM((total_of(front_moves) + 1, width, lanes), jnp.bfloat16),
            pltpu.VMEM((total_of(source_moves) + 1, width, lanes), jnp.bfloat16),
            pltpu.SemaphoreType.DMA((len(front_moves),)),
            pltpu.SemaphoreType.DMA((len(source_moves),)),
        ],
        compiler_params=pltpu.CompilerParams(
            vmem_limit_bytes=2 * blocks * width * lanes + 2 * MIB
        ),
        cost_estimate=pl.CostEstimate(
            flops=4 * width * width * lanes * (nblocks * span + edges),
            bytes_accessed=near.size * 2 + crack.size * 2,
            transcendentals=0,
        ),
        name=f"operator_{step}",
    )(tables[0], tables[1], tables[-1], near, crack, *parts)


def rest_kernel(step, part, sizes, moves, *refs):
    nblocks, span, width, front, start, nrows = sizes
    nparts = moves
    lists, rest = refs[:7], refs[7:]
    near_v, crack_v, acc = rest[:3]
    parts, rest = rest[3 : 3 + nparts], rest[3 + nparts :]
    nextra = 2 if step == 3 else 1
    extras, rest = rest[:nextra], rest[nextra:]
    before = ()
    if part == 1:
        nbefore = 2
        before, rest = rest[:nbefore], rest[nbefore:]
    nouts = 1 if step == 3 else (4, 3)[part]
    outs, rest = rest[:nouts], rest[nouts:]
    numbers = lists[6]
    lanes = acc.shape[2]
    late = nparts > 0
    if late:
        near_src, edge_src = parts
        (extra,) = rest
        extra[...] = jnp.zeros(extra.shape, jnp.float32)

        def add(half, rows, mats, srcs, number, matrix, source):
            offset = half * (rows.shape[0] // 2)
            shift_by = half * (nblocks // 2) if step == 3 else 0

            def some(i, carry):
                spots = [offset + i * GROUP + k for k in range(GROUP)]
                products = [
                    jnp.dot(
                        matrix(mats[spot]), source[srcs[spot]], preferred_element_type=jnp.float32
                    )
                    for spot in spots
                ]
                for k, (spot, product) in enumerate(zip(spots, products)):
                    used = jnp.where(i * GROUP + k < number, 1.0, 0.0)
                    extra[rows[spot] + shift_by] += used * product
                return carry

            lax.fori_loop(0, (number + GROUP - 1) // GROUP, some, 0)

        for half in (0, 1) if step == 3 else (part,):
            add(
                half,
                *lists[:3],
                numbers[half],
                lambda i: near_v[i // span, lax.rem(i, span)],
                near_src,
            )
            add(half, *lists[3:6], numbers[2 + half], lambda i: crack_v[i], edge_src)

    nsums = (1, 3, 5)[step - 1]
    zero = jnp.zeros((8, lanes), jnp.float32)

    def row(g, sums):
        total = acc[g] + extra[g] if late else acc[g]
        new = total[:width] + turn(total[width:])
        rows = pl.ds(pl.multiple_of((start + g) * width, width), width)
        if step == 1:
            new = extras[0][rows, :] - new
            terms = (new * new,)
        elif step == 2:
            first = extras[0][rows, :]
            terms = (first * new, first * turn(new), new * new)
        else:
            first, second, turned = extras[0][rows, :], extras[1][rows, :], turn(new)
            terms = (first * new, first * turned, second * new, second * turned, new * new)
        if step != 3:
            outs[0][rows, :] = new
            rounded = new.astype(jnp.bfloat16)
            outs[1][g] = rounded
            if part == 0:

                @pl.when(g < front)
                def _():
                    outs[2][g] = rounded

        return tuple(total + col_sum(term) for total, term in zip(sums, terms))

    sums = lax.fori_loop(0, nrows, row, (zero,) * nsums, unroll=2)
    sums = [jnp.sum(total, axis=0, keepdims=True) for total in sums]
    sums.append(jnp.zeros((8 - nsums, lanes), jnp.float32))
    sums = jnp.concatenate(sums, axis=0)
    if part == 1:
        sums = sums + before[-1][...]
        if step != 3:
            outs[0][: before[0].shape[0], :] = before[0][...]
    outs[-1][...] = sums


def rest_call(step, part, front, tables, near, crack, found, acc, extras, before=()):
    parts = found[3]
    nblocks, span = near.shape[:2]
    width, lanes = near.shape[3], acc.shape[2]
    nrows = acc.shape[0]
    start = part * (nblocks // 2)
    out_shape = [jax.ShapeDtypeStruct((8, lanes), jnp.float32)]
    if step != 3:
        ends = start + nrows
        vector = jax.ShapeDtypeStruct((ends * width, lanes), jnp.float32)
        low_a, low_b, head = low_shapes(nblocks, width, lanes, front)
        out_shape = [vector, *((low_a, head), (low_b,))[part], *out_shape]
    smem = pl.BlockSpec(memory_space=pltpu.SMEM)
    whole = pl.BlockSpec(memory_space=pltpu.VMEM)
    scratch, held = [], 0
    if parts:
        scratch = [pltpu.VMEM(acc.shape, jnp.float32)]
        held = 4 * acc.size
    return pl.pallas_call(
        functools.partial(
            rest_kernel,
            step,
            part,
            (nblocks, span, width, front, start, nrows),
            len(parts),
        ),
        out_shape=tuple(out_shape),
        in_specs=[smem] * 7
        + [whole] * (3 + len(parts) + len(extras) + len(before)),
        out_specs=tuple(whole for _ in out_shape),
        scratch_shapes=scratch,
        compiler_params=pltpu.CompilerParams(vmem_limit_bytes=held + 2 * MIB),
        cost_estimate=pl.CostEstimate(
            flops=4 * width * width * lanes * nrows * span // 4,
            bytes_accessed=REST_COST * acc.size * 4,
            transcendentals=0,
        ),
        name=f"rest_{step}_{part}",
    )(*tables[2:9], near, crack, acc, *parts, *extras, *before)


def low_shapes(nblocks, width, lanes, front):
    cut = nblocks // 2
    return tuple(
        jax.ShapeDtypeStruct((count, width, lanes), jnp.bfloat16)
        for count in (cut, nblocks - cut, front)
    )


def prepare_kernel(initial, low_a, low_b, head):
    width = low_a.shape[1]

    def one(target, start, g, carry):
        rows = pl.ds(pl.multiple_of((start + g) * width, width), width)
        rounded = jnp.concatenate([initial[0, rows], initial[1, rows]], axis=1)
        target[g] = rounded.astype(jnp.bfloat16)
        return carry

    cut = low_a.shape[0]
    lax.fori_loop(0, cut, functools.partial(one, low_a, 0), 0)
    lax.fori_loop(0, low_b.shape[0], functools.partial(one, low_b, cut), 0)
    lax.fori_loop(0, head.shape[0], functools.partial(one, head, 0), 0)


def swap(value, axis, distance):
    count = lax.axis_size(axis)
    return lax.ppermute(value, axis, [(i, i ^ distance) for i in range(count)])


def shift(value, axis, distance):
    count = lax.axis_size(axis)
    return lax.ppermute(value, axis, [(i, (i + distance) % count) for i in range(count)])


def ring(value, distance):
    count = lax.axis_size("clu")
    pairs = [(i, (i + (-distance if i % 2 else distance)) % count) for i in range(count)]
    return lax.ppermute(value, "clu", pairs)


def tuned():
    return lax.axis_size("clu") == 8


def tie(*values):
    return lax.optimization_barrier(values)


def exchange(lows, early_ties=(), late_ties=(), first_ties=()):
    low_a, low_b, head = lows
    cut, rest, front = (low.shape[0] for low in lows)
    nblocks = cut + rest
    if not tuned():
        count = lax.axis_size("clu")
        if callable(late_ties):
            late_ties = late_ties(early_ties)
        low = jnp.concatenate([low_a, low_b], axis=0)
        every = lax.all_gather(head, "clu", axis=0, tiled=True)
        parts = [low, shift(low, "clu", -1), shift(low, "clu", 1), every]
        source_moves = tuple((k, 0, nblocks, k * nblocks) for k in range(3))
        found = (parts, ((3, 0, count * front, 0),), source_moves, [])
        return found, early_ties, late_ties, first_ties
    beside_a = swap(low_a, "clu", 1)
    same, *first_ties = tie(ring(head, 2), *first_ties)
    other = ring(head, -2)
    tail, beside_a, same, other = tie(low_b, beside_a, same, other)
    onward, *early_ties = tie(jnp.concatenate([beside_a, same], axis=0), *early_ties)
    beyond_a = ring(onward, 2)
    beside_b = swap(tail, "clu", 1)
    if callable(late_ties):
        late_ties = late_ties(early_ties)
    beside_b, *late_ties = tie(beside_b, *late_ties)
    beyond_b = ring(beside_b, 2)
    pairs = swap(jnp.concatenate([same, beyond_a[cut:]], axis=0), "clu", 1)
    parts = [low_a, low_b, beside_a, beside_b, beyond_a, same, other]
    front_moves = tuple(
        (part, begin, front, place * front)
        for place, (part, begin) in enumerate(
            [(0, 0), (2, 0), (4, 0), (5, 0), (6, 0), (4, cut)]
        )
    )
    source_moves = (
        (0, 0, cut, 0),
        (1, 0, rest, cut),
        (2, 0, cut, nblocks),
        (3, 0, rest, nblocks + cut),
        (4, 0, cut, 2 * nblocks),
    )
    last = [beyond_b, pairs]
    found = (parts, front_moves, source_moves, last)
    return found, early_ties, late_ties, first_ties


def sum_over_clusters(value, *tied):
    if not tuned():
        return [lax.psum(value, "clu")], tied
    value, *tied = tie(value + swap(value, "clu", 1), *tied)
    return [value, *(shift(value, "clu", d) for d in (2, 4, 6))], tied


def cmul(a, b):
    return (a[0] * b[0] - a[1] * b[1], a[0] * b[1] + a[1] * b[0])


def cjmul(a, b):
    return (a[0] * b[0] + a[1] * b[1], a[0] * b[1] - a[1] * b[0])


def cadd(*terms):
    return (sum(t[0] for t in terms), sum(t[1] for t in terms))


def scale(factor, a):
    return (factor * a[0], factor * a[1])


def norm2(a):
    return a[0] * a[0] + a[1] * a[1]


def least_squares(beta_norm, first_h, sub_one, second_h, third_h, sub_two):
    r_one = jnp.sqrt(first_h[0] ** 2 + first_h[1] ** 2 + sub_one**2)
    q_real = first_h[0] / r_one
    q_imag = first_h[1] / r_one
    q_low = sub_one / r_one
    mix_real = q_real * second_h[0] + q_imag * second_h[1] + q_low * third_h[0]
    mix_imag = q_real * second_h[1] - q_imag * second_h[0] + q_low * third_h[1]
    top_real = second_h[0] - (mix_real * q_real - mix_imag * q_imag)
    top_imag = second_h[1] - (mix_real * q_imag + mix_imag * q_real)
    mid_real = third_h[0] - mix_real * q_low
    mid_imag = third_h[1] - mix_imag * q_low
    r_two_sq = top_real**2 + top_imag**2 + mid_real**2 + mid_imag**2 + sub_two**2
    later_real = beta_norm * top_real / r_two_sq
    later_imag = -beta_norm * top_imag / r_two_sq
    early_real = (beta_norm * q_real - (mix_real * later_real - mix_imag * later_imag)) / r_one
    early_imag = (-beta_norm * q_imag - (mix_real * later_imag + mix_imag * later_real)) / r_one
    return ((early_real, early_imag), (later_real, later_imag))


def combine(g00, g01, g11, g02, g12, g22):
    beta2 = g00 + EPS
    beta = jnp.sqrt(beta2)
    h11 = ((0.5 * g00 + g01[0]) / beta2, g01[1] / beta2)
    s = ((0.5 * EPS - g01[0]) / beta2, -g01[1] / beta2)
    s01 = cjmul(s, g01)
    w2w2 = g11 + 2.0 * s01[0] + norm2(s) * g00
    h21 = jnp.sqrt(jnp.maximum(w2w2 / beta2, 0.0) + EPS)
    k = 1.0 / (beta * h21)
    d = (s[0] + 0.5, s[1])
    e = scale(0.5, s)
    r0u = cadd(g02, cmul(d, g01), scale(g00, e))
    z1u = cadd(g12, scale(g11, d), cmul(e, (g01[0], -g01[1])))
    h12 = scale(k / beta, r0u)
    h22 = scale(k * k, cadd(z1u, cjmul(s, r0u)))
    uu = (
        g22
        + norm2(d) * g11
        + norm2(e) * g00
        + 2.0 * cjmul(d, g12)[0]
        + 2.0 * cjmul(e, g02)[0]
        + 2.0 * cjmul(e, cmul(d, g01))[0]
    )
    n11 = g00 / beta2
    n22 = k * k * w2w2
    n12 = scale(k / beta, cadd(g01, scale(g00, s)))
    rest = (
        k * k * uu
        + norm2(h12) * (n11 - 2.0)
        + norm2(h22) * (n22 - 2.0)
        + 2.0 * cmul(cjmul(h12, h22), n12)[0]
    )
    h32 = jnp.sqrt(jnp.maximum(rest, 0.0) + EPS)
    early, later = least_squares(beta, h11, h21, h12, h22, h32)
    b = scale(k, later)
    a = cadd(scale(1.0 / beta, early), cmul(b, s))
    return a, b


def small_kernel(nsums, pulse, *refs):
    coefs, sent = refs[nsums:]
    sums = refs[0][...]
    for other in refs[1:nsums]:
        sums = sums + other[...]
    half = sums.shape[1] // 2
    sums = sums[:, :half] + sums[:, half:]

    def row(i):
        return sums[i : i + 1]

    a, b = combine(
        row(0),
        (row(8), -row(9)),
        row(10),
        (row(16), -row(17)),
        (row(18), -row(19)),
        row(20),
    )
    zero = jnp.zeros((4, half), jnp.float32)
    coefs[...] = jnp.concatenate([*a, *b, zero], axis=0)
    factor = (pulse[0, 0], pulse[0, 1])
    sent[...] = jnp.concatenate([*cmul(factor, a), *cmul(factor, b), zero], axis=0)


def scattered_kernel(coefs, initial, first, second, scattered):
    half = initial.shape[2]
    a = (coefs[0:1], coefs[1:2])
    b = (coefs[2:3], coefs[3:4])
    width = 256

    def one(g, carry):
        rows = pl.ds(pl.multiple_of(g * width, width), width)
        x, y = first[rows, :], second[rows, :]
        xr, xi, yr, yi = x[:, :half], x[:, half:], y[:, :half], y[:, half:]
        scattered[0, rows, :] = initial[0, rows] + a[0] * xr - a[1] * xi + b[0] * yr - b[1] * yi
        scattered[1, rows, :] = initial[1, rows] + a[0] * xi + a[1] * xr + b[0] * yi + b[1] * yr
        return carry

    lax.fori_loop(0, first.shape[0] // width, one, 0)


def power_of_i(exponent):
    exponent = lax.rem(exponent, 4)
    real = jnp.where(exponent == 0, 1.0, jnp.where(exponent == 2, -1.0, 0.0))
    imag = jnp.where(exponent == 1, 1.0, jnp.where(exponent == 3, -1.0, 0.0))
    return real, imag


def terms_kernel(place, pulse, initial, send, keep):
    width = 256
    f, core = place[0], lax.rem(place[0], 2)
    factor = (pulse[0, 0], pulse[0, 1])
    sent = cmul(factor, power_of_i((1 - core) * f))
    kept = cmul(factor, power_of_i(core * f))

    def one(g, carry):
        rows = pl.ds(pl.multiple_of(g * width, width), width)
        real, imag = initial[0, rows], initial[1, rows]
        send[rows, :] = sent[0] * real - sent[1] * imag
        keep[rows, :] = kept[0] * real - kept[1] * imag
        return carry

    lax.fori_loop(0, initial.shape[1] // width, one, 0)


def base_kernel(incident, initial, base):
    width = 256

    def one(g, carry):
        rows = pl.ds(pl.multiple_of(g * width, width), width)
        base[rows, :] = jnp.concatenate(
            [incident[half, rows] - 0.5 * initial[half, rows] for half in range(2)], axis=1
        )
        return carry

    lax.fori_loop(0, base.shape[0] // width, one, 0)


def mix_kernel(place, keep, taken, here, away):
    side, sign = place[0] // 2, 1.0 - 2.0 * lax.rem(place[0], 2).astype(jnp.float32)
    near_sign, far_sign = jnp.where(side == 1, sign, 1.0), jnp.where(side == 0, sign, 1.0)
    near_other, far_other = jnp.where(side == 1, -sign, 1.0), jnp.where(side == 0, -sign, 1.0)
    here[...] = near_sign * keep[...] + near_other * taken[...]
    away[...] = far_sign * keep[...] + far_other * taken[...]


def trace_kernel(count, place, here, away, *refs):
    coefs, firsts, seconds = refs[:count], refs[count : 2 * count], refs[2 * count : 3 * count]
    trace = refs[3 * count]
    half = trace.shape[1]
    width = 256
    weights = []
    for k in range(count):
        turned = power_of_i(place[0] * place[k])
        values = coefs[k][...]
        weights.append(
            (
                cmul(turned, (values[0:1], values[1:2])),
                cmul(turned, (values[2:3], values[3:4])),
            )
        )

    def one(g, carry):
        rows = pl.ds(pl.multiple_of(g * width, width), width)
        total = here[rows, :] + away[rows, :]
        for k in range(count):
            a, b = weights[k]
            x, y = firsts[k][rows, :], seconds[k][rows, :]
            total = total + (a[0] * x[:, :half] - a[1] * x[:, half:])
            total = total + (b[0] * y[:, :half] - b[1] * y[:, half:])
        trace[rows, :] = total
        return carry

    lax.fori_loop(0, trace.shape[0] // width, one, 0)


def on_vmem(body, out_shape, smem_args, args, name):
    outs = jax.tree.leaves(out_shape)
    moved = sum(a.size * a.dtype.itemsize for a in (*args, *outs))
    whole = pl.BlockSpec(memory_space=pltpu.VMEM)
    smem = pl.BlockSpec(memory_space=pltpu.SMEM)
    return pl.pallas_call(
        body,
        out_shape=out_shape,
        in_specs=[smem] * len(smem_args) + [whole] * len(args),
        out_specs=jax.tree.map(lambda _: whole, out_shape),
        compiler_params=pltpu.CompilerParams(vmem_limit_bytes=PLAIN_VMEM),
        cost_estimate=pl.CostEstimate(flops=0, bytes_accessed=moved, transcendentals=0),
        name=name,
    )(*smem_args, *args)


def local(
    incident,
    initial,
    near_blocks,
    near_pattern,
    crack_blocks,
    crack_cluster,
    crack_source,
    crack_target,
    pulse_spectrum,
):
    panels, directions = incident.shape[2:]
    nblocks, span = near_blocks.shape[:2]
    width = near_blocks.shape[4]
    edges = crack_blocks.shape[0]
    front = 4
    near = near_blocks.reshape(nblocks, span, 2 * width, width)
    crack = crack_blocks.reshape(edges, 2 * width, width)
    incident, initial = incident[0], initial[0]
    lows = on_vmem(
        prepare_kernel,
        low_shapes(nblocks, width, 2 * directions, front),
        (),
        (initial,),
        "prepare",
    )

    place = lax.axis_index("frq") ^ jnp.arange(4, dtype=jnp.int32)
    real = jax.ShapeDtypeStruct((panels, directions), jnp.float32)
    both = jax.ShapeDtypeStruct((panels, 2 * directions), jnp.float32)

    tables = table_call(
        lax.axis_index("clu").reshape(1),
        near_pattern.reshape(-1),
        crack_cluster[:, 0],
        crack_source,
        crack_target,
        nblocks,
        span,
        front,
    )

    found, (from_start, *tables), base, _ = exchange(
        lows,
        (initial, *tables),
        lambda early: [on_vmem(base_kernel, both, (), (incident, early[0]), "base")],
    )
    base = base[0]
    tables = (*tables, crack_target)
    send, keep = on_vmem(
        terms_kernel, (real, real), (place, pulse_spectrum), (from_start,), "terms"
    )
    here, away = on_vmem(
        mix_kernel, (real, real), (place,), (keep, swap(send, "frq", 1)), "mix"
    )
    away = swap(away, "frq", 2)

    def operate(step, found, extras):
        accs = main_call(step, tables, near, crack, found)
        common = (front, tables, near, crack, found)
        if step == 3:
            return rest_call(3, 0, *common, accs[0], extras)
        upper, low_a, head, sums = rest_call(step, 0, *common, accs[0], extras)
        vector, low_b, sums = rest_call(step, 1, *common, accs[1], extras, (upper, sums))
        return vector, low_a, low_b, head, sums

    first, *lows, sums_one = operate(1, found, (base,))
    found, (away,), _, (first_sent,) = exchange(lows, (away,), (), (first,))
    first_across, first_one = swap(first_sent, "frq", 2), swap(first, "frq", 1)

    second, *lows, sums_two = operate(2, found, (first,))
    second_sent, first_across = tie(second, first_across)
    found, _, _, _ = exchange(lows)
    second_across, first_three = swap(second_sent, "frq", 2), swap(first_across, "frq", 1)
    (sums_three,) = operate(3, found, (first, second))
    second_one = swap(second, "frq", 1)
    sums = jnp.concatenate([sums_one, sums_two, sums_three], axis=0)
    sums, (second_one, first_three) = sum_over_clusters(sums, second_one, first_three)
    *sums, second_across = tie(*sums, second_across)
    second_three = swap(second_across, "frq", 1)
    firsts = [first, first_one, first_across, first_three]
    seconds = [second, second_one, second_across, second_three]

    row = jax.ShapeDtypeStruct((8, directions), jnp.float32)
    coefs, sent = on_vmem(
        functools.partial(small_kernel, len(sums)), (row, row), (pulse_spectrum,), sums, "small"
    )
    every = [sent, *(swap(sent, "frq", d) for d in (1, 2, 3))]
    scattered = on_vmem(
        scattered_kernel,
        jax.ShapeDtypeStruct(initial.shape, jnp.float32),
        (),
        (coefs, initial, first, second),
        "scattered",
    )
    trace = on_vmem(
        functools.partial(trace_kernel, len(firsts)),
        real,
        (place,),
        (here, away, *every, *firsts, *seconds),
        "trace",
    )
    return (scattered[None], trace[None])


def solution(mesh):
    in_specs = (
        P("frq", None, "clu", None),
        P("frq", None, "clu", None),
        P("clu", None, "frq", None, None, None),
        P("clu", None),
        P("clu", "frq", None, None, None),
        P("clu", None),
        P("clu"),
        P("clu"),
        P("frq", None),
    )
    out_specs = (P("frq", None, "clu", None), P("frq", "clu", None))
    return jax.shard_map(local, mesh=mesh, in_specs=in_specs, out_specs=out_specs, check_vma=False)
```

```python
import functools

import jax
import jax.numpy as jnp
from jax import lax
from jax.experimental import pallas as pl
from jax.experimental.pallas import tpu as pltpu
from jax.sharding import PartitionSpec as P

EPS = 1e-06
MIB = 1024 * 1024
PLAIN_VMEM = 10 * MIB


def turn(rows):
    half = rows.shape[1] // 2
    return jnp.concatenate([-rows[:, half:], rows[:, :half]], axis=1)


def col_sum(rows):
    return jnp.sum(rows.reshape(rows.shape[0] // 8, 8, rows.shape[1]), axis=0)


def table_kernel(sizes, place, pattern, cluster, source, target, *outs):
    nblocks, span, edges, front, count, tuned_here = sizes
    near_a, crack_a, near_rows, near_mats, near_srcs, edge_rows, edge_mats, edge_srcs, numbers = outs
    me = place[0]
    odd = lax.rem(me, 2)
    cut = nblocks // 2
    limits = (2 * nblocks + cut, 6 * front) if tuned_here else (3 * nblocks, count * front)

    def fill(i, carry):
        for rows, mats, srcs in (
            (near_rows, near_mats, near_srcs),
            (edge_rows, edge_mats, edge_srcs),
        ):

            @pl.when(i < rows.shape[0])
            def _():
                rows[i] = 0
                mats[i] = 0
                srcs[i] = 0

        return carry

    lax.fori_loop(0, max(near_rows.shape[0], edge_rows.shape[0]), fill, 0)

    def note(lists, half, row, mat, src, late, found):
        rows, mats, srcs = lists
        spot = half * (rows.shape[0] // 2) + jnp.where(half == 0, found[0], found[1])

        @pl.when(late)
        def _():
            rows[spot] = row - half * cut
            mats[spot] = mat
            srcs[spot] = src

        step = jnp.where(late, 1, 0)
        return (
            found[0] + jnp.where(half == 0, step, 0),
            found[1] + jnp.where(half == 1, step, 0),
        )

    def near_one(i, found):
        value = pattern[i]
        side, block = value // nblocks, lax.rem(value, nblocks)
        beside = jnp.where(side == 2, 1 - odd, odd) if tuned_here else jnp.where(side == 2, 1, 0)
        spot = jnp.where(side == 1, 0, jnp.where(beside == 1, 1, 2)) * nblocks + block
        late = spot >= limits[0]
        near_a[i] = jnp.where(late, limits[0], spot)
        row = i // span
        half = jnp.where(row >= cut, 1, 0)
        lists = (near_rows, near_mats, near_srcs)
        return note(lists, half, row, i, spot - limits[0], late, found)

    none = (jnp.int32(0), jnp.int32(0))
    near_found = lax.fori_loop(0, nblocks * span, near_one, none)

    def edge_one(e, found):
        if tuned_here:
            offset = lax.rem(cluster[e] - me + count, count)
            offset = jnp.where(odd == 1, lax.rem(count - offset, count), offset)
            slot = jnp.int32(0)
            for position, distance in enumerate((0, 1, 7, 6, 2, 4, 3, 5)):
                slot = jnp.where(offset == distance, position, slot)
        else:
            slot = cluster[e]
        spot = slot * front + source[e]
        late = spot >= limits[1]
        crack_a[e] = jnp.where(late, limits[1], spot)
        row = target[e]
        half = jnp.where(row >= cut, 1, 0)
        lists = (edge_rows, edge_mats, edge_srcs)
        return note(lists, half, row, e, spot - limits[1], late, found)

    edge_found = lax.fori_loop(0, edges, edge_one, none)
    for half in range(2):
        numbers[half] = near_found[half]
        numbers[2 + half] = edge_found[half]


def table_call(me, pattern, cluster, source, target, nblocks, span, front):
    edges = cluster.shape[0]
    cut = nblocks // 2
    near_list = 2 * max(cut, nblocks - cut) * span
    lengths = (nblocks * span, edges, *(near_list,) * 3, *(2 * edges,) * 3, 4)
    smem = pl.BlockSpec(memory_space=pltpu.SMEM)
    sizes = (nblocks, span, edges, front, lax.axis_size("clu"), tuned())
    return pl.pallas_call(
        functools.partial(table_kernel, sizes),
        out_shape=tuple(jax.ShapeDtypeStruct((length,), jnp.int32) for length in lengths),
        in_specs=[smem] * 5,
        out_specs=tuple(smem for _ in lengths),
        name="tables",
    )(me, pattern, cluster, source, target)


def block_copies(parts, moves, target, sems):
    return [
        pltpu.make_async_copy(
            parts[part].at[pl.ds(begin, count)], target.at[pl.ds(offset, count)], sems.at[place]
        )
        for place, (part, begin, count, offset) in enumerate(moves)
    ]


def total_of(moves):
    return sum(move[2] for move in moves)


GROUP = 4
REST_COST = 3


def main_kernel(sizes, moves, *refs):
    nblocks, span, edges, front_moves, source_moves, nparts = (*sizes, *moves)
    near_idx, crack_idx, crack_tgt, near_v, crack_v = refs[:5]
    parts = refs[5 : 5 + nparts]
    *accs, front_v, source_v, front_sem, source_sem = refs[5 + nparts :]
    cut = nblocks // 2
    if len(accs) == 1:
        accs = [accs[0].at[pl.ds(0, cut)], accs[0].at[pl.ds(cut, nblocks - cut)]]
    acc_a, acc_b = accs
    front_copies = block_copies(parts, front_moves, front_v, front_sem)
    source_copies = block_copies(parts, source_moves, source_v, source_sem)
    for copy in source_copies + front_copies:
        copy.start()
    for store in (front_v, source_v):
        store[store.shape[0] - 1] = jnp.zeros(store.shape[1:], store.dtype)
    for copy in source_copies:
        copy.wait()

    def row(acc, start, g, carry):
        left = jnp.concatenate([near_v[g, s] for s in range(span)], axis=1)
        right = jnp.concatenate([source_v[near_idx[g * span + s]] for s in range(span)], axis=0)
        acc[g - start] = jnp.dot(left, right, preferred_element_type=jnp.float32)
        return carry

    lax.fori_loop(0, cut, functools.partial(row, acc_a, 0), 0, unroll=4)
    lax.fori_loop(cut, nblocks, functools.partial(row, acc_b, cut), 0, unroll=4)
    for copy in front_copies:
        copy.wait()

    def crack_edges(i, carry):
        products = [
            jnp.dot(
                crack_v[i * GROUP + k],
                front_v[crack_idx[i * GROUP + k]],
                preferred_element_type=jnp.float32,
            )
            for k in range(GROUP)
        ]
        for k in range(GROUP):
            target = crack_tgt[i * GROUP + k]

            @pl.when(target < cut)
            def _():
                acc_a[target] += products[k]

            @pl.when(target >= cut)
            def _():
                acc_b[target - cut] += products[k]

        return carry

    lax.fori_loop(0, edges // GROUP, crack_edges, 0)


def main_call(step, tables, near, crack, found):
    parts, front_moves, source_moves = found[:3]
    nblocks, span = near.shape[:2]
    edges, width = crack.shape[0], near.shape[3]
    lanes = parts[0].shape[2]
    cut = nblocks // 2
    smem = pl.BlockSpec(memory_space=pltpu.SMEM)
    anywhere = pl.BlockSpec(memory_space=pl.ANY)
    whole = pl.BlockSpec(memory_space=pltpu.VMEM)
    blocks = total_of(front_moves) + total_of(source_moves) + 2
    counts = (nblocks,) if step == 3 else (cut, nblocks - cut)
    return pl.pallas_call(
        functools.partial(
            main_kernel, (nblocks, span, edges), (front_moves, source_moves, len(parts))
        ),
        out_shape=tuple(
            jax.ShapeDtypeStruct((rows, 2 * width, lanes), jnp.float32)
            for rows in counts
        ),
        in_specs=[smem] * 3 + [whole] * 2 + [anywhere] * len(parts),
        out_specs=tuple(whole for _ in counts),
        scratch_shapes=[
            pltpu.VMEM((total_of(front_moves) + 1, width, lanes), jnp.bfloat16),
            pltpu.VMEM((total_of(source_moves) + 1, width, lanes), jnp.bfloat16),
            pltpu.SemaphoreType.DMA((len(front_moves),)),
            pltpu.SemaphoreType.DMA((len(source_moves),)),
        ],
        compiler_params=pltpu.CompilerParams(
            vmem_limit_bytes=2 * blocks * width * lanes + 2 * MIB
        ),
        cost_estimate=pl.CostEstimate(
            flops=4 * width * width * lanes * (nblocks * span + edges),
            bytes_accessed=near.size * 2 + crack.size * 2,
            transcendentals=0,
        ),
        name=f"operator_{step}",
    )(tables[0], tables[1], tables[-1], near, crack, *parts)


def rest_kernel(step, part, sizes, moves, *refs):
    nblocks, span, width, front, start, nrows = sizes
    nparts = moves
    lists, rest = refs[:7], refs[7:]
    near_v, crack_v, acc = rest[:3]
    parts, rest = rest[3 : 3 + nparts], rest[3 + nparts :]
    nextra = 2 if step == 3 else 1
    extras, rest = rest[:nextra], rest[nextra:]
    before = ()
    if part == 1:
        nbefore = 2
        before, rest = rest[:nbefore], rest[nbefore:]
    nouts = 1 if step == 3 else (4, 3)[part]
    outs, rest = rest[:nouts], rest[nouts:]
    numbers = lists[6]
    lanes = acc.shape[2]
    late = nparts > 0
    if late:
        near_src, edge_src = parts
        (extra,) = rest
        extra[...] = jnp.zeros(extra.shape, jnp.float32)

        def add(half, rows, mats, srcs, number, matrix, source):
            offset = half * (rows.shape[0] // 2)
            shift_by = half * (nblocks // 2) if step == 3 else 0

            def some(i, carry):
                spots = [offset + i * GROUP + k for k in range(GROUP)]
                products = [
                    jnp.dot(
                        matrix(mats[spot]), source[srcs[spot]], preferred_element_type=jnp.float32
                    )
                    for spot in spots
                ]
                for k, (spot, product) in enumerate(zip(spots, products)):
                    used = jnp.where(i * GROUP + k < number, 1.0, 0.0)
                    extra[rows[spot] + shift_by] += used * product
                return carry

            lax.fori_loop(0, (number + GROUP - 1) // GROUP, some, 0)

        for half in (0, 1) if step == 3 else (part,):
            add(
                half,
                *lists[:3],
                numbers[half],
                lambda i: near_v[i // span, lax.rem(i, span)],
                near_src,
            )
            add(half, *lists[3:6], numbers[2 + half], lambda i: crack_v[i], edge_src)

    nsums = (1, 3, 5)[step - 1]
    zero = jnp.zeros((8, lanes), jnp.float32)

    def row(g, sums):
        total = acc[g] + extra[g] if late else acc[g]
        new = total[:width] + turn(total[width:])
        rows = pl.ds(pl.multiple_of((start + g) * width, width), width)
        if step == 1:
            new = extras[0][rows, :] - new
            terms = (new * new,)
        elif step == 2:
            first = extras[0][rows, :]
            terms = (first * new, first * turn(new), new * new)
        else:
            first, second, turned = extras[0][rows, :], extras[1][rows, :], turn(new)
            terms = (first * new, first * turned, second * new, second * turned, new * new)
        if step != 3:
            outs[0][rows, :] = new
            rounded = new.astype(jnp.bfloat16)
            outs[1][g] = rounded
            if part == 0:

                @pl.when(g < front)
                def _():
                    outs[2][g] = rounded

        return tuple(total + col_sum(term) for total, term in zip(sums, terms))

    sums = lax.fori_loop(0, nrows, row, (zero,) * nsums, unroll=2)
    sums = [jnp.sum(total, axis=0, keepdims=True) for total in sums]
    sums = [total[:, : lanes // 2] + total[:, lanes // 2 :] for total in sums]
    blank = jnp.zeros((1, lanes // 2), jnp.float32)
    place = (0, 1, 4)[step - 1]
    sums = jnp.concatenate([blank] * place + sums + [blank] * (16 - place - nsums), axis=0)
    if part == 1:
        sums = sums + before[-1][...]
        if step != 3:
            outs[0][: before[0].shape[0], :] = before[0][...]
    outs[-1][...] = sums


def rest_call(step, part, front, tables, near, crack, found, acc, extras, before=()):
    parts = found[3]
    nblocks, span = near.shape[:2]
    width, lanes = near.shape[3], acc.shape[2]
    nrows = acc.shape[0]
    start = part * (nblocks // 2)
    out_shape = [jax.ShapeDtypeStruct((16, lanes // 2), jnp.float32)]
    if step != 3:
        ends = start + nrows
        vector = jax.ShapeDtypeStruct((ends * width, lanes), jnp.float32)
        low_a, low_b, head = low_shapes(nblocks, width, lanes, front)
        out_shape = [vector, *((low_a, head), (low_b,))[part], *out_shape]
    smem = pl.BlockSpec(memory_space=pltpu.SMEM)
    whole = pl.BlockSpec(memory_space=pltpu.VMEM)
    scratch, held = [], 0
    if parts:
        scratch = [pltpu.VMEM(acc.shape, jnp.float32)]
        held = 4 * acc.size
    return pl.pallas_call(
        functools.partial(
            rest_kernel,
            step,
            part,
            (nblocks, span, width, front, start, nrows),
            len(parts),
        ),
        out_shape=tuple(out_shape),
        in_specs=[smem] * 7
        + [whole] * (3 + len(parts) + len(extras) + len(before)),
        out_specs=tuple(whole for _ in out_shape),
        scratch_shapes=scratch,
        compiler_params=pltpu.CompilerParams(vmem_limit_bytes=held + 2 * MIB),
        cost_estimate=pl.CostEstimate(
            flops=4 * width * width * lanes * nrows * span // 4,
            bytes_accessed=REST_COST * acc.size * 4,
            transcendentals=0,
        ),
        name=f"rest_{step}_{part}",
    )(*tables[2:9], near, crack, acc, *parts, *extras, *before)


def low_shapes(nblocks, width, lanes, front):
    cut = nblocks // 2
    return tuple(
        jax.ShapeDtypeStruct((count, width, lanes), jnp.bfloat16)
        for count in (cut, nblocks - cut, front)
    )


def prepare_kernel(initial, low_a, low_b, head):
    width = low_a.shape[1]

    def one(target, start, g, carry):
        rows = pl.ds(pl.multiple_of((start + g) * width, width), width)
        rounded = jnp.concatenate([initial[0, rows], initial[1, rows]], axis=1)
        target[g] = rounded.astype(jnp.bfloat16)
        return carry

    cut = low_a.shape[0]
    lax.fori_loop(0, cut, functools.partial(one, low_a, 0), 0)
    lax.fori_loop(0, low_b.shape[0], functools.partial(one, low_b, cut), 0)
    lax.fori_loop(0, head.shape[0], functools.partial(one, head, 0), 0)


def swap(value, axis, distance):
    count = lax.axis_size(axis)
    return lax.ppermute(value, axis, [(i, i ^ distance) for i in range(count)])


def shift(value, axis, distance):
    count = lax.axis_size(axis)
    return lax.ppermute(value, axis, [(i, (i + distance) % count) for i in range(count)])


def ring(value, distance):
    count = lax.axis_size("clu")
    pairs = [(i, (i + (-distance if i % 2 else distance)) % count) for i in range(count)]
    return lax.ppermute(value, "clu", pairs)


def tuned():
    return lax.axis_size("clu") == 8


def tie(*values):
    return lax.optimization_barrier(values)


def exchange(lows, early_ties=(), late_ties=(), first_ties=()):
    low_a, low_b, head = lows
    cut, rest, front = (low.shape[0] for low in lows)
    nblocks = cut + rest
    if not tuned():
        count = lax.axis_size("clu")
        if callable(late_ties):
            late_ties = late_ties(early_ties)
        low = jnp.concatenate([low_a, low_b], axis=0)
        every = lax.all_gather(head, "clu", axis=0, tiled=True)
        parts = [low, shift(low, "clu", -1), shift(low, "clu", 1), every]
        source_moves = tuple((k, 0, nblocks, k * nblocks) for k in range(3))
        found = (parts, ((3, 0, count * front, 0),), source_moves, [])
        return found, early_ties, late_ties, first_ties
    beside_a = swap(low_a, "clu", 1)
    same, *first_ties = tie(ring(head, 2), *first_ties)
    other = ring(head, -2)
    tail, beside_a, same, other = tie(low_b, beside_a, same, other)
    onward, *early_ties = tie(jnp.concatenate([beside_a, same], axis=0), *early_ties)
    beyond_a = ring(onward, 2)
    beside_b = swap(tail, "clu", 1)
    if callable(late_ties):
        late_ties = late_ties(early_ties)
    beside_b, *late_ties = tie(beside_b, *late_ties)
    beyond_b = ring(beside_b, 2)
    pairs = swap(jnp.concatenate([same, beyond_a[cut:]], axis=0), "clu", 1)
    parts = [low_a, low_b, beside_a, beside_b, beyond_a, same, other]
    front_moves = tuple(
        (part, begin, front, place * front)
        for place, (part, begin) in enumerate(
            [(0, 0), (2, 0), (4, 0), (5, 0), (6, 0), (4, cut)]
        )
    )
    source_moves = (
        (0, 0, cut, 0),
        (1, 0, rest, cut),
        (2, 0, cut, nblocks),
        (3, 0, rest, nblocks + cut),
        (4, 0, cut, 2 * nblocks),
    )
    last = [beyond_b, pairs]
    found = (parts, front_moves, source_moves, last)
    return found, early_ties, late_ties, first_ties


def sum_over_clusters(value, *tied):
    if not tuned():
        return [lax.psum(value, "clu")], tied
    value, *tied = tie(value + swap(value, "clu", 1), *tied)
    return [value, *(shift(value, "clu", d) for d in (2, 4, 6))], tied


def cmul(a, b):
    return (a[0] * b[0] - a[1] * b[1], a[0] * b[1] + a[1] * b[0])


def cjmul(a, b):
    return (a[0] * b[0] + a[1] * b[1], a[0] * b[1] - a[1] * b[0])


def cadd(*terms):
    return (sum(t[0] for t in terms), sum(t[1] for t in terms))


def scale(factor, a):
    return (factor * a[0], factor * a[1])


def norm2(a):
    return a[0] * a[0] + a[1] * a[1]


def least_squares(beta_norm, first_h, sub_one, second_h, third_h, sub_two):
    r_one = jnp.sqrt(first_h[0] ** 2 + first_h[1] ** 2 + sub_one**2)
    q_real = first_h[0] / r_one
    q_imag = first_h[1] / r_one
    q_low = sub_one / r_one
    mix_real = q_real * second_h[0] + q_imag * second_h[1] + q_low * third_h[0]
    mix_imag = q_real * second_h[1] - q_imag * second_h[0] + q_low * third_h[1]
    top_real = second_h[0] - (mix_real * q_real - mix_imag * q_imag)
    top_imag = second_h[1] - (mix_real * q_imag + mix_imag * q_real)
    mid_real = third_h[0] - mix_real * q_low
    mid_imag = third_h[1] - mix_imag * q_low
    r_two_sq = top_real**2 + top_imag**2 + mid_real**2 + mid_imag**2 + sub_two**2
    later_real = beta_norm * top_real / r_two_sq
    later_imag = -beta_norm * top_imag / r_two_sq
    early_real = (beta_norm * q_real - (mix_real * later_real - mix_imag * later_imag)) / r_one
    early_imag = (-beta_norm * q_imag - (mix_real * later_imag + mix_imag * later_real)) / r_one
    return ((early_real, early_imag), (later_real, later_imag))


def combine(g00, g01, g11, g02, g12, g22):
    beta2 = g00 + EPS
    beta = jnp.sqrt(beta2)
    h11 = ((0.5 * g00 + g01[0]) / beta2, g01[1] / beta2)
    s = ((0.5 * EPS - g01[0]) / beta2, -g01[1] / beta2)
    s01 = cjmul(s, g01)
    w2w2 = g11 + 2.0 * s01[0] + norm2(s) * g00
    h21 = jnp.sqrt(jnp.maximum(w2w2 / beta2, 0.0) + EPS)
    k = 1.0 / (beta * h21)
    d = (s[0] + 0.5, s[1])
    e = scale(0.5, s)
    r0u = cadd(g02, cmul(d, g01), scale(g00, e))
    z1u = cadd(g12, scale(g11, d), cmul(e, (g01[0], -g01[1])))
    h12 = scale(k / beta, r0u)
    h22 = scale(k * k, cadd(z1u, cjmul(s, r0u)))
    uu = (
        g22
        + norm2(d) * g11
        + norm2(e) * g00
        + 2.0 * cjmul(d, g12)[0]
        + 2.0 * cjmul(e, g02)[0]
        + 2.0 * cjmul(e, cmul(d, g01))[0]
    )
    n11 = g00 / beta2
    n22 = k * k * w2w2
    n12 = scale(k / beta, cadd(g01, scale(g00, s)))
    rest = (
        k * k * uu
        + norm2(h12) * (n11 - 2.0)
        + norm2(h22) * (n22 - 2.0)
        + 2.0 * cmul(cjmul(h12, h22), n12)[0]
    )
    h32 = jnp.sqrt(jnp.maximum(rest, 0.0) + EPS)
    early, later = least_squares(beta, h11, h21, h12, h22, h32)
    b = scale(k, later)
    a = cadd(scale(1.0 / beta, early), cmul(b, s))
    return a, b


def small_kernel(nsums, pulse, *refs):
    coefs, sent = refs[nsums:]
    sums = refs[0][...]
    for other in refs[1:nsums]:
        sums = sums + other[...]
    half = sums.shape[1]

    def row(i):
        return sums[i : i + 1]

    a, b = combine(
        row(0),
        (row(1), -row(2)),
        row(3),
        (row(4), -row(5)),
        (row(6), -row(7)),
        row(8),
    )
    zero = jnp.zeros((4, half), jnp.float32)
    coefs[...] = jnp.concatenate([*a, *b, zero], axis=0)
    factor = (pulse[0, 0], pulse[0, 1])
    sent[...] = jnp.concatenate([*cmul(factor, a), *cmul(factor, b), zero], axis=0)


def scattered_kernel(coefs, initial, first, second, scattered):
    half = initial.shape[2]
    a = (coefs[0:1], coefs[1:2])
    b = (coefs[2:3], coefs[3:4])
    width = 256

    def one(g, carry):
        rows = pl.ds(pl.multiple_of(g * width, width), width)
        x, y = first[rows, :], second[rows, :]
        xr, xi, yr, yi = x[:, :half], x[:, half:], y[:, :half], y[:, half:]
        scattered[0, rows, :] = initial[0, rows] + a[0] * xr - a[1] * xi + b[0] * yr - b[1] * yi
        scattered[1, rows, :] = initial[1, rows] + a[0] * xi + a[1] * xr + b[0] * yi + b[1] * yr
        return carry

    lax.fori_loop(0, first.shape[0] // width, one, 0)


def power_of_i(exponent):
    exponent = lax.rem(exponent, 4)
    real = jnp.where(exponent == 0, 1.0, jnp.where(exponent == 2, -1.0, 0.0))
    imag = jnp.where(exponent == 1, 1.0, jnp.where(exponent == 3, -1.0, 0.0))
    return real, imag


def terms_kernel(place, pulse, initial, send, keep):
    width = 256
    f, core = place[0], lax.rem(place[0], 2)
    factor = (pulse[0, 0], pulse[0, 1])
    sent = cmul(factor, power_of_i((1 - core) * f))
    kept = cmul(factor, power_of_i(core * f))

    def one(g, carry):
        rows = pl.ds(pl.multiple_of(g * width, width), width)
        real, imag = initial[0, rows], initial[1, rows]
        send[rows, :] = sent[0] * real - sent[1] * imag
        keep[rows, :] = kept[0] * real - kept[1] * imag
        return carry

    lax.fori_loop(0, initial.shape[1] // width, one, 0)


def base_kernel(incident, initial, base):
    width = 256

    def one(g, carry):
        rows = pl.ds(pl.multiple_of(g * width, width), width)
        base[rows, :] = jnp.concatenate(
            [incident[half, rows] - 0.5 * initial[half, rows] for half in range(2)], axis=1
        )
        return carry

    lax.fori_loop(0, base.shape[0] // width, one, 0)


def mix_kernel(place, keep, taken, here, away):
    side, sign = place[0] // 2, 1.0 - 2.0 * lax.rem(place[0], 2).astype(jnp.float32)
    near_sign, far_sign = jnp.where(side == 1, sign, 1.0), jnp.where(side == 0, sign, 1.0)
    near_other, far_other = jnp.where(side == 1, -sign, 1.0), jnp.where(side == 0, -sign, 1.0)
    here[...] = near_sign * keep[...] + near_other * taken[...]
    away[...] = far_sign * keep[...] + far_other * taken[...]


def trace_kernel(count, place, here, away, *refs):
    coefs, firsts, seconds = refs[:count], refs[count : 2 * count], refs[2 * count : 3 * count]
    trace = refs[3 * count]
    half = trace.shape[1]
    width = 256
    weights = []
    for k in range(count):
        turned = power_of_i(place[0] * place[k])
        values = coefs[k][...]
        weights.append(
            (
                cmul(turned, (values[0:1], values[1:2])),
                cmul(turned, (values[2:3], values[3:4])),
            )
        )

    def one(g, carry):
        rows = pl.ds(pl.multiple_of(g * width, width), width)
        total = here[rows, :] + away[rows, :]
        for k in range(count):
            a, b = weights[k]
            x, y = firsts[k][rows, :], seconds[k][rows, :]
            total = total + (a[0] * x[:, :half] - a[1] * x[:, half:])
            total = total + (b[0] * y[:, :half] - b[1] * y[:, half:])
        trace[rows, :] = total
        return carry

    lax.fori_loop(0, trace.shape[0] // width, one, 0)


def on_vmem(body, out_shape, smem_args, args, name):
    outs = jax.tree.leaves(out_shape)
    moved = sum(a.size * a.dtype.itemsize for a in (*args, *outs))
    whole = pl.BlockSpec(memory_space=pltpu.VMEM)
    smem = pl.BlockSpec(memory_space=pltpu.SMEM)
    return pl.pallas_call(
        body,
        out_shape=out_shape,
        in_specs=[smem] * len(smem_args) + [whole] * len(args),
        out_specs=jax.tree.map(lambda _: whole, out_shape),
        compiler_params=pltpu.CompilerParams(vmem_limit_bytes=PLAIN_VMEM),
        cost_estimate=pl.CostEstimate(flops=0, bytes_accessed=moved, transcendentals=0),
        name=name,
    )(*smem_args, *args)


def local(
    incident,
    initial,
    near_blocks,
    near_pattern,
    crack_blocks,
    crack_cluster,
    crack_source,
    crack_target,
    pulse_spectrum,
):
    panels, directions = incident.shape[2:]
    nblocks, span = near_blocks.shape[:2]
    width = near_blocks.shape[4]
    edges = crack_blocks.shape[0]
    front = 4
    near = near_blocks.reshape(nblocks, span, 2 * width, width)
    crack = crack_blocks.reshape(edges, 2 * width, width)
    incident, initial = incident[0], initial[0]
    lows = on_vmem(
        prepare_kernel,
        low_shapes(nblocks, width, 2 * directions, front),
        (),
        (initial,),
        "prepare",
    )

    place = lax.axis_index("frq") ^ jnp.arange(4, dtype=jnp.int32)
    real = jax.ShapeDtypeStruct((panels, directions), jnp.float32)
    both = jax.ShapeDtypeStruct((panels, 2 * directions), jnp.float32)

    tables = table_call(
        lax.axis_index("clu").reshape(1),
        near_pattern.reshape(-1),
        crack_cluster[:, 0],
        crack_source,
        crack_target,
        nblocks,
        span,
        front,
    )

    found, (from_start, *tables), base, _ = exchange(
        lows,
        (initial, *tables),
        lambda early: [on_vmem(base_kernel, both, (), (incident, early[0]), "base")],
    )
    base = base[0]
    tables = (*tables, crack_target)
    send, keep = on_vmem(
        terms_kernel, (real, real), (place, pulse_spectrum), (from_start,), "terms"
    )
    here, away = on_vmem(
        mix_kernel, (real, real), (place,), (keep, swap(send, "frq", 1)), "mix"
    )
    away = swap(away, "frq", 2)

    def operate(step, found, extras):
        accs = main_call(step, tables, near, crack, found)
        common = (front, tables, near, crack, found)
        if step == 3:
            return rest_call(3, 0, *common, accs[0], extras)
        upper, low_a, head, sums = rest_call(step, 0, *common, accs[0], extras)
        vector, low_b, sums = rest_call(step, 1, *common, accs[1], extras, (upper, sums))
        return vector, low_a, low_b, head, sums

    first, *lows, sums_one = operate(1, found, (base,))
    found, (away,), _, (first_sent,) = exchange(lows, (away,), (), (first,))
    first_across, first_one = swap(first_sent, "frq", 2), swap(first, "frq", 1)

    second, *lows, sums_two = operate(2, found, (first,))
    second_sent, first_across = tie(second, first_across)
    found, _, _, _ = exchange(lows)
    second_across, first_three = swap(second_sent, "frq", 2), swap(first_across, "frq", 1)
    (sums_three,) = operate(3, found, (first, second))
    second_one = swap(second, "frq", 1)
    sums = sums_one + sums_two + sums_three
    sums, (second_one, first_three) = sum_over_clusters(sums, second_one, first_three)
    *sums, second_across = tie(*sums, second_across)
    second_three = swap(second_across, "frq", 1)
    firsts = [first, first_one, first_across, first_three]
    seconds = [second, second_one, second_across, second_three]

    row = jax.ShapeDtypeStruct((8, directions), jnp.float32)
    coefs, sent = on_vmem(
        functools.partial(small_kernel, len(sums)), (row, row), (pulse_spectrum,), sums, "small"
    )
    every = [sent, *(swap(sent, "frq", d) for d in (1, 2, 3))]
    scattered = on_vmem(
        scattered_kernel,
        jax.ShapeDtypeStruct(initial.shape, jnp.float32),
        (),
        (coefs, initial, first, second),
        "scattered",
    )
    trace = on_vmem(
        functools.partial(trace_kernel, len(firsts)),
        real,
        (place,),
        (here, away, *every, *firsts, *seconds),
        "trace",
    )
    return (scattered[None], trace[None])


def solution(mesh):
    in_specs = (
        P("frq", None, "clu", None),
        P("frq", None, "clu", None),
        P("clu", None, "frq", None, None, None),
        P("clu", None),
        P("clu", "frq", None, None, None),
        P("clu", None),
        P("clu"),
        P("clu"),
        P("frq", None),
    )
    out_specs = (P("frq", None, "clu", None), P("frq", "clu", None))
    return jax.shard_map(local, mesh=mesh, in_specs=in_specs, out_specs=out_specs, check_vma=False)
```

```python
import functools

import jax
import jax.numpy as jnp
from jax import lax
from jax.experimental import pallas as pl
from jax.experimental.pallas import tpu as pltpu
from jax.sharding import PartitionSpec as P

EPS = 1e-06
MIB = 1024 * 1024
PLAIN_VMEM = 10 * MIB


def turn(rows):
    half = rows.shape[1] // 2
    return jnp.concatenate([-rows[:, half:], rows[:, :half]], axis=1)


def col_sum(rows):
    return jnp.sum(rows.reshape(rows.shape[0] // 8, 8, rows.shape[1]), axis=0)


def first_blocks(nblocks):
    return nblocks // 2 - 1


def table_kernel(sizes, place, pattern, cluster, source, target, *outs):
    nblocks, span, edges, front, count, tuned_here = sizes
    near_a, crack_a, near_rows, near_mats, near_srcs, edge_rows, edge_mats, edge_srcs, numbers = outs
    me = place[0]
    odd = lax.rem(me, 2)
    cut = first_blocks(nblocks)
    limits = (2 * nblocks + cut, 6 * front) if tuned_here else (3 * nblocks, count * front)

    def fill(i, carry):
        for rows, mats, srcs in (
            (near_rows, near_mats, near_srcs),
            (edge_rows, edge_mats, edge_srcs),
        ):

            @pl.when(i < rows.shape[0])
            def _():
                rows[i] = 0
                mats[i] = 0
                srcs[i] = 0

        return carry

    lax.fori_loop(0, max(near_rows.shape[0], edge_rows.shape[0]), fill, 0)

    def note(lists, half, row, mat, src, late, found):
        rows, mats, srcs = lists
        spot = half * (rows.shape[0] // 2) + jnp.where(half == 0, found[0], found[1])

        @pl.when(late)
        def _():
            rows[spot] = row - half * cut
            mats[spot] = mat
            srcs[spot] = src

        step = jnp.where(late, 1, 0)
        return (
            found[0] + jnp.where(half == 0, step, 0),
            found[1] + jnp.where(half == 1, step, 0),
        )

    def near_one(i, found):
        value = pattern[i]
        side, block = value // nblocks, lax.rem(value, nblocks)
        beside = jnp.where(side == 2, 1 - odd, odd) if tuned_here else jnp.where(side == 2, 1, 0)
        spot = jnp.where(side == 1, 0, jnp.where(beside == 1, 1, 2)) * nblocks + block
        late = spot >= limits[0]
        near_a[i] = jnp.where(late, limits[0], spot)
        row = i // span
        half = jnp.where(row >= cut, 1, 0)
        lists = (near_rows, near_mats, near_srcs)
        return note(lists, half, row, i, spot - limits[0], late, found)

    none = (jnp.int32(0), jnp.int32(0))
    near_found = lax.fori_loop(0, nblocks * span, near_one, none)

    def edge_one(e, found):
        if tuned_here:
            offset = lax.rem(cluster[e] - me + count, count)
            offset = jnp.where(odd == 1, lax.rem(count - offset, count), offset)
            slot = jnp.int32(0)
            for position, distance in enumerate((0, 1, 7, 6, 2, 4, 3, 5)):
                slot = jnp.where(offset == distance, position, slot)
        else:
            slot = cluster[e]
        spot = slot * front + source[e]
        late = spot >= limits[1]
        crack_a[e] = jnp.where(late, limits[1], spot)
        row = target[e]
        half = jnp.where(row >= cut, 1, 0)
        lists = (edge_rows, edge_mats, edge_srcs)
        return note(lists, half, row, e, spot - limits[1], late, found)

    edge_found = lax.fori_loop(0, edges, edge_one, none)
    for half in range(2):
        numbers[half] = near_found[half]
        numbers[2 + half] = edge_found[half]


def table_call(me, pattern, cluster, source, target, nblocks, span, front):
    edges = cluster.shape[0]
    cut = first_blocks(nblocks)
    near_list = 2 * max(cut, nblocks - cut) * span
    lengths = (nblocks * span, edges, *(near_list,) * 3, *(2 * edges,) * 3, 4)
    smem = pl.BlockSpec(memory_space=pltpu.SMEM)
    sizes = (nblocks, span, edges, front, lax.axis_size("clu"), tuned())
    return pl.pallas_call(
        functools.partial(table_kernel, sizes),
        out_shape=tuple(jax.ShapeDtypeStruct((length,), jnp.int32) for length in lengths),
        in_specs=[smem] * 5,
        out_specs=tuple(smem for _ in lengths),
        name="tables",
    )(me, pattern, cluster, source, target)


def block_copies(parts, moves, target, sems):
    return [
        pltpu.make_async_copy(
            parts[part].at[pl.ds(begin, count)], target.at[pl.ds(offset, count)], sems.at[place]
        )
        for place, (part, begin, count, offset) in enumerate(moves)
    ]


def total_of(moves):
    return sum(move[2] for move in moves)


GROUP = 4
REST_COST = 3


def main_kernel(sizes, moves, *refs):
    nblocks, span, edges, front_moves, source_moves, nparts = (*sizes, *moves)
    near_idx, crack_idx, crack_tgt, near_v, crack_v = refs[:5]
    parts = refs[5 : 5 + nparts]
    *accs, front_v, source_v, front_sem, source_sem = refs[5 + nparts :]
    cut = first_blocks(nblocks)
    if len(accs) == 1:
        accs = [accs[0].at[pl.ds(0, cut)], accs[0].at[pl.ds(cut, nblocks - cut)]]
    acc_a, acc_b = accs
    front_copies = block_copies(parts, front_moves, front_v, front_sem)
    source_copies = block_copies(parts, source_moves, source_v, source_sem)
    for copy in source_copies + front_copies:
        copy.start()
    for store in (front_v, source_v):
        store[store.shape[0] - 1] = jnp.zeros(store.shape[1:], store.dtype)
    for copy in source_copies:
        copy.wait()

    def row(acc, start, g, carry):
        left = jnp.concatenate([near_v[g, s] for s in range(span)], axis=1)
        right = jnp.concatenate([source_v[near_idx[g * span + s]] for s in range(span)], axis=0)
        acc[g - start] = jnp.dot(left, right, preferred_element_type=jnp.float32)
        return carry

    lax.fori_loop(0, cut, functools.partial(row, acc_a, 0), 0, unroll=4)
    lax.fori_loop(cut, nblocks, functools.partial(row, acc_b, cut), 0, unroll=4)
    for copy in front_copies:
        copy.wait()

    def crack_edges(i, carry):
        products = [
            jnp.dot(
                crack_v[i * GROUP + k],
                front_v[crack_idx[i * GROUP + k]],
                preferred_element_type=jnp.float32,
            )
            for k in range(GROUP)
        ]
        for k in range(GROUP):
            target = crack_tgt[i * GROUP + k]

            @pl.when(target < cut)
            def _():
                acc_a[target] += products[k]

            @pl.when(target >= cut)
            def _():
                acc_b[target - cut] += products[k]

        return carry

    lax.fori_loop(0, edges // GROUP, crack_edges, 0)


def main_call(step, tables, near, crack, found):
    parts, front_moves, source_moves = found[:3]
    nblocks, span = near.shape[:2]
    edges, width = crack.shape[0], near.shape[3]
    lanes = parts[0].shape[2]
    cut = first_blocks(nblocks)
    smem = pl.BlockSpec(memory_space=pltpu.SMEM)
    anywhere = pl.BlockSpec(memory_space=pl.ANY)
    whole = pl.BlockSpec(memory_space=pltpu.VMEM)
    blocks = total_of(front_moves) + total_of(source_moves) + 2
    counts = (nblocks,) if step == 3 else (cut, nblocks - cut)
    return pl.pallas_call(
        functools.partial(
            main_kernel, (nblocks, span, edges), (front_moves, source_moves, len(parts))
        ),
        out_shape=tuple(
            jax.ShapeDtypeStruct((rows, 2 * width, lanes), jnp.float32)
            for rows in counts
        ),
        in_specs=[smem] * 3 + [whole] * 2 + [anywhere] * len(parts),
        out_specs=tuple(whole for _ in counts),
        scratch_shapes=[
            pltpu.VMEM((total_of(front_moves) + 1, width, lanes), jnp.bfloat16),
            pltpu.VMEM((total_of(source_moves) + 1, width, lanes), jnp.bfloat16),
            pltpu.SemaphoreType.DMA((len(front_moves),)),
            pltpu.SemaphoreType.DMA((len(source_moves),)),
        ],
        compiler_params=pltpu.CompilerParams(
            vmem_limit_bytes=2 * blocks * width * lanes + 2 * MIB
        ),
        cost_estimate=pl.CostEstimate(
            flops=4 * width * width * lanes * (nblocks * span + edges),
            bytes_accessed=near.size * 2 + crack.size * 2,
            transcendentals=0,
        ),
        name=f"operator_{step}",
    )(tables[0], tables[1], tables[-1], near, crack, *parts)


def rest_kernel(step, part, sizes, moves, *refs):
    nblocks, span, width, front, start, nrows = sizes
    nparts = moves
    lists, rest = refs[:7], refs[7:]
    near_v, crack_v, acc = rest[:3]
    parts, rest = rest[3 : 3 + nparts], rest[3 + nparts :]
    nextra = 2 if step == 3 else 1
    extras, rest = rest[:nextra], rest[nextra:]
    before = ()
    if part == 1:
        nbefore = 2
        before, rest = rest[:nbefore], rest[nbefore:]
    nouts = 1 if step == 3 else (4, 3)[part]
    outs, rest = rest[:nouts], rest[nouts:]
    numbers = lists[6]
    lanes = acc.shape[2]
    late = nparts > 0
    if late:
        near_src, edge_src = parts
        (extra,) = rest
        extra[...] = jnp.zeros(extra.shape, jnp.float32)

        def add(half, rows, mats, srcs, number, matrix, source):
            offset = half * (rows.shape[0] // 2)
            shift_by = half * (first_blocks(nblocks)) if step == 3 else 0

            def some(i, carry):
                spots = [offset + i * GROUP + k for k in range(GROUP)]
                products = [
                    jnp.dot(
                        matrix(mats[spot]), source[srcs[spot]], preferred_element_type=jnp.float32
                    )
                    for spot in spots
                ]
                for k, (spot, product) in enumerate(zip(spots, products)):
                    used = jnp.where(i * GROUP + k < number, 1.0, 0.0)
                    extra[rows[spot] + shift_by] += used * product
                return carry

            lax.fori_loop(0, (number + GROUP - 1) // GROUP, some, 0)

        for half in (0, 1) if step == 3 else (part,):
            add(
                half,
                *lists[:3],
                numbers[half],
                lambda i: near_v[i // span, lax.rem(i, span)],
                near_src,
            )
            add(half, *lists[3:6], numbers[2 + half], lambda i: crack_v[i], edge_src)

    nsums = (1, 3, 5)[step - 1]
    zero = jnp.zeros((8, lanes), jnp.float32)

    def row(g, sums):
        total = acc[g] + extra[g] if late else acc[g]
        new = total[:width] + turn(total[width:])
        rows = pl.ds(pl.multiple_of((start + g) * width, width), width)
        if step == 1:
            new = extras[0][rows, :] - new
            terms = (new * new,)
        elif step == 2:
            first = extras[0][rows, :]
            terms = (first * new, first * turn(new), new * new)
        else:
            first, second, turned = extras[0][rows, :], extras[1][rows, :], turn(new)
            terms = (first * new, first * turned, second * new, second * turned, new * new)
        if step != 3:
            outs[0][rows, :] = new
            rounded = new.astype(jnp.bfloat16)
            outs[1][g] = rounded
            if part == 0:

                @pl.when(g < front)
                def _():
                    outs[2][g] = rounded

        return tuple(total + col_sum(term) for total, term in zip(sums, terms))

    sums = lax.fori_loop(0, nrows, row, (zero,) * nsums, unroll=2)
    sums = [jnp.sum(total, axis=0, keepdims=True) for total in sums]
    sums.append(jnp.zeros((8 - nsums, lanes), jnp.float32))
    sums = jnp.concatenate(sums, axis=0)
    if part == 1:
        sums = sums + before[-1][...]
        if step != 3:
            outs[0][: before[0].shape[0], :] = before[0][...]
    outs[-1][...] = sums


def rest_call(step, part, front, tables, near, crack, found, acc, extras, before=()):
    parts = found[3]
    nblocks, span = near.shape[:2]
    width, lanes = near.shape[3], acc.shape[2]
    nrows = acc.shape[0]
    start = part * (first_blocks(nblocks))
    out_shape = [jax.ShapeDtypeStruct((8, lanes), jnp.float32)]
    if step != 3:
        ends = start + nrows
        vector = jax.ShapeDtypeStruct((ends * width, lanes), jnp.float32)
        low_a, low_b, head = low_shapes(nblocks, width, lanes, front)
        out_shape = [vector, *((low_a, head), (low_b,))[part], *out_shape]
    smem = pl.BlockSpec(memory_space=pltpu.SMEM)
    whole = pl.BlockSpec(memory_space=pltpu.VMEM)
    scratch, held = [], 0
    if parts:
        scratch = [pltpu.VMEM(acc.shape, jnp.float32)]
        held = 4 * acc.size
    return pl.pallas_call(
        functools.partial(
            rest_kernel,
            step,
            part,
            (nblocks, span, width, front, start, nrows),
            len(parts),
        ),
        out_shape=tuple(out_shape),
        in_specs=[smem] * 7
        + [whole] * (3 + len(parts) + len(extras) + len(before)),
        out_specs=tuple(whole for _ in out_shape),
        scratch_shapes=scratch,
        compiler_params=pltpu.CompilerParams(vmem_limit_bytes=held + 2 * MIB),
        cost_estimate=pl.CostEstimate(
            flops=4 * width * width * lanes * nrows * span // 4,
            bytes_accessed=REST_COST * acc.size * 4,
            transcendentals=0,
        ),
        name=f"rest_{step}_{part}",
    )(*tables[2:9], near, crack, acc, *parts, *extras, *before)


def low_shapes(nblocks, width, lanes, front):
    cut = first_blocks(nblocks)
    return tuple(
        jax.ShapeDtypeStruct((count, width, lanes), jnp.bfloat16)
        for count in (cut, nblocks - cut, front)
    )


def prepare_kernel(initial, low_a, low_b, head):
    width = low_a.shape[1]

    def one(target, start, g, carry):
        rows = pl.ds(pl.multiple_of((start + g) * width, width), width)
        rounded = jnp.concatenate([initial[0, rows], initial[1, rows]], axis=1)
        target[g] = rounded.astype(jnp.bfloat16)
        return carry

    cut = low_a.shape[0]
    lax.fori_loop(0, cut, functools.partial(one, low_a, 0), 0)
    lax.fori_loop(0, low_b.shape[0], functools.partial(one, low_b, cut), 0)
    lax.fori_loop(0, head.shape[0], functools.partial(one, head, 0), 0)


def swap(value, axis, distance):
    count = lax.axis_size(axis)
    return lax.ppermute(value, axis, [(i, i ^ distance) for i in range(count)])


def shift(value, axis, distance):
    count = lax.axis_size(axis)
    return lax.ppermute(value, axis, [(i, (i + distance) % count) for i in range(count)])


def ring(value, distance):
    count = lax.axis_size("clu")
    pairs = [(i, (i + (-distance if i % 2 else distance)) % count) for i in range(count)]
    return lax.ppermute(value, "clu", pairs)


def tuned():
    return lax.axis_size("clu") == 8


def tie(*values):
    return lax.optimization_barrier(values)


def exchange(lows, early_ties=(), late_ties=(), first_ties=()):
    low_a, low_b, head = lows
    cut, rest, front = (low.shape[0] for low in lows)
    nblocks = cut + rest
    if not tuned():
        count = lax.axis_size("clu")
        if callable(late_ties):
            late_ties = late_ties(early_ties)
        low = jnp.concatenate([low_a, low_b], axis=0)
        every = lax.all_gather(head, "clu", axis=0, tiled=True)
        parts = [low, shift(low, "clu", -1), shift(low, "clu", 1), every]
        source_moves = tuple((k, 0, nblocks, k * nblocks) for k in range(3))
        found = (parts, ((3, 0, count * front, 0),), source_moves, [])
        return found, early_ties, late_ties, first_ties
    beside_a = swap(low_a, "clu", 1)
    same, *first_ties = tie(ring(head, 2), *first_ties)
    other = ring(head, -2)
    tail, beside_a, same, other = tie(low_b, beside_a, same, other)
    onward, *early_ties = tie(jnp.concatenate([beside_a, same], axis=0), *early_ties)
    beyond_a = ring(onward, 2)
    beside_b = swap(tail, "clu", 1)
    if callable(late_ties):
        late_ties = late_ties(early_ties)
    beside_b, *late_ties = tie(beside_b, *late_ties)
    beyond_b = ring(beside_b, 2)
    pairs = swap(jnp.concatenate([same, beyond_a[cut:]], axis=0), "clu", 1)
    parts = [low_a, low_b, beside_a, beside_b, beyond_a, same, other]
    front_moves = tuple(
        (part, begin, front, place * front)
        for place, (part, begin) in enumerate(
            [(0, 0), (2, 0), (4, 0), (5, 0), (6, 0), (4, cut)]
        )
    )
    source_moves = (
        (0, 0, cut, 0),
        (1, 0, rest, cut),
        (2, 0, cut, nblocks),
        (3, 0, rest, nblocks + cut),
        (4, 0, cut, 2 * nblocks),
    )
    last = [beyond_b, pairs]
    found = (parts, front_moves, source_moves, last)
    return found, early_ties, late_ties, first_ties


def sum_over_clusters(value, *tied):
    if not tuned():
        return [lax.psum(value, "clu")], tied
    value, *tied = tie(value + swap(value, "clu", 1), *tied)
    return [value, *(shift(value, "clu", d) for d in (2, 4, 6))], tied


def cmul(a, b):
    return (a[0] * b[0] - a[1] * b[1], a[0] * b[1] + a[1] * b[0])


def cjmul(a, b):
    return (a[0] * b[0] + a[1] * b[1], a[0] * b[1] - a[1] * b[0])


def cadd(*terms):
    return (sum(t[0] for t in terms), sum(t[1] for t in terms))


def scale(factor, a):
    return (factor * a[0], factor * a[1])


def norm2(a):
    return a[0] * a[0] + a[1] * a[1]


def least_squares(beta_norm, first_h, sub_one, second_h, third_h, sub_two):
    r_one = jnp.sqrt(first_h[0] ** 2 + first_h[1] ** 2 + sub_one**2)
    q_real = first_h[0] / r_one
    q_imag = first_h[1] / r_one
    q_low = sub_one / r_one
    mix_real = q_real * second_h[0] + q_imag * second_h[1] + q_low * third_h[0]
    mix_imag = q_real * second_h[1] - q_imag * second_h[0] + q_low * third_h[1]
    top_real = second_h[0] - (mix_real * q_real - mix_imag * q_imag)
    top_imag = second_h[1] - (mix_real * q_imag + mix_imag * q_real)
    mid_real = third_h[0] - mix_real * q_low
    mid_imag = third_h[1] - mix_imag * q_low
    r_two_sq = top_real**2 + top_imag**2 + mid_real**2 + mid_imag**2 + sub_two**2
    later_real = beta_norm * top_real / r_two_sq
    later_imag = -beta_norm * top_imag / r_two_sq
    early_real = (beta_norm * q_real - (mix_real * later_real - mix_imag * later_imag)) / r_one
    early_imag = (-beta_norm * q_imag - (mix_real * later_imag + mix_imag * later_real)) / r_one
    return ((early_real, early_imag), (later_real, later_imag))


def combine(g00, g01, g11, g02, g12, g22):
    beta2 = g00 + EPS
    beta = jnp.sqrt(beta2)
    h11 = ((0.5 * g00 + g01[0]) / beta2, g01[1] / beta2)
    s = ((0.5 * EPS - g01[0]) / beta2, -g01[1] / beta2)
    s01 = cjmul(s, g01)
    w2w2 = g11 + 2.0 * s01[0] + norm2(s) * g00
    h21 = jnp.sqrt(jnp.maximum(w2w2 / beta2, 0.0) + EPS)
    k = 1.0 / (beta * h21)
    d = (s[0] + 0.5, s[1])
    e = scale(0.5, s)
    r0u = cadd(g02, cmul(d, g01), scale(g00, e))
    z1u = cadd(g12, scale(g11, d), cmul(e, (g01[0], -g01[1])))
    h12 = scale(k / beta, r0u)
    h22 = scale(k * k, cadd(z1u, cjmul(s, r0u)))
    uu = (
        g22
        + norm2(d) * g11
        + norm2(e) * g00
        + 2.0 * cjmul(d, g12)[0]
        + 2.0 * cjmul(e, g02)[0]
        + 2.0 * cjmul(e, cmul(d, g01))[0]
    )
    n11 = g00 / beta2
    n22 = k * k * w2w2
    n12 = scale(k / beta, cadd(g01, scale(g00, s)))
    rest = (
        k * k * uu
        + norm2(h12) * (n11 - 2.0)
        + norm2(h22) * (n22 - 2.0)
        + 2.0 * cmul(cjmul(h12, h22), n12)[0]
    )
    h32 = jnp.sqrt(jnp.maximum(rest, 0.0) + EPS)
    early, later = least_squares(beta, h11, h21, h12, h22, h32)
    b = scale(k, later)
    a = cadd(scale(1.0 / beta, early), cmul(b, s))
    return a, b


def small_kernel(nsums, pulse, *refs):
    coefs, sent = refs[nsums:]
    sums = refs[0][...]
    for other in refs[1:nsums]:
        sums = sums + other[...]
    half = sums.shape[1] // 2
    sums = sums[:, :half] + sums[:, half:]

    def row(i):
        return sums[i : i + 1]

    a, b = combine(
        row(0),
        (row(8), -row(9)),
        row(10),
        (row(16), -row(17)),
        (row(18), -row(19)),
        row(20),
    )
    zero = jnp.zeros((4, half), jnp.float32)
    coefs[...] = jnp.concatenate([*a, *b, zero], axis=0)
    factor = (pulse[0, 0], pulse[0, 1])
    sent[...] = jnp.concatenate([*cmul(factor, a), *cmul(factor, b), zero], axis=0)


def scattered_kernel(coefs, initial, first, second, scattered):
    half = initial.shape[2]
    a = (coefs[0:1], coefs[1:2])
    b = (coefs[2:3], coefs[3:4])
    width = 256

    def one(g, carry):
        rows = pl.ds(pl.multiple_of(g * width, width), width)
        x, y = first[rows, :], second[rows, :]
        xr, xi, yr, yi = x[:, :half], x[:, half:], y[:, :half], y[:, half:]
        scattered[0, rows, :] = initial[0, rows] + a[0] * xr - a[1] * xi + b[0] * yr - b[1] * yi
        scattered[1, rows, :] = initial[1, rows] + a[0] * xi + a[1] * xr + b[0] * yi + b[1] * yr
        return carry

    lax.fori_loop(0, first.shape[0] // width, one, 0)


def power_of_i(exponent):
    exponent = lax.rem(exponent, 4)
    real = jnp.where(exponent == 0, 1.0, jnp.where(exponent == 2, -1.0, 0.0))
    imag = jnp.where(exponent == 1, 1.0, jnp.where(exponent == 3, -1.0, 0.0))
    return real, imag


def terms_kernel(place, pulse, initial, send, keep):
    width = 256
    f, core = place[0], lax.rem(place[0], 2)
    factor = (pulse[0, 0], pulse[0, 1])
    sent = cmul(factor, power_of_i((1 - core) * f))
    kept = cmul(factor, power_of_i(core * f))

    def one(g, carry):
        rows = pl.ds(pl.multiple_of(g * width, width), width)
        real, imag = initial[0, rows], initial[1, rows]
        send[rows, :] = sent[0] * real - sent[1] * imag
        keep[rows, :] = kept[0] * real - kept[1] * imag
        return carry

    lax.fori_loop(0, initial.shape[1] // width, one, 0)


def base_kernel(incident, initial, base):
    width = 256

    def one(g, carry):
        rows = pl.ds(pl.multiple_of(g * width, width), width)
        base[rows, :] = jnp.concatenate(
            [incident[half, rows] - 0.5 * initial[half, rows] for half in range(2)], axis=1
        )
        return carry

    lax.fori_loop(0, base.shape[0] // width, one, 0)


def mix_kernel(place, keep, taken, here, away):
    side, sign = place[0] // 2, 1.0 - 2.0 * lax.rem(place[0], 2).astype(jnp.float32)
    near_sign, far_sign = jnp.where(side == 1, sign, 1.0), jnp.where(side == 0, sign, 1.0)
    near_other, far_other = jnp.where(side == 1, -sign, 1.0), jnp.where(side == 0, -sign, 1.0)
    here[...] = near_sign * keep[...] + near_other * taken[...]
    away[...] = far_sign * keep[...] + far_other * taken[...]


def trace_kernel(count, place, here, away, *refs):
    coefs, firsts, seconds = refs[:count], refs[count : 2 * count], refs[2 * count : 3 * count]
    trace = refs[3 * count]
    half = trace.shape[1]
    width = 256
    weights = []
    for k in range(count):
        turned = power_of_i(place[0] * place[k])
        values = coefs[k][...]
        weights.append(
            (
                cmul(turned, (values[0:1], values[1:2])),
                cmul(turned, (values[2:3], values[3:4])),
            )
        )

    def one(g, carry):
        rows = pl.ds(pl.multiple_of(g * width, width), width)
        total = here[rows, :] + away[rows, :]
        for k in range(count):
            a, b = weights[k]
            x, y = firsts[k][rows, :], seconds[k][rows, :]
            total = total + (a[0] * x[:, :half] - a[1] * x[:, half:])
            total = total + (b[0] * y[:, :half] - b[1] * y[:, half:])
        trace[rows, :] = total
        return carry

    lax.fori_loop(0, trace.shape[0] // width, one, 0)


def on_vmem(body, out_shape, smem_args, args, name):
    outs = jax.tree.leaves(out_shape)
    moved = sum(a.size * a.dtype.itemsize for a in (*args, *outs))
    whole = pl.BlockSpec(memory_space=pltpu.VMEM)
    smem = pl.BlockSpec(memory_space=pltpu.SMEM)
    return pl.pallas_call(
        body,
        out_shape=out_shape,
        in_specs=[smem] * len(smem_args) + [whole] * len(args),
        out_specs=jax.tree.map(lambda _: whole, out_shape),
        compiler_params=pltpu.CompilerParams(vmem_limit_bytes=PLAIN_VMEM),
        cost_estimate=pl.CostEstimate(flops=0, bytes_accessed=moved, transcendentals=0),
        name=name,
    )(*smem_args, *args)


def local(
    incident,
    initial,
    near_blocks,
    near_pattern,
    crack_blocks,
    crack_cluster,
    crack_source,
    crack_target,
    pulse_spectrum,
):
    panels, directions = incident.shape[2:]
    nblocks, span = near_blocks.shape[:2]
    width = near_blocks.shape[4]
    edges = crack_blocks.shape[0]
    front = 4
    near = near_blocks.reshape(nblocks, span, 2 * width, width)
    crack = crack_blocks.reshape(edges, 2 * width, width)
    incident, initial = incident[0], initial[0]
    lows = on_vmem(
        prepare_kernel,
        low_shapes(nblocks, width, 2 * directions, front),
        (),
        (initial,),
        "prepare",
    )

    place = lax.axis_index("frq") ^ jnp.arange(4, dtype=jnp.int32)
    real = jax.ShapeDtypeStruct((panels, directions), jnp.float32)
    both = jax.ShapeDtypeStruct((panels, 2 * directions), jnp.float32)

    tables = table_call(
        lax.axis_index("clu").reshape(1),
        near_pattern.reshape(-1),
        crack_cluster[:, 0],
        crack_source,
        crack_target,
        nblocks,
        span,
        front,
    )

    found, (from_start, *tables), base, _ = exchange(
        lows,
        (initial, *tables),
        lambda early: [on_vmem(base_kernel, both, (), (incident, early[0]), "base")],
    )
    base = base[0]
    tables = (*tables, crack_target)
    send, keep = on_vmem(
        terms_kernel, (real, real), (place, pulse_spectrum), (from_start,), "terms"
    )
    here, away = on_vmem(
        mix_kernel, (real, real), (place,), (keep, swap(send, "frq", 1)), "mix"
    )
    away = swap(away, "frq", 2)

    def operate(step, found, extras):
        accs = main_call(step, tables, near, crack, found)
        common = (front, tables, near, crack, found)
        if step == 3:
            return rest_call(3, 0, *common, accs[0], extras)
        upper, low_a, head, sums = rest_call(step, 0, *common, accs[0], extras)
        vector, low_b, sums = rest_call(step, 1, *common, accs[1], extras, (upper, sums))
        return vector, low_a, low_b, head, sums

    first, *lows, sums_one = operate(1, found, (base,))
    found, (away,), _, (first_sent,) = exchange(lows, (away,), (), (first,))
    first_across, first_one = swap(first_sent, "frq", 2), swap(first, "frq", 1)

    second, *lows, sums_two = operate(2, found, (first,))
    second_sent, first_across = tie(second, first_across)
    found, _, _, _ = exchange(lows)
    second_across, first_three = swap(second_sent, "frq", 2), swap(first_across, "frq", 1)
    (sums_three,) = operate(3, found, (first, second))
    second_one = swap(second, "frq", 1)
    sums = jnp.concatenate([sums_one, sums_two, sums_three], axis=0)
    sums, (second_one, first_three) = sum_over_clusters(sums, second_one, first_three)
    *sums, second_across = tie(*sums, second_across)
    second_three = swap(second_across, "frq", 1)
    firsts = [first, first_one, first_across, first_three]
    seconds = [second, second_one, second_across, second_three]

    row = jax.ShapeDtypeStruct((8, directions), jnp.float32)
    coefs, sent = on_vmem(
        functools.partial(small_kernel, len(sums)), (row, row), (pulse_spectrum,), sums, "small"
    )
    every = [sent, *(swap(sent, "frq", d) for d in (1, 2, 3))]
    scattered = on_vmem(
        scattered_kernel,
        jax.ShapeDtypeStruct(initial.shape, jnp.float32),
        (),
        (coefs, initial, first, second),
        "scattered",
    )
    trace = on_vmem(
        functools.partial(trace_kernel, len(firsts)),
        real,
        (place,),
        (here, away, *every, *firsts, *seconds),
        "trace",
    )
    return (scattered[None], trace[None])


def solution(mesh):
    in_specs = (
        P("frq", None, "clu", None),
        P("frq", None, "clu", None),
        P("clu", None, "frq", None, None, None),
        P("clu", None),
        P("clu", "frq", None, None, None),
        P("clu", None),
        P("clu"),
        P("clu"),
        P("frq", None),
    )
    out_specs = (P("frq", None, "clu", None), P("frq", "clu", None))
    return jax.shard_map(local, mesh=mesh, in_specs=in_specs, out_specs=out_specs, check_vma=False)
```
